32 devices in a mesh: pipe: 4 (over y, x), dp: 8 (over z, core).
Axes of the slice: x: 2, y: 2, z: 4, core: 2. Of those that a mesh axis runs over, the one named last changes fastest.
Arguments:
- images_in: bfloat16 [6, 8, 16, 16, 512], P(None, 'dp'), may hold values from -6 to 6
- conv_local: bfloat16 [4, 3, 3, 512, 128], P('pipe'), may hold values from -0.09375 to 0.09375
- conv_cross: bfloat16 [4, 3, 3, 128, 384], P('pipe'), may hold values from -0.1875 to 0.1875
- reduce_weight: bfloat16 [4, 384, 192], P('pipe'), may hold values from -0.3125 to 0.3125
- spectral_weight: bfloat16 [4, 384, 384], P('pipe'), may hold values from -0.3125 to 0.3125
- expand_weight: bfloat16 [4, 192, 384], P('pipe'), may hold values from -0.4375 to 0.4375
- norm_gain: float32 [4, 1088], P('pipe'), may hold values from 0.5 to 1.5
- norm_bias: float32 [4, 1088], P('pipe'), may hold values from -3 to 3
- cotangent: bfloat16 [6, 8, 16, 16, 512], P(None, 'dp'), may hold values from -6 to 6
- hole_mask: int32 [6, 8, 16, 16], P(None, 'dp'), may hold values from 0 to 1, as said below
Outputs:
- activations: bfloat16 [4, 6, 8, 16, 16, 512], P('pipe', None, 'dp')
- input_grads: float32 [4, 6, 8, 16, 16, 512], P('pipe', None, 'dp')
- grad_conv_local: float32 [4, 3, 3, 512, 128], P('pipe')
- grad_conv_cross: float32 [4, 3, 3, 128, 384], P('pipe')
- grad_reduce: float32 [4, 384, 192], P('pipe')
- grad_spectral: float32 [4, 384, 384], P('pipe')
- grad_expand: float32 [4, 192, 384], P('pipe')
- grad_gain: float32 [4, 1088], P('pipe')
- grad_bias: float32 [4, 1088], P('pipe')
The draws below stay inside these ranges and needn't reach their ends.
Inputs may be any that keep to these rules, and one draw needn't show every extreme that they name: `hole_mask`: each image has between none and 9 in 10 of its pixels as holes, a heavy-tailed amount.
All inputs are finite; a program needn't handle non-finite values.
Results may differ from the reference program's by a relative error of at most 0.023.
Values may be sent and summed in bfloat16 or wider, within the bound.
No kernel may reach another device: no remote copies, remote signals or barrier semaphores. Data moves between devices by JAX's collectives and lax.ppermute only.
A program may use at most 64 MiB of HBM per device.

```python
import jax
import jax.numpy as jnp
from jax import lax

CL = 128
CG = 384
CS = 192
CH = 512
NORMS = 1088
SIDE = 16
MB = 6
SECTIONS = 4
IMAGES = 8


def draw_hole_mask(key, part):
    key = jax.random.fold_in(key, 11)
    count_key, order_key = jax.random.split(key)
    pixels = SIDE * SIDE
    levels = jax.random.randint(count_key, (MB, IMAGES), 0, 31)
    hole_count = levels * levels * levels * (9 * pixels // 10) // 27000
    image_keys = jax.random.split(order_key, MB * IMAGES)
    ranking = jax.vmap(lambda image_key: jax.random.permutation(image_key, pixels))(image_keys).reshape(MB, IMAGES, pixels)
    return (ranking < hole_count[..., None]).astype(jnp.int32).reshape(MB, IMAGES, SIDE, SIDE)


def level_of(rng, dims, cuts, least, high):
    factor_of, own = 1.0, jax.random.fold_in(rng, 6)
    for position, blocks in cuts:
        steps = jnp.exp(jax.random.uniform(jax.random.fold_in(own, position), (blocks,), jnp.float32, least / len(cuts), high / len(cuts)))
        factor_of = factor_of * jnp.repeat(steps, dims[position] // blocks).reshape([-1 if axis == position else 1 for axis in range(len(dims))])
    return factor_of


def bell_draw(rng, extent, scale, bound, shards=(), dtype=jnp.bfloat16):
    loudness = level_of(rng, extent, shards, -0.22, 0.18) if shards else 1.0
    values = jax.random.normal(rng, extent, jnp.float32) * scale * loudness
    return jnp.minimum(jnp.maximum(values, -bound), bound).astype(dtype)


def setup_inputs(seed: int = 0) -> dict:
    key_list = jax.random.split(jax.random.key(seed), 11)
    return {
        "images_in": bell_draw(key_list[0], (MB, IMAGES, SIDE, SIDE, CH), 1.0, 6.0, ((1, 8),)),
        "conv_local": bell_draw(key_list[1], (SECTIONS, 3, 3, CH, CL), (9 * CH) ** -0.5, 0.09375, ((0, 4),)),
        "conv_cross": bell_draw(key_list[2], (SECTIONS, 3, 3, CL, CG), (9 * CL) ** -0.5, 0.1875, ((0, 4),)),
        "reduce_weight": bell_draw(key_list[3], (SECTIONS, CG, CS), CG ** -0.5, 0.3125, ((0, 4),)),
        "spectral_weight": bell_draw(key_list[4], (SECTIONS, CG, CG), CG ** -0.5, 0.3125, ((0, 4),)),
        "expand_weight": bell_draw(key_list[5], (SECTIONS, CS, CG), CS ** -0.5, 0.4375, ((0, 4),)),
        "norm_gain": jnp.clip(0.5 + 1.0 * jax.random.uniform(key_list[6], (SECTIONS, NORMS), jnp.float32) ** level_of(key_list[6], (SECTIONS, NORMS), ((0, 4),), -0.2, 0.2), 0.5, 1.5),
        "norm_bias": bell_draw(key_list[7], (SECTIONS, NORMS), 0.5, 3.0, ((0, 4),), jnp.float32),
        "cotangent": bell_draw(key_list[8], (MB, IMAGES, SIDE, SIDE, CH), 1.0, 6.0, ((1, 8),)),
        "hole_mask": draw_hole_mask(jax.random.fold_in(key_list[10], 71), 0),
    }


EPS = 1e-05
HIGH = lax.Precision.HIGHEST

@jax.custom_vjp
def low(v):
    return lax.optimization_barrier(v.astype(jnp.bfloat16)).astype(jnp.float32)

@jax.custom_vjp
def low_back(v):
    return v

def low_keep(v):
    return (low(v), None)

def low_pass(kept, grad):
    return (grad,)

def back_keep(v):
    return (v, None)

def back_low(kept, grad):
    return (low(grad),)
low.defvjp(low_keep, low_pass)
low_back.defvjp(back_keep, back_low)

def smooth(values):
    return values * jax.nn.sigmoid(values)

def patches(values):
    height, breadth = (values.shape[1], values.shape[2])
    padded = jnp.pad(values, ((0, 0), (1, 1), (1, 1), (0, 0)))
    return jnp.concatenate([padded[:, row_off:row_off + height, col_off:col_off + breadth] for row_off in range(3) for col_off in range(3)], axis=-1)

def conv_apply(values, kernel):
    flat_kernel = kernel.reshape(-1, kernel.shape[-1])
    return jnp.einsum('bhwk,kd->bhwd', patches(values), flat_kernel, precision=HIGH)

def project(values, matrix):
    return jnp.einsum('bhwc,cd->bhwd', values, matrix, precision=HIGH)

def batch_norm(values, norm_gains, norm_biases):
    sum_axes = (0, 1, 2)
    average = lax.optimization_barrier(jnp.mean(values, axis=sum_axes))
    spread = lax.optimization_barrier(jnp.mean(jnp.square(values - average), axis=sum_axes))
    return (values - average) * lax.rsqrt(spread + EPS) * norm_gains + norm_biases

def section(inputs, local_kernel, cross_kernel, reduce_matrix, spectral_matrix, expand_matrix, norm_gains, norm_biases):
    local_part = inputs[..., :CL]
    global_part = inputs[..., CL:]
    pre_local = low_back(conv_apply(inputs, local_kernel))
    reduced = low_back(project(global_part, reduce_matrix))
    activated = smooth(batch_norm(reduced, norm_gains[:CS], norm_biases[:CS]))
    spectrum = jnp.fft.rfft2(activated, axes=(1, 2), norm='ortho')
    spec_low = low(jnp.concatenate([jnp.real(spectrum), jnp.imag(spectrum)], axis=-1))
    spectral_mix = low_back(project(spec_low, spectral_matrix))
    spectral_act = smooth(batch_norm(spectral_mix, norm_gains[CS:CS + CG], norm_biases[CS:CS + CG]))
    returned = jnp.fft.irfft2(lax.complex(spectral_act[..., :CS], spectral_act[..., CS:]), s=(SIDE, SIDE), axes=(1, 2), norm='ortho')
    joined = low(activated + returned)
    pre_global = low_back(conv_apply(local_part, cross_kernel) + project(joined, expand_matrix))
    pre_end = jnp.concatenate([pre_local, pre_global], axis=-1)
    return smooth(batch_norm(pre_end, norm_gains[CS + CG:], norm_biases[CS + CG:]))

def relay(params, probes, images, weighting):
    local_all, cross_all, reduce_all, spectral_all, expand_all, gains_all, biases_all = params
    current = images + probes[0]
    residual = current
    outgoing = current
    collected = []
    for section_index in range(SECTIONS):
        if section_index > 0:
            current = outgoing + probes[section_index]
        result = section(current, local_all[section_index], cross_all[section_index], reduce_all[section_index], spectral_all[section_index], expand_all[section_index], gains_all[section_index], biases_all[section_index])
        if section_index % 2 == 0:
            residual = current
            outgoing = low(low_back(result))
        else:
            outgoing = low(low_back(result + residual))
        collected.append(outgoing)
    objective = jnp.sum(outgoing * weighting)
    return (objective, jnp.stack(collected))

def reference(images_in, conv_local, conv_cross, reduce_weight, spectral_weight, expand_weight, norm_gain, norm_bias, cotangent, hole_mask):
    params = (conv_local.astype(jnp.float32), conv_cross.astype(jnp.float32), reduce_weight.astype(jnp.float32), spectral_weight.astype(jnp.float32), expand_weight.astype(jnp.float32), norm_gain, norm_bias)

    def one_batch(running, batch_inputs):
        images, cotan_batch, holes = batch_inputs
        hole_float = holes.astype(jnp.float32)
        pixels = SIDE * SIDE
        hole_counts = lax.optimization_barrier(jnp.sum(hole_float, axis=(1, 2), keepdims=True))
        weighting = cotan_batch.astype(jnp.float32) * (0.25 + hole_float * pixels / (hole_counts + pixels / 8.0))[..., None]
        probes = jnp.zeros((SECTIONS,) + images.shape, jnp.float32)
        images_float = images.astype(jnp.float32)

        def run_all(params_in, probes_in):
            return relay(params_in, probes_in, images_float, weighting)
        objective, pullback, collected = jax.vjp(run_all, params, probes, has_aux=True)
        grad_params, grad_probes = pullback(jnp.ones_like(objective))
        running = jax.tree.map(jnp.add, running, grad_params)
        return (running, (collected.astype(jnp.bfloat16), grad_probes))
    initial = jax.tree.map(jnp.zeros_like, params)
    totals, (outputs_all, grads_all) = lax.scan(one_batch, initial, (images_in, cotangent, hole_mask))
    activations = jnp.swapaxes(outputs_all, 0, 1)
    input_grads = jnp.swapaxes(grads_all, 0, 1)
    return (activations, input_grads, totals[0], totals[1], totals[2], totals[3], totals[4], totals[5], totals[6])
```

```python
import functools
import math

import jax
import jax.numpy as jnp
import numpy as np
from jax import lax
from jax.experimental import pallas as pl
from jax.experimental.pallas import tpu as pltpu
from jax.sharding import PartitionSpec as P

CL = 128
CG = 384
CS = 192
CH = 512
NORMS = 1088
F32 = jnp.float32
BF = jnp.bfloat16
UN = 2


EPS = 1e-05
HIGH = lax.Precision.HIGHEST


def from_behind(x, axis, by):
    length = lax.axis_size(axis)
    pairs = [(i, i + by) for i in range(length) if 0 <= i + by < length]
    return lax.ppermute(x, axis, pairs)


def smooth(values):
    return values * jax.nn.sigmoid(values)


def smooth_slope(values):
    logistic = jax.nn.sigmoid(values)
    return logistic * (1.0 + values * (1.0 - logistic))


def patches(values):
    height, breadth = (values.shape[1], values.shape[2])
    padded = jnp.pad(values, ((0, 0), (1, 1), (1, 1), (0, 0)))
    return jnp.concatenate(
        [
            padded[:, row_off : row_off + height, col_off : col_off + breadth]
            for row_off in range(3)
            for col_off in range(3)
        ],
        axis=-1,
    )


def conv_apply(values, kernel):
    flat_kernel = kernel.reshape(-1, kernel.shape[-1])
    return jnp.einsum(
        "bhwk,kd->bhwd", patches(values), flat_kernel, preferred_element_type=jnp.float32
    )


def conv_weight_grad(values, grad_low, kernel_shape):
    return jnp.einsum(
        "bhwk,bhwd->kd", patches(values), grad_low, preferred_element_type=jnp.float32
    ).reshape(kernel_shape)


def conv_input_grad(grad_low, kernel):
    flipped = jnp.flip(kernel, (0, 1)).transpose(0, 1, 3, 2)
    return conv_apply(grad_low, flipped)


def dft_tables(side_len):
    frequencies = side_len // 2 + 1
    spatial = jnp.arange(side_len, dtype=jnp.int32)
    spectral = jnp.arange(frequencies, dtype=jnp.int32)
    angle_cols = (spatial[:, None] * spectral[None, :] % side_len).astype(jnp.float32) * (
        2.0 * math.pi / side_len
    )
    angle_rows = (spatial[:, None] * spatial[None, :] % side_len).astype(jnp.float32) * (
        2.0 * math.pi / side_len
    )
    fold_factor = jnp.where((spectral == 0) | (2 * spectral == side_len), 1.0, 2.0).astype(
        jnp.float32
    )
    return (
        jnp.cos(angle_cols),
        jnp.sin(angle_cols),
        jnp.cos(angle_rows),
        jnp.sin(angle_rows),
        fold_factor,
    )


def to_spectrum(field_in, tables):
    cosine_cols, sine_cols, cosine_rows, sine_rows, _ = tables
    scaling = 1.0 / math.sqrt(field_in.shape[1] * field_in.shape[2])
    real_along = jnp.einsum("bhwc,wk->bhkc", field_in, cosine_cols, precision=HIGH)
    imaginary_along = -jnp.einsum("bhwc,wk->bhkc", field_in, sine_cols, precision=HIGH)
    real_part = jnp.einsum("bhkc,gh->bgkc", real_along, cosine_rows, precision=HIGH) + jnp.einsum(
        "bhkc,gh->bgkc", imaginary_along, sine_rows, precision=HIGH
    )
    imaginary_part = jnp.einsum(
        "bhkc,gh->bgkc", imaginary_along, cosine_rows, precision=HIGH
    ) - jnp.einsum("bhkc,gh->bgkc", real_along, sine_rows, precision=HIGH)
    return jnp.concatenate([real_part, imaginary_part], axis=-1) * scaling


def from_spectrum(field_in, tables):
    cosine_cols, sine_cols, cosine_rows, sine_rows, fold_factor = tables
    scaling = 1.0 / math.sqrt(field_in.shape[1] * cosine_cols.shape[0])
    half_width = field_in.shape[-1] // 2
    real_in = field_in[..., :half_width]
    imaginary_in = field_in[..., half_width:]
    real_rows = jnp.einsum("bgkc,gh->bhkc", real_in, cosine_rows, precision=HIGH) - jnp.einsum(
        "bgkc,gh->bhkc", imaginary_in, sine_rows, precision=HIGH
    )
    imaginary_rows = jnp.einsum(
        "bgkc,gh->bhkc", imaginary_in, cosine_rows, precision=HIGH
    ) + jnp.einsum("bgkc,gh->bhkc", real_in, sine_rows, precision=HIGH)
    folding = fold_factor[None, None, :, None]
    field_out = jnp.einsum(
        "bhkc,wk->bhwc", real_rows * folding, cosine_cols, precision=HIGH
    ) - jnp.einsum("bhkc,wk->bhwc", imaginary_rows * folding, sine_cols, precision=HIGH)
    return field_out * scaling


def moments(values):
    sum_axes = tuple(range(values.ndim - 1))
    count_all = math.prod(values.shape[:-1]) * lax.axis_size("dp")
    average = lax.psum(jnp.sum(values, axis=sum_axes), "dp") / count_all
    centred = values - average
    spread = lax.psum(jnp.sum(centred * centred, axis=sum_axes), "dp") / count_all
    return (average, lax.rsqrt(spread + EPS))


def norm_back(grad_out, act_values, hat_values, gain_slice, inv_std):
    sum_axes = tuple(range(act_values.ndim - 1))
    count_all = math.prod(act_values.shape[:-1]) * lax.axis_size("dp")
    grad_act = grad_out * smooth_slope(act_values)
    sum_act, sum_hat = lax.psum(
        (jnp.sum(grad_act, axis=sum_axes), jnp.sum(grad_act * hat_values, axis=sum_axes)), "dp"
    )
    grad_values = gain_slice * inv_std * (grad_act - (sum_act + hat_values * sum_hat) / count_all)
    return (grad_values, sum_hat, sum_act)


def section_compute(inputs, weights, norm_gains, norm_biases, measure, tables):
    local_kernel, cross_kernel, reduce_matrix, spectral_matrix, expand_matrix = weights

    def normalize(values, offset):
        extent = values.shape[-1]
        average, inv_std = measure(values, offset)
        hat_values = (values - average) * inv_std
        return (
            hat_values,
            norm_gains[offset : offset + extent] * hat_values
            + norm_biases[offset : offset + extent],
        )

    local_part = inputs[..., :CL]
    global_part = inputs[..., CL:]
    pre_local = conv_apply(inputs, local_kernel)
    reduced = jnp.einsum(
        "bhwc,cd->bhwd", global_part, reduce_matrix, preferred_element_type=jnp.float32
    )
    hat_one, act_one = normalize(reduced, 0)
    activated = smooth(act_one)
    spec_low = to_spectrum(activated, tables).astype(jnp.bfloat16)
    spectral_mix = jnp.einsum(
        "bhkc,cd->bhkd", spec_low, spectral_matrix, preferred_element_type=jnp.float32
    )
    hat_two, act_two = normalize(spectral_mix, CS)
    joined = (activated + from_spectrum(smooth(act_two), tables)).astype(jnp.bfloat16)
    pre_global = conv_apply(local_part, cross_kernel) + jnp.einsum(
        "bhwc,cd->bhwd", joined, expand_matrix, preferred_element_type=jnp.float32
    )
    hat_end, act_end = normalize(jnp.concatenate([pre_local, pre_global], axis=-1), CS + CG)
    return (
        smooth(act_end),
        (hat_one, act_one, activated, spec_low, hat_two, act_two, joined, hat_end, act_end),
    )


def section_backward(inputs, weights, norm_gains, inv_std, saved, grad_result, tables):
    local_kernel, cross_kernel, reduce_matrix, spectral_matrix, expand_matrix = weights
    hat_one, act_one, activated, spec_low, hat_two, act_two, joined, hat_end, act_end = saved
    local_part = inputs[..., :CL]
    global_part = inputs[..., CL:]
    grad_end, gain_end, bias_end = norm_back(
        grad_result, act_end, hat_end, norm_gains[CS + CG :], inv_std[CS + CG :]
    )
    grad_end_low = grad_end.astype(jnp.bfloat16)
    grad_pre_local = grad_end_low[..., :CL]
    grad_pre_global = grad_end_low[..., CL:]
    grad_cross = conv_weight_grad(local_part, grad_pre_global, cross_kernel.shape)
    grad_expand = jnp.einsum(
        "bhwc,bhwd->cd", joined, grad_pre_global, preferred_element_type=jnp.float32
    )
    grad_joined = jnp.einsum(
        "bhwd,cd->bhwc", grad_pre_global, expand_matrix, preferred_element_type=jnp.float32
    )
    _, inverse_pull = jax.vjp(
        lambda field_in: from_spectrum(field_in, tables), jnp.zeros(act_two.shape, jnp.float32)
    )
    (grad_after,) = inverse_pull(grad_joined)
    grad_mix, gain_two, bias_two = norm_back(
        grad_after, act_two, hat_two, norm_gains[CS : CS + CG], inv_std[CS : CS + CG]
    )
    grad_mix_low = grad_mix.astype(jnp.bfloat16)
    grad_spectral = jnp.einsum(
        "bhkc,bhkd->cd", spec_low, grad_mix_low, preferred_element_type=jnp.float32
    )
    grad_spec = jnp.einsum(
        "bhkd,cd->bhkc", grad_mix_low, spectral_matrix, preferred_element_type=jnp.float32
    )
    _, forward_pull = jax.vjp(lambda field_in: to_spectrum(field_in, tables), activated)
    (grad_activated,) = forward_pull(grad_spec)
    grad_reduced, gain_one, bias_one = norm_back(
        grad_activated + grad_joined, act_one, hat_one, norm_gains[:CS], inv_std[:CS]
    )
    grad_reduced_low = grad_reduced.astype(jnp.bfloat16)
    grad_reduce = jnp.einsum(
        "bhwc,bhwd->cd", global_part, grad_reduced_low, preferred_element_type=jnp.float32
    )
    grad_global = jnp.einsum(
        "bhwd,cd->bhwc", grad_reduced_low, reduce_matrix, preferred_element_type=jnp.float32
    )
    grad_local = conv_input_grad(grad_pre_global, cross_kernel)
    grad_local_kernel = conv_weight_grad(inputs, grad_pre_local, local_kernel.shape)
    grad_inputs = conv_input_grad(grad_pre_local, local_kernel) + jnp.concatenate(
        [grad_local, grad_global], axis=-1
    )
    gain_terms = jnp.concatenate([gain_one, gain_two, gain_end])
    bias_terms = jnp.concatenate([bias_one, bias_two, bias_end])
    return (
        grad_inputs,
        (grad_local_kernel, grad_cross, grad_reduce, grad_spectral, grad_expand),
        gain_terms,
        bias_terms,
    )


def store(buffer, value, slot_index, active):
    previous = lax.dynamic_index_in_dim(buffer, slot_index, 0, keepdims=False)
    return lax.dynamic_update_index_in_dim(
        buffer, jnp.where(active, value, previous), slot_index, 0
    )


def general_device(
    images_in,
    conv_local,
    conv_cross,
    reduce_weight,
    spectral_weight,
    expand_weight,
    norm_gain,
    norm_bias,
    cotangent,
    hole_mask,
):
    section_count = lax.axis_size("pipe")
    section_rank = lax.axis_index("pipe")
    batches = images_in.shape[0]
    step_count = batches + section_count - 1
    odd_section = section_rank % 2 == 1
    last_section = section_rank == section_count - 1
    weights = (conv_local[0], conv_cross[0], reduce_weight[0], spectral_weight[0], expand_weight[0])
    norm_gains = norm_gain[0]
    norm_biases = norm_bias[0]
    tables = dft_tables(images_in.shape[2])
    blank = jnp.zeros(images_in.shape[1:], jnp.bfloat16)

    def forward_step(carried, step_index):
        recv_act, recv_res, kept_inputs, kept_stats, kept_outputs = carried
        batch_index = step_index - section_rank
        active = (batch_index >= 0) & (batch_index < batches)
        slot_index = jnp.clip(batch_index, 0, batches - 1)
        fresh_image = lax.dynamic_index_in_dim(images_in, slot_index, 0, keepdims=False)
        inputs = jnp.where(section_rank == 0, fresh_image, recv_act)
        recorded = []

        def measure(values, offset):
            average, inv_std = moments(values)
            recorded.append((average, inv_std))
            return (average, inv_std)

        result, _ = section_compute(inputs, weights, norm_gains, norm_biases, measure, tables)
        summed = result + jnp.where(odd_section, recv_res.astype(jnp.float32), 0.0)
        outgoing = summed.astype(jnp.bfloat16)
        residual_out = jnp.where(odd_section, outgoing, inputs)
        next_act, next_res = from_behind((outgoing, residual_out), "pipe", 1)
        statistics = jnp.stack(
            [
                jnp.concatenate([entry_pair[0] for entry_pair in recorded]),
                jnp.concatenate([entry_pair[1] for entry_pair in recorded]),
            ]
        )
        kept_inputs = store(kept_inputs, inputs, slot_index, active)
        kept_stats = store(kept_stats, statistics, slot_index, active)
        kept_outputs = store(kept_outputs, outgoing, slot_index, active)
        return ((next_act, next_res, kept_inputs, kept_stats, kept_outputs), None)

    forward_init = (
        blank,
        blank,
        jnp.zeros(images_in.shape, jnp.bfloat16),
        jnp.zeros((batches, 2, NORMS), jnp.float32),
        jnp.zeros(images_in.shape, jnp.bfloat16),
    )
    forward_state = lax.scan(forward_step, forward_init, jnp.arange(step_count))[0]
    kept_inputs, kept_stats, kept_outputs = (forward_state[2], forward_state[3], forward_state[4])
    pixels = images_in.shape[2] * images_in.shape[3]
    hole_float = hole_mask.astype(jnp.float32)
    hole_counts = jnp.sum(hole_float, axis=(2, 3), keepdims=True)
    weighting = 0.25 + hole_float * pixels / (hole_counts + pixels / 8.0)

    def backward_step(carried, step_index):
        recv_grad, recv_res, grad_store, weight_sums, gain_sum, bias_sum = carried
        batch_index = step_index - (section_count - 1 - section_rank)
        active = (batch_index >= 0) & (batch_index < batches)
        slot_index = jnp.clip(batch_index, 0, batches - 1)
        cotan_slot = lax.dynamic_index_in_dim(cotangent, slot_index, 0, keepdims=False).astype(
            jnp.float32
        )
        weight_slot = lax.dynamic_index_in_dim(weighting, slot_index, 0, keepdims=False)
        seed_grad = (cotan_slot * weight_slot[..., None]).astype(jnp.bfloat16)
        incoming = jnp.where(last_section, seed_grad, recv_grad)
        inputs = lax.dynamic_index_in_dim(kept_inputs, slot_index, 0, keepdims=False)
        statistics = lax.dynamic_index_in_dim(kept_stats, slot_index, 0, keepdims=False)

        def measure(values, offset):
            extent = values.shape[-1]
            return (
                statistics[0, offset : offset + extent],
                statistics[1, offset : offset + extent],
            )

        _, saved = section_compute(inputs, weights, norm_gains, norm_biases, measure, tables)
        grad_inputs, weight_terms, gain_terms, bias_terms = section_backward(
            inputs, weights, norm_gains, statistics[1], saved, incoming.astype(jnp.float32), tables
        )
        grad_total = grad_inputs + jnp.where(odd_section, 0.0, recv_res.astype(jnp.float32))
        outgoing = grad_total.astype(jnp.bfloat16)
        residual_out = jnp.where(odd_section, incoming, outgoing)
        next_grad, next_res = from_behind((outgoing, residual_out), "pipe", -1)
        weight_sums = tuple(
            (
                running + jnp.where(active, addend, 0.0)
                for running, addend in zip(weight_sums, weight_terms)
            )
        )
        gain_sum = gain_sum + jnp.where(active, gain_terms, 0.0)
        bias_sum = bias_sum + jnp.where(active, bias_terms, 0.0)
        grad_store = store(grad_store, grad_total, slot_index, active)
        return ((next_grad, next_res, grad_store, weight_sums, gain_sum, bias_sum), None)

    zero_weights = tuple((jnp.zeros(entry_weight.shape, jnp.float32) for entry_weight in weights))
    backward_init = (
        blank,
        blank,
        jnp.zeros(images_in.shape, jnp.float32),
        zero_weights,
        jnp.zeros((NORMS,), jnp.float32),
        jnp.zeros((NORMS,), jnp.float32),
    )
    state_end = lax.scan(backward_step, backward_init, jnp.arange(0, 0 + step_count))[0]
    sum_local, sum_cross, sum_reduce, sum_spectral, sum_expand = state_end[3]
    totals = lax.psum((sum_local, sum_cross, sum_reduce, sum_spectral, sum_expand), "dp")
    return (
        kept_outputs[None],
        state_end[2][None],
        totals[0][None],
        totals[1][None],
        totals[2][None],
        totals[3][None],
        totals[4][None],
        state_end[4][None],
        state_end[5][None],
    )


def dft_np(side):
    spatial = np.arange(side)
    spectral = np.arange(side // 2 + 1)
    turns = spatial[:, None, None, None] * spatial[None, None, :, None] + spectral[None, :, None, None] * spatial[None, None, None, :]
    angle = (turns % side).reshape(side * spectral.size, side * side) * (2.0 * np.pi / side)
    fold = np.broadcast_to(np.where((spectral == 0) | (2 * spectral == side), 1.0, 2.0), (side, spectral.size)).reshape(-1, 1)
    forward = np.concatenate([np.cos(angle), -np.sin(angle)]) / side
    inverse = np.concatenate([np.cos(angle) * fold, -np.sin(angle) * fold]).T / side
    return forward, inverse


def dot(a, b):
    return lax.dot_general(a, b, (((1,), (0,)), ((), ())), preferred_element_type=F32)


def dot_nt(a, b):
    return lax.dot_general(a, b, (((1,), (1,)), ((), ())), preferred_element_type=F32)


def dot_tn(a, b):
    return lax.dot_general(a, b, (((0,), (0,)), ((), ())), preferred_element_type=F32)


def sig(u):
    return 0.5 * jnp.tanh(0.5 * u) + 0.5


def slope(u):
    s = sig(u)
    return s * (1.0 + u * (1.0 - s))


QUARTERS, QROWS = 4, 2688
LAYOUT = {
    "local": (0, 1152, 1),
    "cross": (1152, 288, 3),
    "reduce": (2016, 96, 2),
    "spectral": (2208, 96, 3),
    "expand": (2496, 48, 3),
    "norms": (2640, 16, 3),
}


def pieces(name, start, count, block=0):
    base, rows, _ = LAYOUT[name]
    found = []
    while count:
        quarter, offset = divmod(start, rows)
        take = min(count, rows - offset)
        found.append((quarter, base + block * rows + offset, take))
        start, count = start + take, count - take
    return found


def stack_rows(parts):
    return parts[0] if len(parts) == 1 else jnp.concatenate(parts, axis=0)


def stack_cols(parts):
    return parts[0] if len(parts) == 1 else jnp.concatenate(parts, axis=1)


def read(w, name, start, count):
    blocks = LAYOUT[name][2]
    return stack_cols([stack_rows([w[q, r : r + n] for q, r, n in pieces(name, start, count, j)]) for j in range(blocks)])


def write(w, name, start, value):
    for j in range(LAYOUT[name][2]):
        done = 0
        for q, r, n in pieces(name, start, value.shape[0], j):
            w[q, r : r + n] = value[done : done + n, j * 128 : (j + 1) * 128].astype(w.dtype)
            done += n


def read_norms(w):
    base = LAYOUT["norms"][0]
    rows = stack_cols([w[j // 3, base + 16 * (j % 3) : base + 16 * (j % 3) + 16] for j in range(9)]).astype(F32)[:, :NORMS]
    return rows[0:1] + rows[1:2], rows[2:3] + rows[3:4]


def conv_matrix(w):
    return stack_rows([stack_cols([read(w, "local", k * CH, CL), read(w, "cross", k * CL, CL)]) for k in range(9)])


def global_matrix(w):
    return stack_cols([read(w, "local", k * CH + CL, CG) for k in range(9)])


def pack_section(conv_local, conv_cross, reduce_weight, spectral_weight, expand_weight, norm_gain, norm_bias):
    def blocks(matrix):
        rows, columns = matrix.shape
        wide = -(-columns // 128) * 128
        matrix = jnp.pad(matrix, ((0, 0), (0, wide - columns)))
        return matrix.reshape(QUARTERS, rows // QUARTERS, wide // 128, 128).transpose(0, 2, 1, 3).reshape(QUARTERS, -1, 128)

    halves = []
    for values in (norm_gain, norm_bias):
        high = values.astype(BF)
        halves += [high, (values - high.astype(F32)).astype(BF)]
    norms = jnp.pad(jnp.stack(halves), ((0, 12), (0, 12 * 128 - NORMS)))
    norms = norms.reshape(16, QUARTERS, 3, 128).transpose(1, 2, 0, 3).reshape(QUARTERS, 48, 128)
    return jnp.concatenate(
        [
            conv_local.reshape(QUARTERS, -1, 128),
            blocks(conv_cross.reshape(-1, CG)),
            blocks(reduce_weight),
            blocks(spectral_weight),
            blocks(expand_weight),
            norms,
        ],
        axis=1,
    )


def unpack_section(packed):
    def matrix(name, columns):
        base, rows, blocks = LAYOUT[name]
        part = packed[:, base : base + rows * blocks].reshape(QUARTERS, blocks, rows, 128).transpose(0, 2, 1, 3)
        return part.reshape(QUARTERS * rows, blocks * 128)[:, :columns]

    return matrix("local", CL), matrix("cross", CG), matrix("reduce", CS), matrix("spectral", CG), matrix("expand", CG)


SOURCES = (
    (("own", "own"), ("x1", "x2"), ("y1", "y2"), ("x3", "y3")),
    (("x1", "x2"), ("own", "own"), ("y3", "x3"), ("y1", "y2")),
    (("y2", "y1"), ("x3", "y3"), ("own", "own"), ("x1", "x2")),
    (("y2", "x2"), ("y1", "y3"), ("x1", "x3"), ("own", "own")),
)


def load_weights(place, arrived, low, high, w, sems):
    rank, core = place[0], place[1]
    for s in range(low, high):
        for r, sources in enumerate(SOURCES):

            @pl.when(rank == r)
            def _():
                for half, name in enumerate(sources[s]):
                    for other in range(2):
                        quarter = 2 * half + (1 - core if other else core)
                        src = arrived["own"].at[quarter] if name == "own" else arrived[name][other]
                        pltpu.make_async_copy(src, w.at[s - low, quarter], sems.at[s - low, 2 * half + other]).start()


def wait_weights(own, index, w, sems):
    for n in range(4):
        pltpu.make_async_copy(own.at[0], w.at[index, 0], sems.at[index, n]).wait()


def moments_of(v):
    mean = jnp.mean(v, axis=0, keepdims=True)
    centred = v - mean
    return mean, jnp.sum(centred * centred, axis=0, keepdims=True)


def combined(mean_ref, square_ref, rows):
    images = mean_ref.shape[0]
    means = [mean_ref[b] for b in range(images)]
    mean = sum(means) / images
    total = sum(square_ref[b] + rows * (means[b] - mean) ** 2 for b in range(images))
    return mean, lax.rsqrt(total / (images * rows) + EPS)


def beside(v, column, by, side):
    if by < 0:
        return jnp.where(column == 0, 0.0, pltpu.roll(v, 1, 0))
    return jnp.where(column == side - 1, 0.0, pltpu.roll(v, v.shape[0] - 1, 0))


def three_columns(dst, b, x, column, side):
    pixels = x.shape[0]
    wide = x.astype(F32)
    for i, v in enumerate((beside(wide, column, -1, side).astype(BF), x, beside(wide, column, 1, side).astype(BF))):
        dst[i, b, 0:side] = jnp.zeros((side, CL), BF)
        dst[i, b, side : side + pixels] = v
        dst[i, b, side + pixels : 2 * side + pixels] = jnp.zeros((side, CL), BF)


def nine(src, b, side, flipped):
    pixels = side * side
    parts = []
    for dh in range(3):
        for dw in range(3):
            i, j = (2 - dh, 2 - dw) if flipped else (dh, dw)
            parts.append(src[j, b, i * side : i * side + pixels])
    return parts


def forward_kernel(cfg, *refs):
    low, high, parts, has_prev, side, images = cfg
    refs = list(refs)
    take = lambda n: [refs.pop(0) for _ in range(n)]
    (place,) = take(1)
    a_parts = take(parts)
    prev_parts = take(has_prev)
    (own,) = take(1)
    names = needed(low, high)
    arrived = {n: take(2) for n in names}
    arrived["own"] = own
    mf, mi = take(2)
    if low > 0:
        take(4)
    (out,) = take(1) if high < 4 else (None,)
    vh1_o, vh2_o, vh3_o, iv_o, own_in, own_out, own_spec, own_join = take(8)
    (cur, w, xp, q, t, f, p, v1, v2, v3, sv, jv, mu1, sq1, mu2, sq2, mu3, sq3, zb, wsem, asem, psem, osem, ksem) = refs
    pixels = side * side
    modes = side * (side // 2 + 1)
    rank = place[0]
    column = lax.broadcasted_iota(jnp.int32, (pixels, 1), 0) % side
    load_weights(place, arrived, low, high, w, wsem)

    def fill(sources, slot, sem):
        rows = images * pixels // max(len(sources), 1)
        return [pltpu.make_async_copy(ref, cur.at[slot, pl.ds(k * rows, rows)], sem.at[k]) for k, ref in enumerate(sources)]

    copies = fill(a_parts, low % 2, asem) + fill(prev_parts, (low + 1) % 2, psem)
    for c in copies:
        c.start()
    zb[0:side] = jnp.zeros((side, 9 * CL), F32)
    zb[side + pixels : 2 * side + pixels] = jnp.zeros((side, 9 * CL), F32)
    for c in copies:
        c.wait()

    def rows_of(b):
        return pl.ds(pl.multiple_of(b * pixels, pixels), pixels)

    def modes_of(b):
        return pl.ds(pl.multiple_of(b * modes, modes), modes)

    def section(index, _):
        s = index + low
        a = cur.at[s % 2]
        o = cur.at[(s + 1) % 2]
        ws = w.at[index]
        mine = rank == s
        first = index == 0
        saves = [
            pltpu.make_async_copy(v1, vh1_o.at[index], osem.at[0]),
            pltpu.make_async_copy(v2, vh2_o.at[index], osem.at[1]),
            pltpu.make_async_copy(v3, vh3_o.at[index], osem.at[2]),
        ]
        keeps = [
            pltpu.make_async_copy(a, own_in, ksem.at[0]),
            pltpu.make_async_copy(o, own_out, ksem.at[1]),
            pltpu.make_async_copy(sv, own_spec, ksem.at[2]),
            pltpu.make_async_copy(jv, own_join, ksem.at[3]),
        ]

        @pl.when(mine)
        def _():
            keeps[0].start()

        wait_weights(own, index, w, wsem)
        gain, bias = read_norms(ws)

        def reduce_step(b, _):
            r = rows_of(b)
            three_columns(xp, b, a[r, 0:CL], column, side)
            v = dot(a[r, CL:CH], read(ws, "reduce", 0, CG))[:, :CS]
            q[r] = v
            mu1[b], sq1[b] = moments_of(v)
            return 0

        lax.fori_loop(0, images, reduce_step, 0, unroll=UN)
        mean1, inv1 = combined(mu1, sq1, pixels)

        @pl.when(jnp.logical_not(first))
        def _():
            saves[0].wait()

        def spectral_step(b, _):
            r, rs = rows_of(b), modes_of(b)
            hat = (q[r] - mean1) * inv1
            v1[r] = hat.astype(BF)
            u = hat * gain[:, :CS] + bias[:, :CS]
            act = u * sig(u)
            t[r] = act
            spec = dot(mf[...], act.astype(BF)).astype(BF)
            real, imaginary = spec[:modes], spec[modes:]
            sv[0, rs] = real
            sv[1, rs] = imaginary
            mix = dot(real, read(ws, "spectral", 0, CS)) + dot(imaginary, read(ws, "spectral", CS, CS))
            f[rs] = mix
            mu2[b], sq2[b] = moments_of(mix)
            p[r] = dot(stack_cols(nine(xp, b, side, False)), conv_matrix(ws))
            return 0

        lax.fori_loop(0, images, spectral_step, 0, unroll=UN)
        saves[0].start()

        @pl.when(mine)
        def _():
            keeps[2].start()

        mean2, inv2 = combined(mu2, sq2, modes)

        @pl.when(jnp.logical_not(first))
        def _():
            saves[1].wait()

        def join_step(b, _):
            r, rs = rows_of(b), modes_of(b)
            hat = (f[rs] - mean2) * inv2
            v2[rs] = hat.astype(BF)
            u = hat * gain[:, CS : CS + CG] + bias[:, CS : CS + CG]
            e = u * sig(u)
            e = stack_rows([e[:, :CS], e[:, CS:]]).astype(BF)
            j = (t[r] + dot(mi[...], e)).astype(BF)
            jv[r] = j
            pre_global = p[r, CL:CH] + dot(j, read(ws, "expand", 0, CS))
            zb[side : side + pixels] = dot(a[r, CL:CH], global_matrix(ws))
            ys = []
            for dw in range(3):
                ys.append(sum(zb[dh * side : dh * side + pixels, (dh * 3 + dw) * CL : (dh * 3 + dw + 1) * CL] for dh in range(3)))
            pre_local = p[r, 0:CL] + ys[1] + beside(ys[0], column, -1, side) + beside(ys[2], column, 1, side)
            p[r, 0:CL] = pre_local
            p[r, CL:CH] = pre_global
            ml, sl = moments_of(pre_local)
            mg, sg = moments_of(pre_global)
            mu3[b] = stack_cols([ml, mg])
            sq3[b] = stack_cols([sl, sg])
            return 0

        lax.fori_loop(0, images, join_step, 0, unroll=UN)
        saves[1].start()

        @pl.when(mine)
        def _():
            keeps[3].start()

        mean3, inv3 = combined(mu3, sq3, pixels)

        @pl.when(jnp.logical_not(first))
        def _():
            saves[2].wait()

        odd = s % 2 == 1

        def end_step(b, _):
            r = rows_of(b)
            hat = (p[r] - mean3) * inv3
            v3[r] = hat.astype(BF)
            u = hat * gain[:, CS + CG :] + bias[:, CS + CG :]
            y = u * sig(u)
            if high > 1:
                y = y + jnp.where(odd, o[r].astype(F32), 0.0)
            o[r] = y.astype(BF)
            return 0

        lax.fori_loop(0, images, end_step, 0, unroll=UN)
        saves[2].start()
        iv_o[index] = stack_cols([inv1, inv2, inv3])

        @pl.when(mine)
        def _():
            keeps[1].start()
            for k in keeps:
                k.wait()

        return 0

    lax.fori_loop(0, high - low, section, 0)
    last = [
        pltpu.make_async_copy(v1, vh1_o.at[0], osem.at[0]),
        pltpu.make_async_copy(v2, vh2_o.at[0], osem.at[1]),
        pltpu.make_async_copy(v3, vh3_o.at[0], osem.at[2]),
    ]
    if out is not None:
        last.append(pltpu.make_async_copy(cur.at[high % 2], out, asem.at[0]))
        last[-1].start()
    for c in last:
        c.wait()


def needed(low, high):
    return sorted({name for sources in SOURCES for s in range(low, high) for name in sources[s]} - {"own"})


ANY = pl.BlockSpec(memory_space=pl.ANY)
VMEM = pl.BlockSpec(memory_space=pltpu.VMEM)
SMEM = pl.BlockSpec(memory_space=pltpu.SMEM)
VMEM_LIMIT = 63 * 2**20


def forward_call(low, high, place, a_parts, prev_parts, own, arrived, mf, mi, kept, side, images):
    pixels, modes = side * side, side * (side // 2 + 1)
    n, m, count = images * pixels, images * modes, high - low
    names = needed(low, high)
    ins = [place, *a_parts, *prev_parts, own]
    specs = [SMEM] + [ANY] * (len(ins) - 1)
    for name in names:
        ins += arrived[name]
        specs += [ANY, ANY]
    ins += [mf, mi]
    specs += [VMEM, VMEM]
    aliases = {}
    if low > 0:
        for i, x in enumerate(kept):
            aliases[len(ins)] = 4 + (high < 4) + i
            ins.append(x)
            specs.append(ANY)
    shape = jax.ShapeDtypeStruct
    outs = [shape((n, CH), BF)] if high < 4 else []
    outs += [
        shape((count, n, CS), BF),
        shape((count, m, CG), BF),
        shape((count, n, CH), BF),
        shape((count, 1, NORMS), F32),
        shape((n, CH), BF),
        shape((n, CH), BF),
        shape((2, m, CS), BF),
        shape((n, CS), BF),
    ]
    out_specs = [ANY] * (3 + (high < 4)) + [VMEM] + [ANY] * 4
    dma = pltpu.SemaphoreType.DMA
    scratch = [
        pltpu.VMEM((2, n, CH), BF),
        pltpu.VMEM((count, QUARTERS, QROWS, 128), BF),
        pltpu.VMEM((3, images, pixels + 2 * side, CL), BF),
        pltpu.VMEM((n, CS), F32),
        pltpu.VMEM((n, CS), F32),
        pltpu.VMEM((m, CG), F32),
        pltpu.VMEM((n, CH), F32),
        pltpu.VMEM((n, CS), BF),
        pltpu.VMEM((m, CG), BF),
        pltpu.VMEM((n, CH), BF),
        pltpu.VMEM((2, m, CS), BF),
        pltpu.VMEM((n, CS), BF),
        *[pltpu.VMEM((images, 1, c), F32) for c in (CS, CS, CG, CG, CH, CH)],
        pltpu.VMEM((pixels + 2 * side, 9 * CL), F32),
        dma((count, 4)),
        dma((max(len(a_parts), 1),)),
        dma((max(len(prev_parts), 1),)),
        dma((3,)),
        dma((4,)),
    ]
    cfg = (low, high, len(a_parts), len(prev_parts), side, images)
    return pl.pallas_call(
        functools.partial(forward_kernel, cfg),
        out_shape=outs,
        in_specs=specs,
        out_specs=out_specs,
        scratch_shapes=scratch,
        input_output_aliases=aliases,
        name=f"forward_{low}_{high}",
        cost_estimate=pl.CostEstimate(flops=count * images * 650_000_000, bytes_accessed=count * 10_000_000, transcendentals=0),
        compiler_params=pltpu.CompilerParams(vmem_limit_bytes=VMEM_LIMIT),
    )(*ins)


def backward_kernel(cfg, *refs):
    low, high, parts, has_above, side, images = cfg
    refs = list(refs)
    take = lambda n: [refs.pop(0) for _ in range(n)]
    (place,) = take(1)
    g_parts = take(parts)
    above = take(has_above)
    (own,) = take(1)
    arrived = {n: take(2) for n in needed(low, high)}
    arrived["own"] = own
    mft, mit, vh1, vh2, vh3, iv, own_in, own_spec, own_join = take(9)
    g_outs = take(parts) if low > 0 else []
    (above_out,) = take(1) if low > 0 else (None,)
    ab, own_grad, own_terms = take(3)
    (grad, w, xp, du, du1, du2, dj, dxl, dxg, zb, dpv, dqv, dfv, h1, h2, h3, ain, sv, jv, x9, d9, terms) = refs[:22]
    wsem, gsem, asem, hsem, ksem, osem = refs[22:]
    pixels = side * side
    modes = side * (side // 2 + 1)
    n1, n2 = float(images * pixels), float(images * modes)
    count = high - low
    rank = place[0]
    column = lax.broadcasted_iota(jnp.int32, (pixels, 1), 0) % side

    def fill(sources, slot, sem):
        rows = images * pixels // max(len(sources), 1)
        return [pltpu.make_async_copy(ref, grad.at[slot, pl.ds(k * rows, rows)], sem.at[k]) for k, ref in enumerate(sources)]

    def hats(index, slot):
        return [
            pltpu.make_async_copy(vh3.at[index], h3.at[slot], hsem.at[slot, 0]),
            pltpu.make_async_copy(vh2.at[index], h2.at[slot], hsem.at[slot, 1]),
            pltpu.make_async_copy(vh1.at[index], h1.at[slot], hsem.at[slot, 2]),
        ]

    top = high - 1
    copies = fill(g_parts, top % 2, gsem) + fill(above, (top + 1) % 2, asem)
    for c in copies + hats(count - 1, top % 2):
        c.start()
    load_weights(place, arrived, low, high, w, wsem)

    owns = [
        pltpu.make_async_copy(own_in, ain, ksem.at[0]),
        pltpu.make_async_copy(own_spec, sv, ksem.at[1]),
        pltpu.make_async_copy(own_join, jv, ksem.at[2]),
    ]
    in_range = jnp.logical_and(rank >= low, rank < high)

    @pl.when(in_range)
    def _():
        for c in owns:
            c.start()

    zb[0:side] = jnp.zeros((side, 9 * CL), F32)
    zb[side + pixels : 2 * side + pixels] = jnp.zeros((side, 9 * CL), F32)
    for c in copies:
        c.wait()

    def rows_of(b):
        return pl.ds(pl.multiple_of(b * pixels, pixels), pixels)

    def modes_of(b):
        return pl.ds(pl.multiple_of(b * modes, modes), modes)

    def part(v):
        return jnp.sum(v.reshape(v.shape[0] // 8, 8, v.shape[1]), axis=0)

    def fin(v):
        return jnp.sum(v, axis=0, keepdims=True)

    def none(c):
        return jnp.zeros((8, c), F32), jnp.zeros((8, c), F32)

    def section(step, _):
        index = count - 1 - step
        s = low + index
        slot = s % 2
        g = grad.at[s % 2]
        o = grad.at[(s + 1) % 2]
        ws = w.at[index]
        v1, v2, v3 = h1.at[slot], h2.at[slot], h3.at[slot]
        mine = rank == s
        for c in hats(index, slot):
            c.wait()

        @pl.when(index > 0)
        def _():
            for c in hats(index - 1, 1 - slot):
                c.start()

        wait_weights(own, index, w, wsem)
        gain, bias = read_norms(ws)
        inv = iv[index]
        g1, g2, g3 = gain[:, :CS], gain[:, CS : CS + CG], gain[:, CS + CG :]
        b1, b2, b3 = bias[:, :CS], bias[:, CS : CS + CG], bias[:, CS + CG :]
        c1, c2, c3 = g1 * inv[:, :CS], g2 * inv[:, CS : CS + CG], g3 * inv[:, CS + CG :]

        def end_step(b, c):
            r = rows_of(b)
            hat = v3[r].astype(F32)
            d = g[r].astype(F32) * slope(g3 * hat + b3)
            du[r] = d
            return c[0] + part(d), c[1] + part(d * hat)

        suma, sumb = lax.fori_loop(0, images, end_step, none(CH), unroll=UN)
        suma3, sumb3 = fin(suma), fin(sumb)
        mean_a3, mean_b3 = suma3 / n1, sumb3 / n1

        def join_step(b, c):
            r, rs = rows_of(b), modes_of(b)
            dp = (c3 * (du[r] - (mean_a3 + v3[r].astype(F32) * mean_b3))).astype(BF)
            dpv[r] = dp
            three_columns(xp, b, dp[:, :CL], column, side)
            djv = dot_nt(dp[:, CL:], read(ws, "expand", 0, CS))
            dj[r] = djv
            de = dot(mit[...], djv.astype(BF))
            de = stack_cols([de[:modes], de[modes:]])
            hat = v2[rs].astype(F32)
            d = de * slope(g2 * hat + b2)
            du2[rs] = d
            zb[side : side + pixels] = dot_nt(dp, conv_matrix(ws))
            ys = []
            for dw in range(3):
                ys.append(
                    sum(zb[(2 - dh) * side : (2 - dh) * side + pixels, (dh * 3 + dw) * CL : (dh * 3 + dw + 1) * CL] for dh in range(3))
                )
            dxl[r] = ys[1] + beside(ys[0], column, 1, side) + beside(ys[2], column, -1, side)
            return c[0] + part(d), c[1] + part(d * hat)

        suma, sumb = lax.fori_loop(0, images, join_step, none(CG), unroll=UN)
        suma2, sumb2 = fin(suma), fin(sumb)
        mean_a2, mean_b2 = suma2 / n2, sumb2 / n2

        def spectral_step(b, c):
            r, rs = rows_of(b), modes_of(b)
            df = (c2 * (du2[rs] - (mean_a2 + v2[rs].astype(F32) * mean_b2))).astype(BF)
            dfv[rs] = df
            ds = dot_nt(df, read(ws, "spectral", 0, CG))
            ds = stack_rows([ds[:, :CS], ds[:, CS:]]).astype(BF)
            dt = dj[r] + dot(mft[...], ds)
            hat = v1[r].astype(F32)
            d = dt * slope(g1 * hat + b1)
            du1[r] = d
            dxg[r] = dot_nt(stack_cols(nine(xp, b, side, True)), global_matrix(ws))
            return c[0] + part(d), c[1] + part(d * hat)

        suma, sumb = lax.fori_loop(0, images, spectral_step, none(CS), unroll=UN)
        suma1, sumb1 = fin(suma), fin(sumb)
        mean_a1, mean_b1 = suma1 / n1, sumb1 / n1
        even = s % 2 == 0

        def reduce_step(b, c):
            r = rows_of(b)
            dq = (c1 * (du1[r] - (mean_a1 + v1[r].astype(F32) * mean_b1))).astype(BF)
            dqv[r] = dq
            dx = stack_cols([dxl[r], dxg[r] + dot_nt(dq, read(ws, "reduce", 0, CG)[:, :CS])])
            if low < 3:
                dx = dx + jnp.where(even, o[r].astype(F32), 0.0)
            o[r] = dx.astype(BF)
            return c

        lax.fori_loop(0, images, reduce_step, 0, unroll=UN)
        ab[index, 0:1] = stack_cols([suma1, suma2, suma3])
        ab[index, 1:2] = stack_cols([sumb1, sumb2, sumb3])

        @pl.when(mine)
        def _():
            keep = pltpu.make_async_copy(o, own_grad, osem.at[0])
            keep.start()
            for c in owns:
                c.wait()

            def nine_step(b, _):
                r = rows_of(b)
                for k, v in enumerate(nine(xp, b, side, True)):
                    d9[r, k * CL : (k + 1) * CL] = v
                return 0

            lax.fori_loop(0, images, nine_step, 0)

            def nine_inputs(b, _):
                r = rows_of(b)
                three_columns(xp, b, ain[r, 0:CL], column, side)
                for k, v in enumerate(nine(xp, b, side, False)):
                    x9[r, k * CL : (k + 1) * CL] = v
                return 0

            lax.fori_loop(0, images, nine_inputs, 0)
            for dh in range(3):
                v = dot_tn(x9[:, dh * 3 * CL : (dh + 1) * 3 * CL], dpv[...])
                for dw in range(3):
                    k = dh * 3 + dw
                    write(terms, "local", k * CH, v[dw * CL : (dw + 1) * CL, :CL])
                    write(terms, "cross", k * CL, v[dw * CL : (dw + 1) * CL, CL:])
            for dh in range(3):
                v = dot_tn(ain[:, CL:], d9[:, dh * 3 * CL : (dh + 1) * 3 * CL])
                for dw in range(3):
                    write(terms, "local", (dh * 3 + dw) * CH + CL, v[:, dw * CL : (dw + 1) * CL])
            v = dot_tn(ain[:, CL:], dqv[...])
            write(terms, "reduce", 0, stack_cols([v, jnp.zeros((CG, 256 - CS), F32)]))
            write(terms, "spectral", 0, dot_tn(sv[0], dfv[...]))
            write(terms, "spectral", CS, dot_tn(sv[1], dfv[...]))
            write(terms, "expand", 0, dot_tn(jv[...], dpv[:, CL:]))
            for quarter in range(QUARTERS):
                terms[quarter, LAYOUT["norms"][0] :] = jnp.zeros((48, 128), BF)
            send = pltpu.make_async_copy(terms, own_terms, osem.at[1])
            send.start()
            send.wait()
            keep.wait()

        return 0

    lax.fori_loop(0, count, section, 0)
    if low > 0:
        rows = images * pixels // parts
        finals = [pltpu.make_async_copy(grad.at[low % 2], above_out, asem.at[0])]
        for k, ref in enumerate(g_outs):
            finals.append(pltpu.make_async_copy(grad.at[(low + 1) % 2, pl.ds(k * rows, rows)], ref, gsem.at[k]))
        for c in finals:
            c.start()
        for c in finals:
            c.wait()


def backward_call(low, high, place, g_parts, above, own, arrived, mft, mit, hats, iv, kept, side, images):
    pixels, modes = side * side, side * (side // 2 + 1)
    n, m, count = images * pixels, images * modes, high - low
    own_in, own_spec, own_join = kept
    ins = [place, *g_parts, *above, own]
    specs = [SMEM] + [ANY] * (len(ins) - 1)
    own_at = len(ins) - 1
    for name in needed(low, high):
        ins += arrived[name]
        specs += [ANY, ANY]
    ins += [mft, mit, *hats, iv, own_in, own_spec, own_join]
    specs += [VMEM, VMEM, ANY, ANY, ANY, VMEM, ANY, ANY, ANY]
    shape = jax.ShapeDtypeStruct
    outs, out_specs, aliases = [], [], {}
    if low > 0:
        outs += [shape(g.shape, BF) for g in g_parts] + [shape((n, CH), BF)]
        out_specs += [ANY] * len(outs)
        aliases = {1 + k: k for k in range(len(g_parts))}
    aliases[len(ins) - 3] = len(outs) + 1
    aliases[own_at] = len(outs) + 2
    outs += [shape((count, 2, NORMS), F32), shape((n, CH), BF), shape((QUARTERS, QROWS, 128), BF)]
    out_specs += [VMEM, ANY, ANY]
    dma = pltpu.SemaphoreType.DMA
    scratch = [
        pltpu.VMEM((2, n, CH), BF),
        pltpu.VMEM((count, QUARTERS, QROWS, 128), BF),
        pltpu.VMEM((3, images, pixels + 2 * side, CL), BF),
        pltpu.VMEM((n, CH), F32),
        pltpu.VMEM((n, CS), F32),
        pltpu.VMEM((m, CG), F32),
        pltpu.VMEM((n, CS), F32),
        pltpu.VMEM((n, CL), F32),
        pltpu.VMEM((n, CG), F32),
        pltpu.VMEM((pixels + 2 * side, 9 * CL), F32),
        pltpu.VMEM((n, CH), BF),
        pltpu.VMEM((n, CS), BF),
        pltpu.VMEM((m, CG), BF),
        pltpu.VMEM((2, n, CS), BF),
        pltpu.VMEM((2, m, CG), BF),
        pltpu.VMEM((2, n, CH), BF),
        pltpu.VMEM((n, CH), BF),
        pltpu.VMEM((2, m, CS), BF),
        pltpu.VMEM((n, CS), BF),
        pltpu.VMEM((n, 9 * CL), BF),
        pltpu.VMEM((n, 9 * CL), BF),
        pltpu.VMEM((QUARTERS, QROWS, 128), BF),
        dma((count, 4)),
        dma((len(g_parts),)),
        dma((max(len(above), 1),)),
        dma((2, 3)),
        dma((3,)),
        dma((2,)),
    ]
    cfg = (low, high, len(g_parts), len(above), side, images)
    return pl.pallas_call(
        functools.partial(backward_kernel, cfg),
        out_shape=outs,
        in_specs=specs,
        out_specs=out_specs,
        scratch_shapes=scratch,
        input_output_aliases=aliases,
        name=f"backward_{low}_{high}",
        cost_estimate=pl.CostEstimate(flops=count * images * 900_000_000, bytes_accessed=count * 10_000_000, transcendentals=0),
        compiler_params=pltpu.CompilerParams(vmem_limit_bytes=VMEM_LIMIT),
    )(*ins)


def exchange_weights(own, rank, core):
    def over(bit, x):
        return lax.ppermute(x, "pipe", [(i, i ^ bit) for i in range(4)])

    def swap(x):
        return lax.ppermute(x, "dp", [(i, i ^ 1) for i in range(lax.axis_size("dp"))])

    def quarter(half):
        return lax.dynamic_index_in_dim(own, 2 * half + core, 0, keepdims=False)

    first, second = quarter(0), quarter(1)
    got = {}
    got["x1"] = over(1, first)
    got["y1"] = over(2, jnp.where(rank == 0, second, first))
    got["x2"] = over(1, jnp.where(rank == 2, got["y1"], second))
    got["y2"] = over(2, jnp.where(rank == 0, first, jnp.where(rank == 1, got["x1"], second)))
    got["x3"] = over(1, jnp.where(rank == 0, got["y2"], jnp.where(rank == 2, second, got["y1"])))
    got["y3"] = over(2, jnp.where(rank == 1, second, jnp.where(rank == 3, got["x1"], got["x2"])))
    return {name: (x, swap(x)) for name, x in got.items()}


def local_device(images_in, conv_local, conv_cross, reduce_weight, spectral_weight, expand_weight, norm_gain, norm_bias, cotangent, hole_mask):
    batches, _, side, _, channels = images_in.shape
    pixels = side * side
    dp_size = lax.axis_size("dp")
    chips = dp_size // 2
    rank = lax.axis_index("pipe")
    dp_rank = lax.axis_index("dp")
    z, core = dp_rank // 2, dp_rank % 2
    before = (dp_size - batches) // 2
    after = dp_size - batches - before
    holders = range(before, before + batches)
    table_to, table_from = dft_np(side)
    mf, mi = jnp.asarray(table_to, BF), jnp.asarray(table_from, BF)
    mft, mit = jnp.asarray(table_to.T, BF), jnp.asarray(table_from.T, BF)

    def swap(x):
        return lax.ppermute(x, "dp", [(i, i ^ 1) for i in range(dp_size)])

    def to_batches(x):
        x = jnp.pad(x, ((before, after), (0, 0), (0, 0))).reshape(chips, 2, pixels, channels)
        mine = lax.dynamic_index_in_dim(x, core, 1, keepdims=False)
        other = swap(lax.dynamic_index_in_dim(x, 1 - core, 1, keepdims=False))
        pairs = jnp.stack([mine, other], axis=1)
        parts = []
        for k in range(chips):
            part = lax.dynamic_index_in_dim(pairs, z ^ k, 0, keepdims=False)
            if k:
                part = lax.ppermute(part, "dp", [(i, i ^ (2 * k)) for i in range(dp_size) if i ^ (2 * k) in holders])
            parts.append(part.reshape(2 * pixels, channels))
        return parts

    def to_images(x):
        x = x.reshape(chips, 2, pixels, channels)
        parts = []
        for k in range(chips):
            part = x[k]
            if k:
                part = lax.ppermute(part, "dp", [(i, i ^ (2 * k)) for i in holders])
            parts.append(part)
        parts = jnp.stack(parts)
        parts = jnp.stack([lax.dynamic_index_in_dim(parts, z ^ k, 0, keepdims=False) for k in range(chips)])
        mine, other = parts[:, 0], swap(parts[:, 1])
        both = jnp.where(core == 0, jnp.stack([mine, other], axis=1), jnp.stack([other, mine], axis=1))
        return both.reshape(dp_size, pixels, channels)[before : before + batches]

    own = pack_section(
        conv_local[0], conv_cross[0], reduce_weight[0], spectral_weight[0], expand_weight[0], norm_gain[0], norm_bias[0]
    )
    arrived = exchange_weights(own, rank, core)
    inputs = to_batches(images_in.reshape(batches, pixels, channels))
    hole_float = hole_mask.astype(F32)
    hole_counts = jnp.sum(hole_float, axis=(2, 3), keepdims=True)
    weighting = 0.25 + hole_float * pixels / (hole_counts + pixels / 8.0)
    seed = (cotangent.astype(F32) * weighting[..., None]).astype(BF)
    seeds = to_batches(seed.reshape(batches, pixels, channels))
    place = jnp.stack([rank, core]).astype(jnp.int32)

    out0, *hats0, iv0, in_k, out_k, spec_k, join_k = forward_call(
        0, 1, place, inputs, [], own, arrived, mf, mi, (), side, dp_size
    )
    kept = (in_k, out_k, spec_k, join_k)
    *hats1, iv1, in_k, out_k, spec_k, join_k = forward_call(
        1, 4, place, [out0], inputs, own, arrived, mf, mi, kept, side, dp_size
    )
    activations = to_images(out_k)
    *grads0, grad1, ab1, in_k, own = backward_call(
        1, 4, place, seeds, [], own, arrived, mft, mit, hats1, iv1, (in_k, spec_k, join_k), side, dp_size
    )
    ab0, own_grad, own_terms = backward_call(
        0, 1, place, grads0, [grad1], own, arrived, mft, mit, hats0, iv0, (in_k, spec_k, join_k), side, dp_size
    )
    input_grads = to_images(own_grad).astype(F32)
    terms = lax.psum(own_terms, "dp").astype(F32)
    ab = lax.psum(lax.dynamic_index_in_dim(jnp.concatenate([ab0, ab1]), rank, 0, keepdims=False), "dp")
    shapes = (conv_local.shape, conv_cross.shape, reduce_weight.shape, spectral_weight.shape, expand_weight.shape)
    outs = (1, batches, 1, side, side, channels)
    return (
        activations.reshape(outs),
        input_grads.reshape(outs),
        *(t.reshape(n) for t, n in zip(unpack_section(terms), shapes)),
        ab[1:2],
        ab[0:1],
    )


def solution(mesh):
    placed = (
        P(None, "dp", None, None, None),
        P("pipe", None, None, None, None),
        P("pipe", None, None, None, None),
        P("pipe", None, None),
        P("pipe", None, None),
        P("pipe", None, None),
        P("pipe", None),
        P("pipe", None),
        P(None, "dp", None, None, None),
        P(None, "dp", None, None),
    )

    def on_device(images_in, *rest):
        dp_size = lax.axis_size("dp")
        fits = images_in.shape[1] == 1 and dp_size == 8 and images_in.shape[0] <= dp_size and lax.axis_size("pipe") == 4
        return (local_device if fits else general_device)(images_in, *rest)

    return jax.shard_map(
        on_device,
        mesh=mesh,
        in_specs=placed,
        out_specs=(
            P("pipe", None, "dp", None, None, None),
            P("pipe", None, "dp", None, None, None),
            P("pipe", None, None, None, None),
            P("pipe", None, None, None, None),
            P("pipe", None, None),
            P("pipe", None, None),
            P("pipe", None, None),
            P("pipe", None),
            P("pipe", None),
        ),
        check_vma=False,
    )
```

```python
import functools
import math

import jax
import jax.numpy as jnp
import numpy as np
from jax import lax
from jax.experimental import pallas as pl
from jax.experimental.pallas import tpu as pltpu
from jax.sharding import PartitionSpec as P

CL = 128
CG = 384
CS = 192
CH = 512
NORMS = 1088
F32 = jnp.float32
BF = jnp.bfloat16
IM = 4
UN = 2


EPS = 1e-05
HIGH = lax.Precision.HIGHEST


def from_behind(x, axis, by):
    length = lax.axis_size(axis)
    pairs = [(i, i + by) for i in range(length) if 0 <= i + by < length]
    return lax.ppermute(x, axis, pairs)


def smooth(values):
    return values * jax.nn.sigmoid(values)


def smooth_slope(values):
    logistic = jax.nn.sigmoid(values)
    return logistic * (1.0 + values * (1.0 - logistic))


def patches(values):
    height, breadth = (values.shape[1], values.shape[2])
    padded = jnp.pad(values, ((0, 0), (1, 1), (1, 1), (0, 0)))
    return jnp.concatenate(
        [
            padded[:, row_off : row_off + height, col_off : col_off + breadth]
            for row_off in range(3)
            for col_off in range(3)
        ],
        axis=-1,
    )


def conv_apply(values, kernel):
    flat_kernel = kernel.reshape(-1, kernel.shape[-1])
    return jnp.einsum(
        "bhwk,kd->bhwd", patches(values), flat_kernel, preferred_element_type=jnp.float32
    )


def conv_weight_grad(values, grad_low, kernel_shape):
    return jnp.einsum(
        "bhwk,bhwd->kd", patches(values), grad_low, preferred_element_type=jnp.float32
    ).reshape(kernel_shape)


def conv_input_grad(grad_low, kernel):
    flipped = jnp.flip(kernel, (0, 1)).transpose(0, 1, 3, 2)
    return conv_apply(grad_low, flipped)


def dft_tables(side_len):
    frequencies = side_len // 2 + 1
    spatial = jnp.arange(side_len, dtype=jnp.int32)
    spectral = jnp.arange(frequencies, dtype=jnp.int32)
    angle_cols = (spatial[:, None] * spectral[None, :] % side_len).astype(jnp.float32) * (
        2.0 * math.pi / side_len
    )
    angle_rows = (spatial[:, None] * spatial[None, :] % side_len).astype(jnp.float32) * (
        2.0 * math.pi / side_len
    )
    fold_factor = jnp.where((spectral == 0) | (2 * spectral == side_len), 1.0, 2.0).astype(
        jnp.float32
    )
    return (
        jnp.cos(angle_cols),
        jnp.sin(angle_cols),
        jnp.cos(angle_rows),
        jnp.sin(angle_rows),
        fold_factor,
    )


def to_spectrum(field_in, tables):
    cosine_cols, sine_cols, cosine_rows, sine_rows, _ = tables
    scaling = 1.0 / math.sqrt(field_in.shape[1] * field_in.shape[2])
    real_along = jnp.einsum("bhwc,wk->bhkc", field_in, cosine_cols, precision=HIGH)
    imaginary_along = -jnp.einsum("bhwc,wk->bhkc", field_in, sine_cols, precision=HIGH)
    real_part = jnp.einsum("bhkc,gh->bgkc", real_along, cosine_rows, precision=HIGH) + jnp.einsum(
        "bhkc,gh->bgkc", imaginary_along, sine_rows, precision=HIGH
    )
    imaginary_part = jnp.einsum(
        "bhkc,gh->bgkc", imaginary_along, cosine_rows, precision=HIGH
    ) - jnp.einsum("bhkc,gh->bgkc", real_along, sine_rows, precision=HIGH)
    return jnp.concatenate([real_part, imaginary_part], axis=-1) * scaling


def from_spectrum(field_in, tables):
    cosine_cols, sine_cols, cosine_rows, sine_rows, fold_factor = tables
    scaling = 1.0 / math.sqrt(field_in.shape[1] * cosine_cols.shape[0])
    half_width = field_in.shape[-1] // 2
    real_in = field_in[..., :half_width]
    imaginary_in = field_in[..., half_width:]
    real_rows = jnp.einsum("bgkc,gh->bhkc", real_in, cosine_rows, precision=HIGH) - jnp.einsum(
        "bgkc,gh->bhkc", imaginary_in, sine_rows, precision=HIGH
    )
    imaginary_rows = jnp.einsum(
        "bgkc,gh->bhkc", imaginary_in, cosine_rows, precision=HIGH
    ) + jnp.einsum("bgkc,gh->bhkc", real_in, sine_rows, precision=HIGH)
    folding = fold_factor[None, None, :, None]
    field_out = jnp.einsum(
        "bhkc,wk->bhwc", real_rows * folding, cosine_cols, precision=HIGH
    ) - jnp.einsum("bhkc,wk->bhwc", imaginary_rows * folding, sine_cols, precision=HIGH)
    return field_out * scaling


def moments(values):
    sum_axes = tuple(range(values.ndim - 1))
    count_all = math.prod(values.shape[:-1]) * lax.axis_size("dp")
    average = lax.psum(jnp.sum(values, axis=sum_axes), "dp") / count_all
    centred = values - average
    spread = lax.psum(jnp.sum(centred * centred, axis=sum_axes), "dp") / count_all
    return (average, lax.rsqrt(spread + EPS))


def norm_back(grad_out, act_values, hat_values, gain_slice, inv_std):
    sum_axes = tuple(range(act_values.ndim - 1))
    count_all = math.prod(act_values.shape[:-1]) * lax.axis_size("dp")
    grad_act = grad_out * smooth_slope(act_values)
    sum_act, sum_hat = lax.psum(
        (jnp.sum(grad_act, axis=sum_axes), jnp.sum(grad_act * hat_values, axis=sum_axes)), "dp"
    )
    grad_values = gain_slice * inv_std * (grad_act - (sum_act + hat_values * sum_hat) / count_all)
    return (grad_values, sum_hat, sum_act)


def section_compute(inputs, weights, norm_gains, norm_biases, measure, tables):
    local_kernel, cross_kernel, reduce_matrix, spectral_matrix, expand_matrix = weights

    def normalize(values, offset):
        extent = values.shape[-1]
        average, inv_std = measure(values, offset)
        hat_values = (values - average) * inv_std
        return (
            hat_values,
            norm_gains[offset : offset + extent] * hat_values
            + norm_biases[offset : offset + extent],
        )

    local_part = inputs[..., :CL]
    global_part = inputs[..., CL:]
    pre_local = conv_apply(inputs, local_kernel)
    reduced = jnp.einsum(
        "bhwc,cd->bhwd", global_part, reduce_matrix, preferred_element_type=jnp.float32
    )
    hat_one, act_one = normalize(reduced, 0)
    activated = smooth(act_one)
    spec_low = to_spectrum(activated, tables).astype(jnp.bfloat16)
    spectral_mix = jnp.einsum(
        "bhkc,cd->bhkd", spec_low, spectral_matrix, preferred_element_type=jnp.float32
    )
    hat_two, act_two = normalize(spectral_mix, CS)
    joined = (activated + from_spectrum(smooth(act_two), tables)).astype(jnp.bfloat16)
    pre_global = conv_apply(local_part, cross_kernel) + jnp.einsum(
        "bhwc,cd->bhwd", joined, expand_matrix, preferred_element_type=jnp.float32
    )
    hat_end, act_end = normalize(jnp.concatenate([pre_local, pre_global], axis=-1), CS + CG)
    return (
        smooth(act_end),
        (hat_one, act_one, activated, spec_low, hat_two, act_two, joined, hat_end, act_end),
    )


def section_backward(inputs, weights, norm_gains, inv_std, saved, grad_result, tables):
    local_kernel, cross_kernel, reduce_matrix, spectral_matrix, expand_matrix = weights
    hat_one, act_one, activated, spec_low, hat_two, act_two, joined, hat_end, act_end = saved
    local_part = inputs[..., :CL]
    global_part = inputs[..., CL:]
    grad_end, gain_end, bias_end = norm_back(
        grad_result, act_end, hat_end, norm_gains[CS + CG :], inv_std[CS + CG :]
    )
    grad_end_low = grad_end.astype(jnp.bfloat16)
    grad_pre_local = grad_end_low[..., :CL]
    grad_pre_global = grad_end_low[..., CL:]
    grad_cross = conv_weight_grad(local_part, grad_pre_global, cross_kernel.shape)
    grad_expand = jnp.einsum(
        "bhwc,bhwd->cd", joined, grad_pre_global, preferred_element_type=jnp.float32
    )
    grad_joined = jnp.einsum(
        "bhwd,cd->bhwc", grad_pre_global, expand_matrix, preferred_element_type=jnp.float32
    )
    _, inverse_pull = jax.vjp(
        lambda field_in: from_spectrum(field_in, tables), jnp.zeros(act_two.shape, jnp.float32)
    )
    (grad_after,) = inverse_pull(grad_joined)
    grad_mix, gain_two, bias_two = norm_back(
        grad_after, act_two, hat_two, norm_gains[CS : CS + CG], inv_std[CS : CS + CG]
    )
    grad_mix_low = grad_mix.astype(jnp.bfloat16)
    grad_spectral = jnp.einsum(
        "bhkc,bhkd->cd", spec_low, grad_mix_low, preferred_element_type=jnp.float32
    )
    grad_spec = jnp.einsum(
        "bhkd,cd->bhkc", grad_mix_low, spectral_matrix, preferred_element_type=jnp.float32
    )
    _, forward_pull = jax.vjp(lambda field_in: to_spectrum(field_in, tables), activated)
    (grad_activated,) = forward_pull(grad_spec)
    grad_reduced, gain_one, bias_one = norm_back(
        grad_activated + grad_joined, act_one, hat_one, norm_gains[:CS], inv_std[:CS]
    )
    grad_reduced_low = grad_reduced.astype(jnp.bfloat16)
    grad_reduce = jnp.einsum(
        "bhwc,bhwd->cd", global_part, grad_reduced_low, preferred_element_type=jnp.float32
    )
    grad_global = jnp.einsum(
        "bhwd,cd->bhwc", grad_reduced_low, reduce_matrix, preferred_element_type=jnp.float32
    )
    grad_local = conv_input_grad(grad_pre_global, cross_kernel)
    grad_local_kernel = conv_weight_grad(inputs, grad_pre_local, local_kernel.shape)
    grad_inputs = conv_input_grad(grad_pre_local, local_kernel) + jnp.concatenate(
        [grad_local, grad_global], axis=-1
    )
    gain_terms = jnp.concatenate([gain_one, gain_two, gain_end])
    bias_terms = jnp.concatenate([bias_one, bias_two, bias_end])
    return (
        grad_inputs,
        (grad_local_kernel, grad_cross, grad_reduce, grad_spectral, grad_expand),
        gain_terms,
        bias_terms,
    )


def store(buffer, value, slot_index, active):
    previous = lax.dynamic_index_in_dim(buffer, slot_index, 0, keepdims=False)
    return lax.dynamic_update_index_in_dim(
        buffer, jnp.where(active, value, previous), slot_index, 0
    )


def general_device(
    images_in,
    conv_local,
    conv_cross,
    reduce_weight,
    spectral_weight,
    expand_weight,
    norm_gain,
    norm_bias,
    cotangent,
    hole_mask,
):
    section_count = lax.axis_size("pipe")
    section_rank = lax.axis_index("pipe")
    batches = images_in.shape[0]
    step_count = batches + section_count - 1
    odd_section = section_rank % 2 == 1
    last_section = section_rank == section_count - 1
    weights = (conv_local[0], conv_cross[0], reduce_weight[0], spectral_weight[0], expand_weight[0])
    norm_gains = norm_gain[0]
    norm_biases = norm_bias[0]
    tables = dft_tables(images_in.shape[2])
    blank = jnp.zeros(images_in.shape[1:], jnp.bfloat16)

    def forward_step(carried, step_index):
        recv_act, recv_res, kept_inputs, kept_stats, kept_outputs = carried
        batch_index = step_index - section_rank
        active = (batch_index >= 0) & (batch_index < batches)
        slot_index = jnp.clip(batch_index, 0, batches - 1)
        fresh_image = lax.dynamic_index_in_dim(images_in, slot_index, 0, keepdims=False)
        inputs = jnp.where(section_rank == 0, fresh_image, recv_act)
        recorded = []

        def measure(values, offset):
            average, inv_std = moments(values)
            recorded.append((average, inv_std))
            return (average, inv_std)

        result, _ = section_compute(inputs, weights, norm_gains, norm_biases, measure, tables)
        summed = result + jnp.where(odd_section, recv_res.astype(jnp.float32), 0.0)
        outgoing = summed.astype(jnp.bfloat16)
        residual_out = jnp.where(odd_section, outgoing, inputs)
        next_act, next_res = from_behind((outgoing, residual_out), "pipe", 1)
        statistics = jnp.stack(
            [
                jnp.concatenate([entry_pair[0] for entry_pair in recorded]),
                jnp.concatenate([entry_pair[1] for entry_pair in recorded]),
            ]
        )
        kept_inputs = store(kept_inputs, inputs, slot_index, active)
        kept_stats = store(kept_stats, statistics, slot_index, active)
        kept_outputs = store(kept_outputs, outgoing, slot_index, active)
        return ((next_act, next_res, kept_inputs, kept_stats, kept_outputs), None)

    forward_init = (
        blank,
        blank,
        jnp.zeros(images_in.shape, jnp.bfloat16),
        jnp.zeros((batches, 2, NORMS), jnp.float32),
        jnp.zeros(images_in.shape, jnp.bfloat16),
    )
    forward_state = lax.scan(forward_step, forward_init, jnp.arange(step_count))[0]
    kept_inputs, kept_stats, kept_outputs = (forward_state[2], forward_state[3], forward_state[4])
    pixels = images_in.shape[2] * images_in.shape[3]
    hole_float = hole_mask.astype(jnp.float32)
    hole_counts = jnp.sum(hole_float, axis=(2, 3), keepdims=True)
    weighting = 0.25 + hole_float * pixels / (hole_counts + pixels / 8.0)

    def backward_step(carried, step_index):
        recv_grad, recv_res, grad_store, weight_sums, gain_sum, bias_sum = carried
        batch_index = step_index - (section_count - 1 - section_rank)
        active = (batch_index >= 0) & (batch_index < batches)
        slot_index = jnp.clip(batch_index, 0, batches - 1)
        cotan_slot = lax.dynamic_index_in_dim(cotangent, slot_index, 0, keepdims=False).astype(
            jnp.float32
        )
        weight_slot = lax.dynamic_index_in_dim(weighting, slot_index, 0, keepdims=False)
        seed_grad = (cotan_slot * weight_slot[..., None]).astype(jnp.bfloat16)
        incoming = jnp.where(last_section, seed_grad, recv_grad)
        inputs = lax.dynamic_index_in_dim(kept_inputs, slot_index, 0, keepdims=False)
        statistics = lax.dynamic_index_in_dim(kept_stats, slot_index, 0, keepdims=False)

        def measure(values, offset):
            extent = values.shape[-1]
            return (
                statistics[0, offset : offset + extent],
                statistics[1, offset : offset + extent],
            )

        _, saved = section_compute(inputs, weights, norm_gains, norm_biases, measure, tables)
        grad_inputs, weight_terms, gain_terms, bias_terms = section_backward(
            inputs, weights, norm_gains, statistics[1], saved, incoming.astype(jnp.float32), tables
        )
        grad_total = grad_inputs + jnp.where(odd_section, 0.0, recv_res.astype(jnp.float32))
        outgoing = grad_total.astype(jnp.bfloat16)
        residual_out = jnp.where(odd_section, incoming, outgoing)
        next_grad, next_res = from_behind((outgoing, residual_out), "pipe", -1)
        weight_sums = tuple(
            (
                running + jnp.where(active, addend, 0.0)
                for running, addend in zip(weight_sums, weight_terms)
            )
        )
        gain_sum = gain_sum + jnp.where(active, gain_terms, 0.0)
        bias_sum = bias_sum + jnp.where(active, bias_terms, 0.0)
        grad_store = store(grad_store, grad_total, slot_index, active)
        return ((next_grad, next_res, grad_store, weight_sums, gain_sum, bias_sum), None)

    zero_weights = tuple((jnp.zeros(entry_weight.shape, jnp.float32) for entry_weight in weights))
    backward_init = (
        blank,
        blank,
        jnp.zeros(images_in.shape, jnp.float32),
        zero_weights,
        jnp.zeros((NORMS,), jnp.float32),
        jnp.zeros((NORMS,), jnp.float32),
    )
    state_end = lax.scan(backward_step, backward_init, jnp.arange(0, 0 + step_count))[0]
    sum_local, sum_cross, sum_reduce, sum_spectral, sum_expand = state_end[3]
    totals = lax.psum((sum_local, sum_cross, sum_reduce, sum_spectral, sum_expand), "dp")
    return (
        kept_outputs[None],
        state_end[2][None],
        totals[0][None],
        totals[1][None],
        totals[2][None],
        totals[3][None],
        totals[4][None],
        state_end[4][None],
        state_end[5][None],
    )


PARTS = 4
ANY = pl.BlockSpec(memory_space=pl.ANY)
VMEM = pl.BlockSpec(memory_space=pltpu.VMEM)
SMEM = pl.BlockSpec(memory_space=pltpu.SMEM)
VMEM_LIMIT = 63 * 2**20


def dft_np(side):
    spatial = np.arange(side)
    spectral = np.arange(side // 2 + 1)
    turns = spatial[:, None, None, None] * spatial[None, None, :, None] + spectral[None, :, None, None] * spatial[None, None, None, :]
    angle = (turns % side).reshape(side * spectral.size, side * side) * (2.0 * np.pi / side)
    fold = np.broadcast_to(np.where((spectral == 0) | (2 * spectral == side), 1.0, 2.0), (side, spectral.size)).reshape(-1, 1)
    forward = np.concatenate([np.cos(angle), -np.sin(angle)]) / side
    inverse = np.concatenate([np.cos(angle) * fold, -np.sin(angle) * fold]).T / side
    return forward, inverse


def dot(a, b):
    return lax.dot_general(a, b, (((1,), (0,)), ((), ())), preferred_element_type=F32)


def dot_nt(a, b):
    return lax.dot_general(a, b, (((1,), (1,)), ((), ())), preferred_element_type=F32)


def dot_tn(a, b):
    return lax.dot_general(a, b, (((0,), (0,)), ((), ())), preferred_element_type=F32)


def silu_of_half(h):
    return h + h * jnp.tanh(h)


def twice_slope(h):
    t = jnp.tanh(h)
    return (1.0 + t) * (1.0 + h * (1.0 - t))


QUARTERS, QROWS = 4, 2640
LAYOUT = {
    "local": (0, 1152, 1),
    "cross": (1152, 288, 3),
    "reduce": (2016, 48, 3),
    "spectral": (2160, 96, 3),
    "expand": (2448, 48, 3),
    "norms": (2592, 16, 3),
}


def pieces(name, start, count, block=0):
    base, rows, _ = LAYOUT[name]
    found = []
    while count:
        quarter, offset = divmod(start, rows)
        take = min(count, rows - offset)
        found.append((quarter, base + block * rows + offset, take))
        start, count = start + take, count - take
    return found


def stack_rows(parts):
    return parts[0] if len(parts) == 1 else jnp.concatenate(parts, axis=0)


def stack_cols(parts):
    return parts[0] if len(parts) == 1 else jnp.concatenate(parts, axis=1)


def read(w, name, start, count):
    blocks = LAYOUT[name][2]
    return stack_cols([stack_rows([w[q, r : r + n] for q, r, n in pieces(name, start, count, j)]) for j in range(blocks)])


def write(w, name, start, value):
    for j in range(LAYOUT[name][2]):
        done = 0
        for q, r, n in pieces(name, start, value.shape[0], j):
            w[q, r : r + n] = value[done : done + n, j * 128 : (j + 1) * 128].astype(w.dtype)
            done += n


def norm_rows(w):
    base = LAYOUT["norms"][0]
    return stack_cols([w[j // 3, base + 16 * (j % 3) : base + 16 * (j % 3) + 16] for j in range(9)]).astype(F32)[:, :NORMS]


def read_norms(w):
    rows = norm_rows(w)
    return rows[0:1] + rows[1:2], rows[2:3] + rows[3:4]


def norm_block(vectors):
    rows = stack_rows([*vectors, jnp.zeros((16 - len(vectors), NORMS), F32)])
    return stack_cols([rows, jnp.zeros((16, 12 * 128 - NORMS), F32)]).astype(BF)


def write_norms(w, vectors):
    base = LAYOUT["norms"][0]
    rows = norm_block(vectors)
    for j in range(12):
        w[j // 3, base + 16 * (j % 3) : base + 16 * (j % 3) + 16] = rows[:, j * 128 : (j + 1) * 128]


TERMS = {
    "local": (0, 9 * CH, 1),
    "cross": (9 * CH, 9 * CL, 3),
    "reduce": (9 * (CH + CG), CS, 3),
    "spectral": (9 * (CH + CG) + 3 * CS, CG, 3),
    "expand": (9 * (CH + CG) + 3 * (CS + CG), CS, 3),
    "norms": (9 * (CH + CG) + 3 * (2 * CS + CG), 16, 12),
}


def put_terms(w, name, start, value):
    base, rows, blocks = TERMS[name]
    count = value.shape[0]
    for j in range(blocks):
        first = base + j * rows + start
        w[pl.ds(first if isinstance(first, int) else pl.multiple_of(first, 128), count)] = value[:, j * 128 : (j + 1) * 128].astype(BF)


def put_norm_terms(w, vectors):
    base = TERMS["norms"][0]
    rows = norm_block(vectors)
    for j in range(12):
        w[base + 16 * j : base + 16 * (j + 1)] = rows[:, j * 128 : (j + 1) * 128]


def get_terms(w, name, columns):
    base, rows, blocks = TERMS[name]
    return stack_cols([w[base + j * rows : base + (j + 1) * rows] for j in range(blocks)]).astype(F32)[:, :columns]


def conv_matrix(w):
    return stack_rows([stack_cols([read(w, "local", k * CH, CL), read(w, "cross", k * CL, CL)]) for k in range(9)])


def global_matrix(w):
    return stack_cols([read(w, "local", k * CH + CL, CG) for k in range(9)])


def global_by_row(w):
    return stack_rows([stack_cols([read(w, "local", (dh * 3 + dw) * CH + CL, CG) for dw in range(3)]) for dh in range(3)])


def conv_by_column(w):
    return stack_rows(
        [
            stack_cols([part for k in (dw, 3 + dw, 6 + dw) for part in (read(w, "local", k * CH, CL), read(w, "cross", k * CL, CL))])
            for dw in range(3)
        ]
    )


def pack_kernel(place, local, cross, reduce_w, spectral, expand, gains, biases, own, send, packed, sem):
    packed_rows = lambda name, value: write(packed, name, 0, value)
    packed_rows("local", local[...])
    packed_rows("cross", cross[...])
    packed_rows("reduce", reduce_w[...])
    packed_rows("spectral", spectral[...])
    packed_rows("expand", expand[...])
    halves = []
    for values in (gains[...], biases[...]):
        high = values.astype(BF)
        halves += [high.astype(F32), values - high.astype(F32)]
    write_norms(packed, halves)
    core = place[1]
    copies = [pltpu.make_async_copy(packed.at[2 * half + core], send.at[half], sem.at[half]) for half in range(2)]
    copies += [pltpu.make_async_copy(packed.at[q], own.at[pl.ds(q * QROWS, QROWS)], sem.at[2 + q]) for q in range(QUARTERS)]
    for c in copies:
        c.start()
    for c in copies:
        c.wait()


def pack_call(place, *weights):
    shape = jax.ShapeDtypeStruct
    return pl.pallas_call(
        pack_kernel,
        out_shape=[shape((QUARTERS * QROWS, 128), BF), shape((2, QROWS, 128), BF)],
        in_specs=[SMEM] + [VMEM] * 7,
        out_specs=[ANY] * 2,
        scratch_shapes=[pltpu.VMEM((QUARTERS, QROWS, 128), BF), pltpu.SemaphoreType.DMA((2 + QUARTERS,))],
        name="pack_weights",
        compiler_params=pltpu.CompilerParams(vmem_limit_bytes=VMEM_LIMIT),
    )(place, *weights)


def relay_kernel(skip, *refs):
    y1, x1 = refs[:2]
    over_x, over_y, stage, sem_in, sem_out = refs[2 + skip :]
    loads = [pltpu.make_async_copy(y1.at[0], stage.at[0], sem_in.at[0]), pltpu.make_async_copy(x1.at[1], stage.at[1], sem_in.at[1])]
    stores = [pltpu.make_async_copy(stage.at[i], ref.at[0], sem_out.at[i]) for i, ref in enumerate((over_x, over_y))]
    for c in loads:
        c.start()
    for load, store in zip(loads, stores):
        load.wait()
        store.start()
    for c in stores:
        c.wait()


def relay_call(y1, x1, after):
    dma = pltpu.SemaphoreType.DMA
    return pl.pallas_call(
        functools.partial(relay_kernel, len(after)),
        out_shape=[jax.ShapeDtypeStruct((1, QROWS, 128), BF)] * 2,
        in_specs=[ANY] * (2 + len(after)),
        out_specs=[ANY] * 2,
        scratch_shapes=[pltpu.VMEM((2, QROWS, 128), BF), dma((2,)), dma((2,))],
        name="relay_weights",
    )(y1, x1, *after)


def unpack_kernel(packed, local, cross, reduce_w, spectral, expand, gains, biases):
    local[...] = get_terms(packed, "local", CL)
    cross[...] = get_terms(packed, "cross", CG)
    reduce_w[...] = get_terms(packed, "reduce", CG)
    spectral[...] = get_terms(packed, "spectral", CG)
    expand[...] = get_terms(packed, "expand", CG)
    rows = get_terms(packed, "norms", NORMS)
    biases[...] = rows[0:1]
    gains[...] = rows[1:2]


def unpack_call(packed):
    shape = jax.ShapeDtypeStruct
    dims = ((9 * CH, CL), (9 * CL, CG), (CS, CG), (CG, CG), (CS, CG), (1, NORMS), (1, NORMS))
    return pl.pallas_call(
        unpack_kernel,
        out_shape=[shape(d, F32) for d in dims],
        in_specs=[VMEM],
        out_specs=[VMEM] * 7,
        name="unpack_terms",
        compiler_params=pltpu.CompilerParams(vmem_limit_bytes=VMEM_LIMIT),
    )(packed)


def spread_kernel(batches, place, images, other, *refs):
    parts, sem = refs[:PARTS], refs[-1]
    core, z = place[1], place[2]
    copies = []
    for k, part in enumerate(parts):
        i = jnp.clip((z ^ k) - (1 - core), 0, batches // 2 - 1)
        copies.append(pltpu.make_async_copy(images.at[2 * i + 1 - core], part.at[0], sem.at[k, 0]))
        copies.append(pltpu.make_async_copy(other.at[i], part.at[1], sem.at[k, 1]))
    for c in copies:
        c.start()
    for c in copies:
        c.wait()


def spread_call(place, images, other, through=(), after=()):
    batches, pixels, channels = images.shape
    skip = len(through) + len(after)

    def kernel(place, images, other, *refs):
        spread_kernel(batches, place, images, other, *refs[skip:])

    return pl.pallas_call(
        kernel,
        out_shape=[jax.ShapeDtypeStruct((2, pixels, channels), BF)] * PARTS + [jax.ShapeDtypeStruct(x.shape, x.dtype) for x in through],
        in_specs=[SMEM, VMEM, VMEM] + [ANY] * skip,
        out_specs=[ANY] * (PARTS + len(through)),
        scratch_shapes=[pltpu.SemaphoreType.DMA((PARTS, 2))],
        input_output_aliases={3 + i: PARTS + i for i in range(len(through))},
        name="spread_images",
        compiler_params=pltpu.CompilerParams(vmem_limit_bytes=VMEM_LIMIT),
    )(place, images, other, *through, *after)


def second_images(p0, p1, p2, p3, out, stage, sem_in, sem_out):
    pixels = out.shape[1]
    loads = [pltpu.make_async_copy(p.at[pl.ds(pixels, pixels)], stage.at[k], sem_in.at[k]) for k, p in enumerate((p0, p1, p2, p3))]
    for c in loads:
        c.start()
    stores = [pltpu.make_async_copy(stage.at[k], out.at[k], sem_out.at[k]) for k in range(PARTS)]
    for load, store in zip(loads, stores):
        load.wait()
        store.start()
    for c in stores:
        c.wait()


def second_images_call(parts):
    rows, channels = parts[0].shape
    dma = pltpu.SemaphoreType.DMA
    return pl.pallas_call(
        second_images,
        out_shape=jax.ShapeDtypeStruct((PARTS, rows // 2, channels), BF),
        in_specs=[ANY] * PARTS,
        out_specs=ANY,
        scratch_shapes=[pltpu.VMEM((PARTS, rows // 2, channels), BF), dma((PARTS,)), dma((PARTS,))],
        name="second_images",
    )(*parts)


def collect_kernel(batches, place, p0, p1, p2, p3, other, out, stage, sem):
    core, z = place[1], place[2]
    parts = (p0, p1, p2, p3)
    pixels = p0.shape[0] // 2
    copies = []
    for k, part in enumerate(parts):
        copies.append(pltpu.make_async_copy(part.at[pl.ds(0, pixels)], stage.at[k, 0], sem.at[k, 0]))
        copies.append(pltpu.make_async_copy(other.at[k], stage.at[k, 1], sem.at[k, 1]))
    for c in copies:
        c.start()
    for k in range(PARTS):
        for j in range(2):
            copies[2 * k + j].wait()
            batch = 2 * (z ^ k) + (1 - core if j else core) - 1

            @pl.when(jnp.logical_and(batch >= 0, batch < batches))
            def _():
                out[batch] = stage[k, j].astype(out.dtype)


def collect_call(place, batches, parts, other, dtype):
    rows, channels = parts[0].shape
    return pl.pallas_call(
        functools.partial(collect_kernel, batches),
        out_shape=jax.ShapeDtypeStruct((batches, rows // 2, channels), dtype),
        in_specs=[SMEM] + [ANY] * (PARTS + 1),
        out_specs=VMEM,
        scratch_shapes=[pltpu.VMEM((PARTS, 2, rows // 2, channels), BF), pltpu.SemaphoreType.DMA((PARTS, 2))],
        name="collect_images",
        compiler_params=pltpu.CompilerParams(vmem_limit_bytes=VMEM_LIMIT),
    )(place, *parts, other)


SOURCES = (
    (("own", "own"), ("x1", "x1"), ("y1", "y1"), ("x2", "y2")),
    (("x1", "x1"), ("own", "own"), ("x2", "y2"), ("y1", "y1")),
    (("y1", "y1"), ("x2", "y2"), ("own", "own"), ("x1", "x1")),
    (("x2", "y2"), ("y1", "y1"), ("x1", "x1"), ("own", "own")),
)


def load_weights(place, arrived, low, high, w, sems):
    rank, core = place[0], place[1]
    for s in range(low, high):
        for r, sources in enumerate(SOURCES):

            @pl.when(rank == r)
            def _():
                for half, name in enumerate(sources[s]):
                    for other in range(2):
                        quarter = 2 * half + (1 - core if other else core)
                        if name == "own":
                            src = arrived["own"].at[pl.ds(pl.multiple_of(quarter * QROWS, 16), QROWS)]
                        else:
                            src = arrived[name][other].at[half if name in ("x1", "y1") else 0]
                        pltpu.make_async_copy(src, w.at[s - low, quarter], sems.at[s - low, 2 * half + other]).start()


def wait_weights(own, index, w, sems):
    for n in range(4):
        pltpu.make_async_copy(own.at[pl.ds(0, QROWS)], w.at[index, 0], sems.at[index, n]).wait()


def moments_of(v):
    mean = jnp.mean(v, axis=0, keepdims=True)
    centred = v - mean
    return mean, jnp.sum(centred * centred, axis=0, keepdims=True)


def combined(mean_ref, square_ref, rows):
    images = mean_ref.shape[0]
    means = [mean_ref[b] for b in range(images)]
    mean = sum(means) / images
    total = sum(square_ref[b] + rows * (means[b] - mean) ** 2 for b in range(images))
    return mean, lax.rsqrt(total / (images * rows) + EPS)


def halves(gain, bias, mean, inv):
    scale = 0.5 * gain * inv
    return scale, 0.5 * bias - mean * scale


def beside(v, column, by, side):
    if by < 0:
        return jnp.where(column == 0, 0.0, pltpu.roll(v, 1, 0))
    return jnp.where(column == side - 1, 0.0, pltpu.roll(v, v.shape[0] - 1, 0))


def three_columns(dst, b, x, column, side):
    pixels = x.shape[0]
    wide = x.astype(F32)
    for i, v in enumerate((beside(wide, column, -1, side).astype(BF), x, beside(wide, column, 1, side).astype(BF))):
        dst[i, b, 0:side] = jnp.zeros((side, CL), BF)
        dst[i, b, side : side + pixels] = v
        dst[i, b, side + pixels : 2 * side + pixels] = jnp.zeros((side, CL), BF)


def three_rows(x, side, images):
    pixels = x.shape[0] // images
    none = jnp.zeros((side, x.shape[1]), x.dtype)
    back, on = [], []
    for i in range(images):
        back += [none, x[i * pixels : (i + 1) * pixels - side]]
        on += [x[i * pixels + side : (i + 1) * pixels], none]
    return stack_rows(back), x, stack_rows(on)


def nine(src, b, side, flipped):
    pixels = side * side
    parts = []
    for dh in range(3):
        for dw in range(3):
            i, j = (2 - dh, 2 - dw) if flipped else (dh, dw)
            parts.append(src[j, b, i * side : i * side + pixels])
    return parts


def part_copies(whole, parts, sems):
    rows = whole.shape[0] // len(parts)
    return [pltpu.make_async_copy(whole.at[pl.ds(k * rows, rows)], ref, sems.at[k]) for k, ref in enumerate(parts)]


def needed(low, high):
    return sorted({name for sources in SOURCES for s in range(low, high) for name in sources[s]} - {"own"})


class Space:
    def __init__(self, **named):
        self.__dict__.update(named)


def geometry(side, images):
    pixels, modes = side * side, side * (side // 2 + 1)
    column = lambda: lax.broadcasted_iota(jnp.int32, (pixels, 1), 0) % side
    wide = lambda: lax.broadcasted_iota(jnp.int32, (IM * pixels, 1), 0) % side
    return Space(
        side=side,
        images=images,
        pixels=pixels,
        modes=modes,
        steps=images // IM,
        column=column,
        wide=wide,
        rows_of=lambda b: pl.ds(pl.multiple_of(b * (IM * pixels), IM * pixels), IM * pixels),
        modes_of=lambda b: pl.ds(pl.multiple_of(b * (IM * modes), IM * modes), IM * modes),
        image_rows=lambda b, i: pl.ds(pl.multiple_of(b * (IM * pixels) + i * pixels, pixels), pixels),
    )


def forward_section(geo, v, ws, a, o, odd):
    column, wide = geo.column(), geo.wide()
    side, pixels, modes = geo.side, geo.pixels, geo.modes
    gain, bias = read_norms(ws)

    def reduce_step(b, _):
        r = geo.rows_of(b)
        for i in range(IM):
            three_columns(v.xp, b * IM + i, a[geo.image_rows(b, i), 0:CL], column, side)
        x = dot_nt(a[r, CL:CH], read(ws, "reduce", 0, CS))
        v.q[r] = x
        v.mu1[b], v.sq1[b] = moments_of(x)
        return 0

    lax.fori_loop(0, geo.steps, reduce_step, 0, unroll=UN)
    mean1, inv1 = combined(v.mu1, v.sq1, IM * pixels)
    scale1, shift1 = halves(gain[:, :CS], bias[:, :CS], mean1, inv1)

    def spectral_step(b, _):
        r, rs = geo.rows_of(b), geo.modes_of(b)
        h = v.q[r] * scale1 + shift1
        v.h1[r] = h.astype(BF)
        act = silu_of_half(h)
        v.t[r] = act
        act = act.astype(BF)
        spec = [dot(v.mf[...], act[i * pixels : (i + 1) * pixels]).astype(BF) for i in range(IM)]
        real = stack_rows([x[:modes] for x in spec])
        imaginary = stack_rows([x[modes:] for x in spec])
        v.sv[0, rs] = real
        v.sv[1, rs] = imaginary
        mix = dot(real, read(ws, "spectral", 0, CS)) + dot(imaginary, read(ws, "spectral", CS, CS))
        v.f[rs] = mix
        v.mu2[b], v.sq2[b] = moments_of(mix)
        taps = stack_rows([stack_cols(nine(v.xp, b * IM + i, side, False)) for i in range(IM)])
        v.p[r] = dot(taps, conv_matrix(ws))
        return 0

    lax.fori_loop(0, geo.steps, spectral_step, 0, unroll=UN)
    mean2, inv2 = combined(v.mu2, v.sq2, IM * modes)
    scale2, shift2 = halves(gain[:, CS : CS + CG], bias[:, CS : CS + CG], mean2, inv2)

    def join_step(b, _):
        r, rs = geo.rows_of(b), geo.modes_of(b)
        h = v.f[rs] * scale2 + shift2
        v.h2[rs] = h.astype(BF)
        e = silu_of_half(h)
        er, ei = e[:, :CS].astype(BF), e[:, CS:].astype(BF)
        back = []
        for i in range(IM):
            m = slice(i * modes, (i + 1) * modes)
            back.append(dot(v.mi[...], stack_rows([er[m], ei[m]])))
        j = (v.t[r] + stack_rows(back)).astype(BF)
        v.jv[r] = j
        pre_global = v.p[r, CL:CH] + dot(j, read(ws, "expand", 0, CS))
        y = dot(stack_cols(three_rows(a[r, CL:CH], side, IM)), global_by_row(ws))
        pre_local = v.p[r, 0:CL] + beside(y[:, :CL], wide, -1, side) + y[:, CL : 2 * CL] + beside(y[:, 2 * CL :], wide, 1, side)
        v.p[r, 0:CL] = pre_local
        v.p[r, CL:CH] = pre_global
        ml, sl = moments_of(pre_local)
        mg, sg = moments_of(pre_global)
        v.mu3[b] = stack_cols([ml, mg])
        v.sq3[b] = stack_cols([sl, sg])
        return 0

    lax.fori_loop(0, geo.steps, join_step, 0, unroll=UN)
    mean3, inv3 = combined(v.mu3, v.sq3, IM * pixels)
    scale3, shift3 = halves(gain[:, CS + CG :], bias[:, CS + CG :], mean3, inv3)

    def end_step(b, _):
        r = geo.rows_of(b)
        h = v.p[r] * scale3 + shift3
        v.h3[r] = h.astype(BF)
        y = silu_of_half(h)
        if odd is not None:
            y = y + jnp.where(odd, o[r].astype(F32), 0.0)
        o[r] = y.astype(BF)
        return 0

    lax.fori_loop(0, geo.steps, end_step, 0, unroll=UN)
    return stack_cols([inv1, inv2, inv3])


def norm_terms(sums, gain, bias, factor, count):
    first, second = (jnp.sum(x, axis=0, keepdims=True) for x in sums)
    first = 0.5 * first
    second = (second - bias * first) / gain
    k1 = factor / count * (second * bias / gain - first)
    return first, second, (0.5 * factor, k1, 2.0 / count * factor * second / gain)


def part_sums(c, d, h):
    add = lambda x: jnp.sum(x.reshape(x.shape[0] // 8, 8, x.shape[1]), axis=0)
    return c[0] + add(d), c[1] + add(d * h)


def no_sums(c):
    return jnp.zeros((8, c), F32), jnp.zeros((8, c), F32)


def local_adjoint(geo, v, ws, dp, wide):
    back, same, on = three_rows(dp, geo.side, IM)
    y = dot_nt(stack_cols([on, same, back]), conv_by_column(ws))
    return beside(y[:, :CL], wide, 1, geo.side) + y[:, CL : 2 * CL] + beside(y[:, 2 * CL :], wide, -1, geo.side)


def global_adjoint(geo, v, ws, b):
    taps = stack_rows([stack_cols(nine(v.xp, b * IM + i, geo.side, True)) for i in range(IM)])
    return dot_nt(taps, global_matrix(ws))


def backward_section(geo, v, ws, inv, g, o, even, convs):
    column, wide = geo.column(), geo.wide()
    side, pixels, modes = geo.side, geo.pixels, geo.modes
    n1, n2 = float(geo.images * pixels), float(geo.images * modes)
    gain, bias = read_norms(ws)
    g1, g2, g3 = gain[:, :CS], gain[:, CS : CS + CG], gain[:, CS + CG :]
    b1, b2, b3 = bias[:, :CS], bias[:, CS : CS + CG], bias[:, CS + CG :]
    c1, c2, c3 = g1 * inv[:, :CS], g2 * inv[:, CS : CS + CG], g3 * inv[:, CS + CG :]

    def end_step(b, c):
        r = geo.rows_of(b)
        h = v.h3[r].astype(F32)
        d = g[r].astype(F32) * twice_slope(h)
        v.p[r] = d
        return part_sums(c, d, h)

    first3, second3, k3 = norm_terms(lax.fori_loop(0, geo.steps, end_step, no_sums(CH), unroll=UN), g3, b3, c3, n1)

    def join_step(b, c):
        r, rs = geo.rows_of(b), geo.modes_of(b)
        dp = (k3[0] * v.p[r] + (k3[1] - k3[2] * v.h3[r].astype(F32))).astype(BF)
        v.dpv[r] = dp
        djv = dot_nt(dp[:, CL:], read(ws, "expand", 0, CS))
        v.dj[r] = djv
        djv = djv.astype(BF)
        de = [dot(v.mit[...], djv[i * pixels : (i + 1) * pixels]) for i in range(IM)]
        de = stack_cols([stack_rows([x[:modes] for x in de]), stack_rows([x[modes:] for x in de])])
        h = v.h2[rs].astype(F32)
        d = de * twice_slope(h)
        v.du2[rs] = d
        if convs:
            for i in range(IM):
                three_columns(v.xp, b * IM + i, dp[i * pixels : (i + 1) * pixels, :CL], column, side)
            v.p[r, 0:CL] = local_adjoint(geo, v, ws, dp, wide)
        return part_sums(c, d, h)

    first2, second2, k2 = norm_terms(lax.fori_loop(0, geo.steps, join_step, no_sums(CG), unroll=UN), g2, b2, c2, n2)

    def spectral_step(b, c):
        r, rs = geo.rows_of(b), geo.modes_of(b)
        df = (k2[0] * v.du2[rs] + (k2[1] - k2[2] * v.h2[rs].astype(F32))).astype(BF)
        v.dfv[rs] = df
        ds = dot_nt(df, read(ws, "spectral", 0, CG))
        dr, di = ds[:, :CS].astype(BF), ds[:, CS:].astype(BF)
        back = []
        for i in range(IM):
            m = slice(i * modes, (i + 1) * modes)
            back.append(dot(v.mft[...], stack_rows([dr[m], di[m]])))
        dt = v.dj[r] + stack_rows(back)
        h = v.h1[r].astype(F32)
        d = dt * twice_slope(h)
        v.du1[r] = d
        if convs:
            v.p[r, CL:CH] = global_adjoint(geo, v, ws, b)
        return part_sums(c, d, h)

    first1, second1, k1 = norm_terms(lax.fori_loop(0, geo.steps, spectral_step, no_sums(CS), unroll=UN), g1, b1, c1, n1)

    def reduce_step(b, c):
        r = geo.rows_of(b)
        dq = (k1[0] * v.du1[r] + (k1[1] - k1[2] * v.h1[r].astype(F32))).astype(BF)
        v.dqv[r] = dq
        if convs:
            dx = stack_cols([v.p[r, 0:CL], v.p[r, CL:CH] + dot(dq, read(ws, "reduce", 0, CS))])
            if even is not None:
                dx = dx + jnp.where(even, o[r].astype(F32), 0.0)
            o[r] = dx.astype(BF)
        return c

    lax.fori_loop(0, geo.steps, reduce_step, 0, unroll=UN)
    return stack_cols([first1, first2, first3]), stack_cols([second1, second2, second3])


def weight_terms(geo, v, norms):
    column, side, pixels = geo.column(), geo.side, geo.pixels

    def tap_products(source, flipped, product):
        def columns(b, _):
            three_columns(v.xp, b, source[pl.ds(pl.multiple_of(b * pixels, pixels), pixels), 0:CL], column, side)
            return 0

        lax.fori_loop(0, geo.images, columns, 0)

        def one_row(dh, _):
            def gather(b, _):
                r = pl.ds(pl.multiple_of(b * pixels, pixels), pixels)
                first = pl.multiple_of((2 - dh if flipped else dh) * side, side)
                for dw in range(3):
                    v.taps[r, dw * CL : (dw + 1) * CL] = v.xp[2 - dw if flipped else dw, b, pl.ds(first, pixels)]
                return 0

            lax.fori_loop(0, geo.images, gather, 0)
            product(dh)
            return 0

        lax.fori_loop(0, 3, one_row, 0)

    def from_gradient(dh):
        u = dot_tn(v.ain[:, CL:], v.taps[...])
        for dw in range(3):
            put_terms(v.terms, "local", (dh * 3 + dw) * CH + CL, u[:, dw * CL : (dw + 1) * CL])

    def from_input(dh):
        u = dot_tn(v.taps[...], v.dpv[...])
        for dw in range(3):
            tap = slice(dw * CL, (dw + 1) * CL)
            put_terms(v.terms, "local", (dh * 3 + dw) * CH, u[tap, :CL])
            put_terms(v.terms, "cross", (dh * 3 + dw) * CL, u[tap, CL:])

    tap_products(v.dpv, True, from_gradient)
    tap_products(v.ain, False, from_input)
    put_terms(v.terms, "reduce", 0, dot_tn(v.dqv[...], v.ain[:, CL:]))
    put_terms(v.terms, "spectral", 0, dot_tn(v.sv[0], v.dfv[...]))
    put_terms(v.terms, "spectral", CS, dot_tn(v.sv[1], v.dfv[...]))
    put_terms(v.terms, "expand", 0, dot_tn(v.jv[...], v.dpv[:, CL:]))
    put_norm_terms(v.terms, norms)


def fill_parts(parts, whole, sems):
    rows = whole.shape[0] // len(parts)
    return [pltpu.make_async_copy(ref, whole.at[pl.ds(k * rows, rows)], sems.at[k]) for k, ref in enumerate(parts)]


def start_all(copies):
    for c in copies:
        c.start()


def wait_all(copies):
    for c in copies:
        c.wait()


DMA = pltpu.SemaphoreType.DMA


class Arguments:
    def __init__(self):
        self.ins, self.specs, self.outs, self.out_specs, self.scratch, self.aliases = [], [], [], [], [], {}
        self.names = [[], [], []]

    def take(self, name, value, spec):
        many = isinstance(value, (list, tuple))
        values = list(value) if many else [value]
        self.names[0].append((name, len(values) if many else None))
        at = len(self.ins)
        self.ins += values
        self.specs += [spec] * len(values)
        return at

    def give(self, name, shape, dtype, spec, count=None, over=None):
        self.names[1].append((name, count))
        for i in range(count or 1):
            if over is not None:
                self.aliases[over + i] = len(self.outs)
            self.outs.append(jax.ShapeDtypeStruct(shape, dtype))
            self.out_specs.append(spec)

    def hold(self, name, kind):
        self.names[2].append((name, None))
        self.scratch.append(kind)

    def unpack(self, refs):
        refs, space = list(refs), Space()
        for group in self.names:
            for name, count in group:
                setattr(space, name, refs.pop(0) if count is None else [refs.pop(0) for _ in range(count)])
        return space

    def call(self, body, name, flops, moved=20_000_000):
        results = pl.pallas_call(
            lambda *refs: body(self.unpack(refs)),
            out_shape=self.outs,
            in_specs=self.specs,
            out_specs=self.out_specs,
            scratch_shapes=self.scratch,
            input_output_aliases=self.aliases,
            name=name,
            cost_estimate=pl.CostEstimate(flops=int(flops), bytes_accessed=moved, transcendentals=0),
            compiler_params=pltpu.CompilerParams(vmem_limit_bytes=VMEM_LIMIT),
        )(*self.ins)
        results, space = list(results), Space()
        for out_name, count in self.names[1]:
            setattr(space, out_name, results.pop(0) if count is None else [results.pop(0) for _ in range(count)])
        return space


def take_weights(args, own, arrived, low, high):
    names = needed(low, high)
    args.take("own", own, ANY)
    for name in names:
        args.take("got_" + name, arrived[name], ANY)
    args.hold("w", pltpu.VMEM((high - low, QUARTERS, QROWS, 128), BF))
    args.hold("wsem", DMA((high - low, 4)))
    return names


def got_weights(v, names):
    return {"own": v.own, **{name: getattr(v, "got_" + name) for name in names}}


def hold_forward(args, n, m, images, pixels, side):
    args.hold("mu1", pltpu.VMEM((images // IM, 1, CS), F32))
    args.hold("sq1", pltpu.VMEM((images // IM, 1, CS), F32))
    args.hold("mu2", pltpu.VMEM((images // IM, 1, CG), F32))
    args.hold("sq2", pltpu.VMEM((images // IM, 1, CG), F32))
    args.hold("mu3", pltpu.VMEM((images // IM, 1, CH), F32))
    args.hold("sq3", pltpu.VMEM((images // IM, 1, CH), F32))


def hold_work(args, n, m, images, pixels, side):
    args.hold("xp", pltpu.VMEM((3, images, pixels + 2 * side, CL), BF))
    args.hold("q", pltpu.VMEM((n, CS), F32))
    args.hold("t", pltpu.VMEM((n, CS), F32))
    args.hold("f", pltpu.VMEM((m, CG), F32))
    args.hold("p", pltpu.VMEM((n, CH), F32))


def hold_terms(args, n, m):
    args.hold("dpv", pltpu.VMEM((n, CH), BF))
    args.hold("dqv", pltpu.VMEM((n, CS), BF))
    args.hold("dfv", pltpu.VMEM((m, CG), BF))
    args.hold("ain", pltpu.VMEM((n, CH), BF))
    args.hold("sv", pltpu.VMEM((2, m, CS), BF))
    args.hold("jv", pltpu.VMEM((n, CS), BF))
    args.hold("taps", pltpu.VMEM((n, 3 * CL), BF))
    args.hold("terms", pltpu.VMEM((QUARTERS * QROWS, 128), BF))


def first_call(place, inputs, own, arrived, mf, mi, after, side, images):
    geo = geometry(side, images)
    n, m = images * geo.pixels, images * geo.modes
    args = Arguments()
    args.take("place", place, SMEM)
    args.take("inputs", inputs, ANY)
    args.take("mf", mf, VMEM)
    args.take("mi", mi, VMEM)
    args.take("after", after, ANY)
    names = take_weights(args, own, arrived, 0, 1)
    args.give("out", (n, CH), BF, ANY)
    args.give("h1_out", (n, CS), BF, ANY)
    args.give("h2_out", (m, CG), BF, ANY)
    args.give("h3_out", (n, CH), BF, ANY)
    args.give("spec_out", (2, m, CS), BF, ANY)
    args.give("join_out", (n, CS), BF, ANY)
    args.give("inv_out", (1, NORMS), F32, VMEM)
    args.hold("a", pltpu.VMEM((n, CH), BF))
    args.hold("o", pltpu.VMEM((n, CH), BF))
    args.hold("h1", pltpu.VMEM((n, CS), BF))
    args.hold("h2", pltpu.VMEM((m, CG), BF))
    args.hold("h3", pltpu.VMEM((n, CH), BF))
    args.hold("sv", pltpu.VMEM((2, m, CS), BF))
    args.hold("jv", pltpu.VMEM((n, CS), BF))
    hold_work(args, n, m, images, geo.pixels, side)
    hold_forward(args, n, m, images, geo.pixels, side)
    args.hold("isem", DMA((PARTS,)))
    args.hold("osem", DMA((6,)))

    def body(v):
        loads = fill_parts(v.inputs, v.a, v.isem)
        start_all(loads)
        load_weights(v.place, got_weights(v, names), 0, 1, v.w, v.wsem)
        wait_all(loads)
        wait_weights(v.own, 0, v.w, v.wsem)
        v.inv_out[...] = forward_section(geo, v, v.w.at[0], v.a, v.o, None)
        pairs = (
            (v.o, v.out),
            (v.h1, v.h1_out),
            (v.h2, v.h2_out),
            (v.h3, v.h3_out),
            (v.sv, v.spec_out),
            (v.jv, v.join_out),
        )
        stores = [pltpu.make_async_copy(a, b, v.osem.at[i]) for i, (a, b) in enumerate(pairs)]
        start_all(stores)
        wait_all(stores)

    return args.call(body, "forward_0", 1, 1)


def middle_call(place, out0, inputs, seeds, own, arrived, tables, side, images):
    low, high = 1, 4
    geo = geometry(side, images)
    n, m, count = images * geo.pixels, images * geo.modes, high - low
    args = Arguments()
    args.take("place", place, SMEM)
    args.take("out0", out0, ANY)
    args.take("inputs", inputs, ANY)
    seeds_at = args.take("seeds", seeds, ANY)
    for name, table in zip(("mf", "mi", "mft", "mit"), tables):
        args.take(name, table, VMEM)
    names = take_weights(args, own, arrived, low, high)
    args.give("grads0", (n // PARTS, CH), BF, ANY, PARTS, seeds_at)
    args.give("grad1", (n, CH), BF, ANY)
    args.give("own_out", (n // PARTS, CH), BF, ANY, PARTS)
    args.give("own_grad", (n // PARTS, CH), BF, ANY, PARTS)
    args.give("own_terms", (QUARTERS * QROWS, 128), BF, ANY)
    args.hold("cur", pltpu.VMEM((2, n, CH), BF))
    args.hold("hats1", pltpu.VMEM((count, n, CS), BF))
    args.hold("hats2", pltpu.VMEM((count, m, CG), BF))
    args.hold("hats3", pltpu.VMEM((count, n, CH), BF))
    args.hold("inv", pltpu.VMEM((count, 1, NORMS), F32))
    args.hold("spec", pltpu.VMEM((2, m, CS), BF))
    args.hold("join", pltpu.VMEM((n, CS), BF))
    hold_work(args, n, m, images, geo.pixels, side)
    hold_forward(args, n, m, images, geo.pixels, side)
    hold_terms(args, n, m)
    args.hold("asem", DMA((1,)))
    args.hold("isem", DMA((PARTS,)))
    args.hold("gsem", DMA((PARTS,)))
    args.hold("outsem", DMA((PARTS,)))
    args.hold("gradsem", DMA((PARTS,)))
    args.hold("ksem", DMA((3,)))
    args.hold("tsem", DMA((1,)))
    args.hold("lastsem", DMA((PARTS + 1,)))

    def body(v):
        rank = v.place[0]
        loads = [pltpu.make_async_copy(v.out0, v.cur.at[1], v.asem.at[0])] + fill_parts(v.inputs, v.cur.at[0], v.isem)
        start_all(loads)
        load_weights(v.place, got_weights(v, names), low, high, v.w, v.wsem)
        wait_all(loads)
        rank0_out = part_copies(v.cur.at[1], v.own_out, v.outsem)

        @pl.when(rank == 0)
        def _():
            start_all(rank0_out)

        def at(index, **more):
            return Space(**{**v.__dict__, "h1": v.hats1.at[index], "h2": v.hats2.at[index], "h3": v.hats3.at[index], **more})

        def forward_one(index, _):
            s = index + low
            a, o = v.cur.at[s % 2], v.cur.at[(s + 1) % 2]
            mine = rank == s
            wait_weights(v.own, index, v.w, v.wsem)
            keep_in = pltpu.make_async_copy(a, v.ain, v.ksem.at[0])

            @pl.when(mine)
            def _():
                keep_in.start()

            v.inv[index] = forward_section(geo, at(index, sv=v.spec, jv=v.join), v.w.at[index], a, o, s % 2 == 1)

            @pl.when(mine)
            def _():
                keeps = [
                    pltpu.make_async_copy(v.spec, v.sv, v.ksem.at[1]),
                    pltpu.make_async_copy(v.join, v.jv, v.ksem.at[2]),
                    *part_copies(o, v.own_out, v.outsem),
                ]
                start_all(keeps)
                wait_all([keep_in, *keeps])

            @pl.when(jnp.logical_and(rank == 0, index == 0))
            def _():
                wait_all(rank0_out)

            return 0

        lax.fori_loop(0, count, forward_one, 0)
        loads = fill_parts(v.seeds, v.cur.at[(high - 1) % 2], v.gsem)
        start_all(loads)
        wait_all(loads)

        @pl.when(v.place[3] == 0)
        def _():
            v.cur[(high - 1) % 2] = jnp.zeros((n, CH), BF)

        def backward_one(step, _):
            index = count - 1 - step
            s = index + low
            g, o = v.cur.at[s % 2], v.cur.at[(s + 1) % 2]
            norms = backward_section(geo, at(index, du1=v.q, du2=v.f, dj=v.t), v.w.at[index], v.inv[index], g, o, s % 2 == 0, True)

            @pl.when(rank == s)
            def _():
                keeps = part_copies(o, v.own_grad, v.gradsem)
                start_all(keeps)
                weight_terms(geo, v, norms)
                keeps.append(pltpu.make_async_copy(v.terms, v.own_terms, v.tsem.at[0]))
                keeps[-1].start()
                wait_all(keeps)

            return 0

        lax.fori_loop(0, count, backward_one, 0)
        stores = part_copies(v.cur.at[0], v.grads0, v.lastsem)
        stores.append(pltpu.make_async_copy(v.cur.at[1], v.grad1, v.lastsem.at[PARTS]))
        start_all(stores)
        wait_all(stores)

    return args.call(body, "sections_1_3", images * 6e9)


def last_norms_call(place, first, grads0, inputs, own_terms, weights, arrived, tables, side, images):
    geo = geometry(side, images)
    n, m = images * geo.pixels, images * geo.modes
    args = Arguments()
    args.take("place", place, SMEM)
    args.take("grads0", grads0, ANY)
    args.take("inputs", inputs, ANY)
    args.take("h1_in", first.h1_out, ANY)
    args.take("h2_in", first.h2_out, ANY)
    args.take("h3_in", first.h3_out, ANY)
    args.take("spec_in", first.spec_out, ANY)
    args.take("join_in", first.join_out, ANY)
    args.take("inv", first.inv_out, VMEM)
    for name, table in zip(("mft", "mit"), tables):
        args.take(name, table, VMEM)
    terms_at = args.take("terms_in", own_terms, ANY)
    names = take_weights(args, weights, arrived, 0, 1)
    args.give("dp", (n, CH), BF, ANY)
    args.give("dq", (n, CS), BF, ANY)
    args.give("own_terms", (QUARTERS * QROWS, 128), BF, ANY, None, terms_at)
    args.hold("g", pltpu.VMEM((n, CH), BF))
    args.hold("h1", pltpu.VMEM((n, CS), BF))
    args.hold("h2", pltpu.VMEM((m, CG), BF))
    args.hold("h3", pltpu.VMEM((n, CH), BF))
    hold_work(args, n, m, images, geo.pixels, side)
    hold_terms(args, n, m)
    args.hold("gsem", DMA((PARTS,)))
    args.hold("isem", DMA((PARTS,)))
    args.hold("hsem", DMA((3,)))
    args.hold("ksem", DMA((2,)))
    args.hold("osem", DMA((3,)))

    def body(v):
        rank = v.place[0]
        loads = fill_parts(v.grads0, v.g, v.gsem)
        hats = ((v.h1_in, v.h1), (v.h2_in, v.h2), (v.h3_in, v.h3))
        loads += [pltpu.make_async_copy(a, b, v.hsem.at[i]) for i, (a, b) in enumerate(hats)]
        start_all(loads)
        load_weights(v.place, got_weights(v, names), 0, 1, v.w, v.wsem)
        kept = fill_parts(v.inputs, v.ain, v.isem)
        kept += [pltpu.make_async_copy(v.spec_in, v.sv, v.ksem.at[0]), pltpu.make_async_copy(v.join_in, v.jv, v.ksem.at[1])]

        @pl.when(rank == 0)
        def _():
            start_all(kept)

        wait_all(loads)
        wait_weights(v.own, 0, v.w, v.wsem)
        space = Space(**{**v.__dict__, "du1": v.q, "du2": v.f, "dj": v.t})
        norms = backward_section(geo, space, v.w.at[0], v.inv[...], v.g, None, None, False)
        stores = [pltpu.make_async_copy(v.dpv, v.dp, v.osem.at[0]), pltpu.make_async_copy(v.dqv, v.dq, v.osem.at[1])]
        start_all(stores)

        @pl.when(rank == 0)
        def _():
            wait_all(kept)
            weight_terms(geo, v, norms)
            out = pltpu.make_async_copy(v.terms, v.own_terms, v.osem.at[2])
            out.start()
            out.wait()

        wait_all(stores)

    return args.call(body, "backward_0_norms", images * 400e6)


def last_convs_call(place, back, grad1, own_grad, weights, arrived, side, images):
    geo = geometry(side, images)
    n, m = images * geo.pixels, images * geo.modes
    args = Arguments()
    args.take("place", place, SMEM)
    args.take("dp", back.dp, ANY)
    args.take("dq", back.dq, ANY)
    args.take("grad1", grad1, ANY)
    grad_at = args.take("grad_in", own_grad, ANY)
    names = take_weights(args, weights, arrived, 0, 1)
    args.give("own_grad", (n // PARTS, CH), BF, ANY, PARTS, grad_at)
    args.hold("dpv", pltpu.VMEM((n, CH), BF))
    args.hold("dqv", pltpu.VMEM((n, CS), BF))
    args.hold("o", pltpu.VMEM((n, CH), BF))
    args.hold("xp", pltpu.VMEM((3, images, geo.pixels + 2 * side, CL), BF))
    args.hold("lsem", DMA((3,)))
    args.hold("osem", DMA((PARTS,)))

    def body(v):
        @pl.when(v.place[0] == 0)
        def _():
            pairs = ((v.dp, v.dpv), (v.dq, v.dqv), (v.grad1, v.o))
            loads = [pltpu.make_async_copy(a, b, v.lsem.at[i]) for i, (a, b) in enumerate(pairs)]
            start_all(loads)
            load_weights(v.place, got_weights(v, names), 0, 1, v.w, v.wsem)
            wait_all(loads)
            wait_weights(v.own, 0, v.w, v.wsem)
            ws = v.w.at[0]
            column, wide = geo.column(), geo.wide()

            def step(b, _):
                r = geo.rows_of(b)
                dp = v.dpv[r]
                for i in range(IM):
                    three_columns(v.xp, b * IM + i, dp[i * geo.pixels : (i + 1) * geo.pixels, :CL], column, side)
                dxl = local_adjoint(geo, v, ws, dp, wide)
                dxg = global_adjoint(geo, v, ws, b) + dot(v.dqv[r], read(ws, "reduce", 0, CS))
                v.o[r] = (stack_cols([dxl, dxg]) + v.o[r].astype(F32)).astype(BF)
                return 0

            lax.fori_loop(0, geo.steps, step, 0)
            stores = part_copies(v.o, v.own_grad, v.osem)
            start_all(stores)
            wait_all(stores)

    return args.call(body, "backward_0_convs", images * 600e6)


def exchange_weights(send, after):
    def over(bit, x):
        return lax.ppermute(x, "pipe", [(i ^ bit, i) for i in range(4)])

    def swap(x):
        return lax.ppermute(x, "dp", [(i, i ^ 1) for i in range(lax.axis_size("dp"))])

    got = {"x1": over(1, send), "y1": over(2, send)}
    over_x, over_y = relay_call(got["y1"], got["x1"], after)
    got["x2"], got["y2"] = over(1, over_x), over(2, over_y)
    return {name: (x, swap(x)) for name, x in got.items()}


def local_device(images_in, conv_local, conv_cross, reduce_weight, spectral_weight, expand_weight, norm_gain, norm_bias, cotangent, hole_mask):
    batches, _, side, _, channels = images_in.shape
    pixels = side * side
    dp_size = lax.axis_size("dp")
    dp_rank = lax.axis_index("dp")
    core = dp_rank % 2
    holders = range(1, 1 + batches)
    holds = jnp.logical_and(dp_rank >= holders.start, dp_rank < holders.stop)
    place = jnp.stack([lax.axis_index("pipe"), core, dp_rank // 2, holds]).astype(jnp.int32)
    table_to, table_from = dft_np(side)
    mf, mi = jnp.asarray(table_to, BF), jnp.asarray(table_from, BF)
    mft, mit = jnp.asarray(table_to.T, BF), jnp.asarray(table_from.T, BF)

    def swap(x):
        return lax.ppermute(x, "dp", [(i, i ^ 1) for i in range(dp_size)])

    def along_z(k, x, pairs):
        return lax.ppermute(x, "dp", [(i, j) for i, j in pairs if i ^ j == 2 * k])

    to_holders = [(i, j) for i in range(dp_size) for j in holders]
    from_holders = [(j, i) for i, j in to_holders]

    def to_batches(x, through=(), after=()):
        other = swap(lax.dynamic_index_in_dim(x.reshape(batches // 2, 2, pixels, channels), core, 1, keepdims=False))
        parts = spread_call(place, x, other, through, after)
        through = parts[PARTS:]
        parts = list(parts[:1]) + [along_z(k, parts[k], to_holders) for k in range(1, PARTS)]
        return [part.reshape(2 * pixels, channels) for part in parts], *through

    def to_images(parts, dtype):
        parts = list(parts[:1]) + [along_z(k, parts[k], from_holders) for k in range(1, PARTS)]
        other = swap(second_images_call(parts))
        return collect_call(place, batches, parts, other, dtype).reshape(1, batches, 1, side, side, channels)

    own, send = pack_call(
        place,
        conv_local.reshape(-1, CL),
        conv_cross.reshape(-1, CG),
        reduce_weight[0].T,
        spectral_weight[0],
        expand_weight[0],
        norm_gain,
        norm_bias,
    )
    inputs, send = to_batches(images_in.reshape(batches, pixels, channels), (send,))
    hole_float = hole_mask.astype(F32)
    hole_counts = jnp.sum(hole_float, axis=(2, 3), keepdims=True)
    weighting = 0.25 + hole_float * pixels / (hole_counts + pixels / 8.0)
    seed = (cotangent.astype(F32) * weighting[..., None]).astype(BF)

    seeds, *_ = to_batches(seed.reshape(batches, pixels, channels), after=inputs[1:])
    arrived = exchange_weights(send, seeds[:1])
    first = first_call(place, inputs, own, arrived, mf, mi, seeds[1:3], side, dp_size)
    middle = middle_call(place, first.out, inputs, seeds, own, arrived, (mf, mi, mft, mit), side, dp_size)
    activations = to_images(middle.own_out, BF)
    back = last_norms_call(
        place, first, middle.grads0, inputs, middle.own_terms, own, arrived, (mft, mit), side, dp_size
    )
    own_grad = last_convs_call(place, back, middle.grad1, middle.own_grad, own, arrived, side, dp_size).own_grad
    own_terms = back.own_terms
    input_grads = to_images(own_grad, F32)
    local, cross, reduce_w, spectral, expand, gain, bias = unpack_call(lax.psum(own_terms, "dp"))
    return (
        activations,
        input_grads,
        local.reshape(conv_local.shape),
        cross.reshape(conv_cross.shape),
        reduce_w.T[None],
        spectral[None],
        expand[None],
        gain,
        bias,
    )


def solution(mesh):
    placed = (
        P(None, "dp", None, None, None),
        P("pipe", None, None, None, None),
        P("pipe", None, None, None, None),
        P("pipe", None, None),
        P("pipe", None, None),
        P("pipe", None, None),
        P("pipe", None),
        P("pipe", None),
        P(None, "dp", None, None, None),
        P(None, "dp", None, None),
    )

    def on_device(images_in, *rest):
        dp_size = lax.axis_size("dp")
        fits = images_in.shape[1] == 1 and dp_size == 8 and images_in.shape[0] == dp_size - 2 and lax.axis_size("pipe") == 4
        return (local_device if fits else general_device)(images_in, *rest)

    return jax.shard_map(
        on_device,
        mesh=mesh,
        in_specs=placed,
        out_specs=(
            P("pipe", None, "dp", None, None, None),
            P("pipe", None, "dp", None, None, None),
            P("pipe", None, None, None, None),
            P("pipe", None, None, None, None),
            P("pipe", None, None),
            P("pipe", None, None),
            P("pipe", None, None),
            P("pipe", None),
            P("pipe", None),
        ),
        check_vma=False,
    )
```

```python
import functools
import math

import jax
import jax.numpy as jnp
import numpy as np
from jax import lax
from jax.experimental import pallas as pl
from jax.experimental.pallas import tpu as pltpu
from jax.sharding import PartitionSpec as P

CL = 128
CG = 384
CS = 192
CH = 512
NORMS = 1088
F32 = jnp.float32
BF = jnp.bfloat16
IM = 4
UN = 2


EPS = 1e-05
HIGH = lax.Precision.HIGHEST


def from_behind(x, axis, by):
    length = lax.axis_size(axis)
    pairs = [(i, i + by) for i in range(length) if 0 <= i + by < length]
    return lax.ppermute(x, axis, pairs)


def smooth(values):
    return values * jax.nn.sigmoid(values)


def smooth_slope(values):
    logistic = jax.nn.sigmoid(values)
    return logistic * (1.0 + values * (1.0 - logistic))


def patches(values):
    height, breadth = (values.shape[1], values.shape[2])
    padded = jnp.pad(values, ((0, 0), (1, 1), (1, 1), (0, 0)))
    return jnp.concatenate(
        [
            padded[:, row_off : row_off + height, col_off : col_off + breadth]
            for row_off in range(3)
            for col_off in range(3)
        ],
        axis=-1,
    )


def conv_apply(values, kernel):
    flat_kernel = kernel.reshape(-1, kernel.shape[-1])
    return jnp.einsum(
        "bhwk,kd->bhwd", patches(values), flat_kernel, preferred_element_type=jnp.float32
    )


def conv_weight_grad(values, grad_low, kernel_shape):
    return jnp.einsum(
        "bhwk,bhwd->kd", patches(values), grad_low, preferred_element_type=jnp.float32
    ).reshape(kernel_shape)


def conv_input_grad(grad_low, kernel):
    flipped = jnp.flip(kernel, (0, 1)).transpose(0, 1, 3, 2)
    return conv_apply(grad_low, flipped)


def dft_tables(side_len):
    frequencies = side_len // 2 + 1
    spatial = jnp.arange(side_len, dtype=jnp.int32)
    spectral = jnp.arange(frequencies, dtype=jnp.int32)
    angle_cols = (spatial[:, None] * spectral[None, :] % side_len).astype(jnp.float32) * (
        2.0 * math.pi / side_len
    )
    angle_rows = (spatial[:, None] * spatial[None, :] % side_len).astype(jnp.float32) * (
        2.0 * math.pi / side_len
    )
    fold_factor = jnp.where((spectral == 0) | (2 * spectral == side_len), 1.0, 2.0).astype(
        jnp.float32
    )
    return (
        jnp.cos(angle_cols),
        jnp.sin(angle_cols),
        jnp.cos(angle_rows),
        jnp.sin(angle_rows),
        fold_factor,
    )


def to_spectrum(field_in, tables):
    cosine_cols, sine_cols, cosine_rows, sine_rows, _ = tables
    scaling = 1.0 / math.sqrt(field_in.shape[1] * field_in.shape[2])
    real_along = jnp.einsum("bhwc,wk->bhkc", field_in, cosine_cols, precision=HIGH)
    imaginary_along = -jnp.einsum("bhwc,wk->bhkc", field_in, sine_cols, precision=HIGH)
    real_part = jnp.einsum("bhkc,gh->bgkc", real_along, cosine_rows, precision=HIGH) + jnp.einsum(
        "bhkc,gh->bgkc", imaginary_along, sine_rows, precision=HIGH
    )
    imaginary_part = jnp.einsum(
        "bhkc,gh->bgkc", imaginary_along, cosine_rows, precision=HIGH
    ) - jnp.einsum("bhkc,gh->bgkc", real_along, sine_rows, precision=HIGH)
    return jnp.concatenate([real_part, imaginary_part], axis=-1) * scaling


def from_spectrum(field_in, tables):
    cosine_cols, sine_cols, cosine_rows, sine_rows, fold_factor = tables
    scaling = 1.0 / math.sqrt(field_in.shape[1] * cosine_cols.shape[0])
    half_width = field_in.shape[-1] // 2
    real_in = field_in[..., :half_width]
    imaginary_in = field_in[..., half_width:]
    real_rows = jnp.einsum("bgkc,gh->bhkc", real_in, cosine_rows, precision=HIGH) - jnp.einsum(
        "bgkc,gh->bhkc", imaginary_in, sine_rows, precision=HIGH
    )
    imaginary_rows = jnp.einsum(
        "bgkc,gh->bhkc", imaginary_in, cosine_rows, precision=HIGH
    ) + jnp.einsum("bgkc,gh->bhkc", real_in, sine_rows, precision=HIGH)
    folding = fold_factor[None, None, :, None]
    field_out = jnp.einsum(
        "bhkc,wk->bhwc", real_rows * folding, cosine_cols, precision=HIGH
    ) - jnp.einsum("bhkc,wk->bhwc", imaginary_rows * folding, sine_cols, precision=HIGH)
    return field_out * scaling


def moments(values):
    sum_axes = tuple(range(values.ndim - 1))
    count_all = math.prod(values.shape[:-1]) * lax.axis_size("dp")
    average = lax.psum(jnp.sum(values, axis=sum_axes), "dp") / count_all
    centred = values - average
    spread = lax.psum(jnp.sum(centred * centred, axis=sum_axes), "dp") / count_all
    return (average, lax.rsqrt(spread + EPS))


def norm_back(grad_out, act_values, hat_values, gain_slice, inv_std):
    sum_axes = tuple(range(act_values.ndim - 1))
    count_all = math.prod(act_values.shape[:-1]) * lax.axis_size("dp")
    grad_act = grad_out * smooth_slope(act_values)
    sum_act, sum_hat = lax.psum(
        (jnp.sum(grad_act, axis=sum_axes), jnp.sum(grad_act * hat_values, axis=sum_axes)), "dp"
    )
    grad_values = gain_slice * inv_std * (grad_act - (sum_act + hat_values * sum_hat) / count_all)
    return (grad_values, sum_hat, sum_act)


def section_compute(inputs, weights, norm_gains, norm_biases, measure, tables):
    local_kernel, cross_kernel, reduce_matrix, spectral_matrix, expand_matrix = weights

    def normalize(values, offset):
        extent = values.shape[-1]
        average, inv_std = measure(values, offset)
        hat_values = (values - average) * inv_std
        return (
            hat_values,
            norm_gains[offset : offset + extent] * hat_values
            + norm_biases[offset : offset + extent],
        )

    local_part = inputs[..., :CL]
    global_part = inputs[..., CL:]
    pre_local = conv_apply(inputs, local_kernel)
    reduced = jnp.einsum(
        "bhwc,cd->bhwd", global_part, reduce_matrix, preferred_element_type=jnp.float32
    )
    hat_one, act_one = normalize(reduced, 0)
    activated = smooth(act_one)
    spec_low = to_spectrum(activated, tables).astype(jnp.bfloat16)
    spectral_mix = jnp.einsum(
        "bhkc,cd->bhkd", spec_low, spectral_matrix, preferred_element_type=jnp.float32
    )
    hat_two, act_two = normalize(spectral_mix, CS)
    joined = (activated + from_spectrum(smooth(act_two), tables)).astype(jnp.bfloat16)
    pre_global = conv_apply(local_part, cross_kernel) + jnp.einsum(
        "bhwc,cd->bhwd", joined, expand_matrix, preferred_element_type=jnp.float32
    )
    hat_end, act_end = normalize(jnp.concatenate([pre_local, pre_global], axis=-1), CS + CG)
    return (
        smooth(act_end),
        (hat_one, act_one, activated, spec_low, hat_two, act_two, joined, hat_end, act_end),
    )


def section_backward(inputs, weights, norm_gains, inv_std, saved, grad_result, tables):
    local_kernel, cross_kernel, reduce_matrix, spectral_matrix, expand_matrix = weights
    hat_one, act_one, activated, spec_low, hat_two, act_two, joined, hat_end, act_end = saved
    local_part = inputs[..., :CL]
    global_part = inputs[..., CL:]
    grad_end, gain_end, bias_end = norm_back(
        grad_result, act_end, hat_end, norm_gains[CS + CG :], inv_std[CS + CG :]
    )
    grad_end_low = grad_end.astype(jnp.bfloat16)
    grad_pre_local = grad_end_low[..., :CL]
    grad_pre_global = grad_end_low[..., CL:]
    grad_cross = conv_weight_grad(local_part, grad_pre_global, cross_kernel.shape)
    grad_expand = jnp.einsum(
        "bhwc,bhwd->cd", joined, grad_pre_global, preferred_element_type=jnp.float32
    )
    grad_joined = jnp.einsum(
        "bhwd,cd->bhwc", grad_pre_global, expand_matrix, preferred_element_type=jnp.float32
    )
    _, inverse_pull = jax.vjp(
        lambda field_in: from_spectrum(field_in, tables), jnp.zeros(act_two.shape, jnp.float32)
    )
    (grad_after,) = inverse_pull(grad_joined)
    grad_mix, gain_two, bias_two = norm_back(
        grad_after, act_two, hat_two, norm_gains[CS : CS + CG], inv_std[CS : CS + CG]
    )
    grad_mix_low = grad_mix.astype(jnp.bfloat16)
    grad_spectral = jnp.einsum(
        "bhkc,bhkd->cd", spec_low, grad_mix_low, preferred_element_type=jnp.float32
    )
    grad_spec = jnp.einsum(
        "bhkd,cd->bhkc", grad_mix_low, spectral_matrix, preferred_element_type=jnp.float32
    )
    _, forward_pull = jax.vjp(lambda field_in: to_spectrum(field_in, tables), activated)
    (grad_activated,) = forward_pull(grad_spec)
    grad_reduced, gain_one, bias_one = norm_back(
        grad_activated + grad_joined, act_one, hat_one, norm_gains[:CS], inv_std[:CS]
    )
    grad_reduced_low = grad_reduced.astype(jnp.bfloat16)
    grad_reduce = jnp.einsum(
        "bhwc,bhwd->cd", global_part, grad_reduced_low, preferred_element_type=jnp.float32
    )
    grad_global = jnp.einsum(
        "bhwd,cd->bhwc", grad_reduced_low, reduce_matrix, preferred_element_type=jnp.float32
    )
    grad_local = conv_input_grad(grad_pre_global, cross_kernel)
    grad_local_kernel = conv_weight_grad(inputs, grad_pre_local, local_kernel.shape)
    grad_inputs = conv_input_grad(grad_pre_local, local_kernel) + jnp.concatenate(
        [grad_local, grad_global], axis=-1
    )
    gain_terms = jnp.concatenate([gain_one, gain_two, gain_end])
    bias_terms = jnp.concatenate([bias_one, bias_two, bias_end])
    return (
        grad_inputs,
        (grad_local_kernel, grad_cross, grad_reduce, grad_spectral, grad_expand),
        gain_terms,
        bias_terms,
    )


def store(buffer, value, slot_index, active):
    previous = lax.dynamic_index_in_dim(buffer, slot_index, 0, keepdims=False)
    return lax.dynamic_update_index_in_dim(
        buffer, jnp.where(active, value, previous), slot_index, 0
    )


def general_device(
    images_in,
    conv_local,
    conv_cross,
    reduce_weight,
    spectral_weight,
    expand_weight,
    norm_gain,
    norm_bias,
    cotangent,
    hole_mask,
):
    section_count = lax.axis_size("pipe")
    section_rank = lax.axis_index("pipe")
    batches = images_in.shape[0]
    step_count = batches + section_count - 1
    odd_section = section_rank % 2 == 1
    last_section = section_rank == section_count - 1
    weights = (conv_local[0], conv_cross[0], reduce_weight[0], spectral_weight[0], expand_weight[0])
    norm_gains = norm_gain[0]
    norm_biases = norm_bias[0]
    tables = dft_tables(images_in.shape[2])
    blank = jnp.zeros(images_in.shape[1:], jnp.bfloat16)

    def forward_step(carried, step_index):
        recv_act, recv_res, kept_inputs, kept_stats, kept_outputs = carried
        batch_index = step_index - section_rank
        active = (batch_index >= 0) & (batch_index < batches)
        slot_index = jnp.clip(batch_index, 0, batches - 1)
        fresh_image = lax.dynamic_index_in_dim(images_in, slot_index, 0, keepdims=False)
        inputs = jnp.where(section_rank == 0, fresh_image, recv_act)
        recorded = []

        def measure(values, offset):
            average, inv_std = moments(values)
            recorded.append((average, inv_std))
            return (average, inv_std)

        result, _ = section_compute(inputs, weights, norm_gains, norm_biases, measure, tables)
        summed = result + jnp.where(odd_section, recv_res.astype(jnp.float32), 0.0)
        outgoing = summed.astype(jnp.bfloat16)
        residual_out = jnp.where(odd_section, outgoing, inputs)
        next_act, next_res = from_behind((outgoing, residual_out), "pipe", 1)
        statistics = jnp.stack(
            [
                jnp.concatenate([entry_pair[0] for entry_pair in recorded]),
                jnp.concatenate([entry_pair[1] for entry_pair in recorded]),
            ]
        )
        kept_inputs = store(kept_inputs, inputs, slot_index, active)
        kept_stats = store(kept_stats, statistics, slot_index, active)
        kept_outputs = store(kept_outputs, outgoing, slot_index, active)
        return ((next_act, next_res, kept_inputs, kept_stats, kept_outputs), None)

    forward_init = (
        blank,
        blank,
        jnp.zeros(images_in.shape, jnp.bfloat16),
        jnp.zeros((batches, 2, NORMS), jnp.float32),
        jnp.zeros(images_in.shape, jnp.bfloat16),
    )
    forward_state = lax.scan(forward_step, forward_init, jnp.arange(step_count))[0]
    kept_inputs, kept_stats, kept_outputs = (forward_state[2], forward_state[3], forward_state[4])
    pixels = images_in.shape[2] * images_in.shape[3]
    hole_float = hole_mask.astype(jnp.float32)
    hole_counts = jnp.sum(hole_float, axis=(2, 3), keepdims=True)
    weighting = 0.25 + hole_float * pixels / (hole_counts + pixels / 8.0)

    def backward_step(carried, step_index):
        recv_grad, recv_res, grad_store, weight_sums, gain_sum, bias_sum = carried
        batch_index = step_index - (section_count - 1 - section_rank)
        active = (batch_index >= 0) & (batch_index < batches)
        slot_index = jnp.clip(batch_index, 0, batches - 1)
        cotan_slot = lax.dynamic_index_in_dim(cotangent, slot_index, 0, keepdims=False).astype(
            jnp.float32
        )
        weight_slot = lax.dynamic_index_in_dim(weighting, slot_index, 0, keepdims=False)
        seed_grad = (cotan_slot * weight_slot[..., None]).astype(jnp.bfloat16)
        incoming = jnp.where(last_section, seed_grad, recv_grad)
        inputs = lax.dynamic_index_in_dim(kept_inputs, slot_index, 0, keepdims=False)
        statistics = lax.dynamic_index_in_dim(kept_stats, slot_index, 0, keepdims=False)

        def measure(values, offset):
            extent = values.shape[-1]
            return (
                statistics[0, offset : offset + extent],
                statistics[1, offset : offset + extent],
            )

        _, saved = section_compute(inputs, weights, norm_gains, norm_biases, measure, tables)
        grad_inputs, weight_terms, gain_terms, bias_terms = section_backward(
            inputs, weights, norm_gains, statistics[1], saved, incoming.astype(jnp.float32), tables
        )
        grad_total = grad_inputs + jnp.where(odd_section, 0.0, recv_res.astype(jnp.float32))
        outgoing = grad_total.astype(jnp.bfloat16)
        residual_out = jnp.where(odd_section, incoming, outgoing)
        next_grad, next_res = from_behind((outgoing, residual_out), "pipe", -1)
        weight_sums = tuple(
            (
                running + jnp.where(active, addend, 0.0)
                for running, addend in zip(weight_sums, weight_terms)
            )
        )
        gain_sum = gain_sum + jnp.where(active, gain_terms, 0.0)
        bias_sum = bias_sum + jnp.where(active, bias_terms, 0.0)
        grad_store = store(grad_store, grad_total, slot_index, active)
        return ((next_grad, next_res, grad_store, weight_sums, gain_sum, bias_sum), None)

    zero_weights = tuple((jnp.zeros(entry_weight.shape, jnp.float32) for entry_weight in weights))
    backward_init = (
        blank,
        blank,
        jnp.zeros(images_in.shape, jnp.float32),
        zero_weights,
        jnp.zeros((NORMS,), jnp.float32),
        jnp.zeros((NORMS,), jnp.float32),
    )
    state_end = lax.scan(backward_step, backward_init, jnp.arange(0, 0 + step_count))[0]
    sum_local, sum_cross, sum_reduce, sum_spectral, sum_expand = state_end[3]
    totals = lax.psum((sum_local, sum_cross, sum_reduce, sum_spectral, sum_expand), "dp")
    return (
        kept_outputs[None],
        state_end[2][None],
        totals[0][None],
        totals[1][None],
        totals[2][None],
        totals[3][None],
        totals[4][None],
        state_end[4][None],
        state_end[5][None],
    )


PARTS = 4
ANY = pl.BlockSpec(memory_space=pl.ANY)
VMEM = pl.BlockSpec(memory_space=pltpu.VMEM)
SMEM = pl.BlockSpec(memory_space=pltpu.SMEM)
VMEM_LIMIT = 63 * 2**20


def dft_np(side):
    spatial = np.arange(side)
    spectral = np.arange(side // 2 + 1)
    turns = spatial[:, None, None, None] * spatial[None, None, :, None] + spectral[None, :, None, None] * spatial[None, None, None, :]
    angle = (turns % side).reshape(side * spectral.size, side * side) * (2.0 * np.pi / side)
    fold = np.broadcast_to(np.where((spectral == 0) | (2 * spectral == side), 1.0, 2.0), (side, spectral.size)).reshape(-1, 1)
    forward = np.concatenate([np.cos(angle), -np.sin(angle)]) / side
    inverse = np.concatenate([np.cos(angle) * fold, -np.sin(angle) * fold]).T / side
    return forward, inverse


def dot(a, b):
    return lax.dot_general(a, b, (((1,), (0,)), ((), ())), preferred_element_type=F32)


def dot_nt(a, b):
    return lax.dot_general(a, b, (((1,), (1,)), ((), ())), preferred_element_type=F32)


def dot_tn(a, b):
    return lax.dot_general(a, b, (((0,), (0,)), ((), ())), preferred_element_type=F32)


def silu_of_half(h):
    return h + h * jnp.tanh(h)


def twice_slope(h):
    t = jnp.tanh(h)
    return (1.0 + t) * (1.0 + h * (1.0 - t))


QUARTERS, QROWS = 4, 2640
LAYOUT = {
    "local": (0, 1152, 1),
    "cross": (1152, 288, 3),
    "reduce": (2016, 48, 3),
    "spectral": (2160, 96, 3),
    "expand": (2448, 48, 3),
    "norms": (2592, 16, 3),
}


def pieces(name, start, count, block=0):
    base, rows, _ = LAYOUT[name]
    found = []
    while count:
        quarter, offset = divmod(start, rows)
        take = min(count, rows - offset)
        found.append((quarter, base + block * rows + offset, take))
        start, count = start + take, count - take
    return found


def stack_rows(parts):
    return parts[0] if len(parts) == 1 else jnp.concatenate(parts, axis=0)


def stack_cols(parts):
    return parts[0] if len(parts) == 1 else jnp.concatenate(parts, axis=1)


def read(w, name, start, count):
    blocks = LAYOUT[name][2]
    return stack_cols([stack_rows([w[q, r : r + n] for q, r, n in pieces(name, start, count, j)]) for j in range(blocks)])


def write(w, name, start, value):
    for j in range(LAYOUT[name][2]):
        done = 0
        for q, r, n in pieces(name, start, value.shape[0], j):
            w[q, r : r + n] = value[done : done + n, j * 128 : (j + 1) * 128].astype(w.dtype)
            done += n


def norm_rows(w):
    base = LAYOUT["norms"][0]
    return stack_cols([w[j // 3, base + 16 * (j % 3) : base + 16 * (j % 3) + 16] for j in range(9)]).astype(F32)[:, :NORMS]


def read_norms(w):
    rows = norm_rows(w)
    return rows[0:1] + rows[1:2], rows[2:3] + rows[3:4]


def norm_block(vectors):
    rows = stack_rows([*vectors, jnp.zeros((16 - len(vectors), NORMS), F32)])
    return stack_cols([rows, jnp.zeros((16, 12 * 128 - NORMS), F32)]).astype(BF)


def write_norms(w, vectors):
    base = LAYOUT["norms"][0]
    rows = norm_block(vectors)
    for j in range(12):
        w[j // 3, base + 16 * (j % 3) : base + 16 * (j % 3) + 16] = rows[:, j * 128 : (j + 1) * 128]


TERMS = {
    "local": (0, 9 * CH, 1),
    "cross": (9 * CH, 9 * CL, 3),
    "reduce": (9 * (CH + CG), CS, 3),
    "spectral": (9 * (CH + CG) + 3 * CS, CG, 3),
    "expand": (9 * (CH + CG) + 3 * (CS + CG), CS, 3),
    "norms": (9 * (CH + CG) + 3 * (2 * CS + CG), 16, 12),
}


def put_terms(w, name, start, value):
    base, rows, blocks = TERMS[name]
    count = value.shape[0]
    for j in range(blocks):
        first = base + j * rows + start
        w[pl.ds(first if isinstance(first, int) else pl.multiple_of(first, 128), count)] = value[:, j * 128 : (j + 1) * 128].astype(BF)


def put_norm_terms(w, vectors):
    base = TERMS["norms"][0]
    rows = norm_block(vectors)
    for j in range(12):
        w[base + 16 * j : base + 16 * (j + 1)] = rows[:, j * 128 : (j + 1) * 128]


def get_terms(w, name, columns):
    base, rows, blocks = TERMS[name]
    return stack_cols([w[base + j * rows : base + (j + 1) * rows] for j in range(blocks)]).astype(F32)[:, :columns]


def conv_matrix(w):
    return stack_rows([stack_cols([read(w, "local", k * CH, CL), read(w, "cross", k * CL, CL)]) for k in range(9)])


def global_matrix(w):
    return stack_cols([read(w, "local", k * CH + CL, CG) for k in range(9)])


def global_by_row(w):
    return stack_rows([stack_cols([read(w, "local", (dh * 3 + dw) * CH + CL, CG) for dw in range(3)]) for dh in range(3)])


def conv_by_column(w):
    return stack_rows(
        [
            stack_cols([part for k in (dw, 3 + dw, 6 + dw) for part in (read(w, "local", k * CH, CL), read(w, "cross", k * CL, CL))])
            for dw in range(3)
        ]
    )


def pack_kernel(place, local, cross, reduce_w, spectral, expand, gains, biases, own, send, packed, sem):
    packed_rows = lambda name, value: write(packed, name, 0, value)
    packed_rows("local", local[...])
    packed_rows("cross", cross[...])
    packed_rows("reduce", reduce_w[...])
    packed_rows("spectral", spectral[...])
    packed_rows("expand", expand[...])
    halves = []
    for values in (gains[...], biases[...]):
        high = values.astype(BF)
        halves += [high.astype(F32), values - high.astype(F32)]
    write_norms(packed, halves)
    core = place[1]
    copies = [pltpu.make_async_copy(packed.at[2 * half + core], send.at[half], sem.at[half]) for half in range(2)]
    copies += [pltpu.make_async_copy(packed.at[q], own.at[pl.ds(q * QROWS, QROWS)], sem.at[2 + q]) for q in range(QUARTERS)]
    for c in copies:
        c.start()
    for c in copies:
        c.wait()


def pack_call(place, *weights):
    shape = jax.ShapeDtypeStruct
    return pl.pallas_call(
        pack_kernel,
        out_shape=[shape((QUARTERS * QROWS, 128), BF), shape((2, QROWS, 128), BF)],
        in_specs=[SMEM] + [VMEM] * 7,
        out_specs=[ANY] * 2,
        scratch_shapes=[pltpu.VMEM((QUARTERS, QROWS, 128), BF), pltpu.SemaphoreType.DMA((2 + QUARTERS,))],
        name="pack_weights",
        compiler_params=pltpu.CompilerParams(vmem_limit_bytes=VMEM_LIMIT),
    )(place, *weights)


def relay_kernel(skip, *refs):
    y1, x1 = refs[:2]
    over_x, over_y, stage, sem_in, sem_out = refs[2 + skip :]
    loads = [pltpu.make_async_copy(y1.at[0], stage.at[0], sem_in.at[0]), pltpu.make_async_copy(x1.at[1], stage.at[1], sem_in.at[1])]
    stores = [pltpu.make_async_copy(stage.at[i], ref.at[0], sem_out.at[i]) for i, ref in enumerate((over_x, over_y))]
    for c in loads:
        c.start()
    for load, store in zip(loads, stores):
        load.wait()
        store.start()
    for c in stores:
        c.wait()


def relay_call(y1, x1, after):
    dma = pltpu.SemaphoreType.DMA
    return pl.pallas_call(
        functools.partial(relay_kernel, len(after)),
        out_shape=[jax.ShapeDtypeStruct((1, QROWS, 128), BF)] * 2,
        in_specs=[ANY] * (2 + len(after)),
        out_specs=[ANY] * 2,
        scratch_shapes=[pltpu.VMEM((2, QROWS, 128), BF), dma((2,)), dma((2,))],
        name="relay_weights",
    )(y1, x1, *after)


def unpack_kernel(packed, *refs):
    local, cross, reduce_w, spectral, expand, gains, biases = refs[-7:]
    local[...] = get_terms(packed, "local", CL)
    cross[...] = get_terms(packed, "cross", CG)
    reduce_w[...] = get_terms(packed, "reduce", CG)
    spectral[...] = get_terms(packed, "spectral", CG)
    expand[...] = get_terms(packed, "expand", CG)
    rows = get_terms(packed, "norms", NORMS)
    biases[...] = rows[0:1]
    gains[...] = rows[1:2]


def unpack_call(packed, after):
    shape = jax.ShapeDtypeStruct
    dims = ((9 * CH, CL), (9 * CL, CG), (CS, CG), (CG, CG), (CS, CG), (1, NORMS), (1, NORMS))
    return pl.pallas_call(
        unpack_kernel,
        out_shape=[shape(d, F32) for d in dims],
        in_specs=[VMEM] + [ANY] * len(after),
        out_specs=[VMEM] * 7,
        name="unpack_terms",
        compiler_params=pltpu.CompilerParams(vmem_limit_bytes=VMEM_LIMIT),
    )(packed, *after)


def spread_kernel(batches, place, images, other, *refs):
    parts, sem = refs[:PARTS], refs[-1]
    core, z = place[1], place[2]
    copies = []
    for k, part in enumerate(parts):
        i = jnp.clip((z ^ k) - (1 - core), 0, batches // 2 - 1)
        copies.append(pltpu.make_async_copy(images.at[2 * i + 1 - core], part.at[0], sem.at[k, 0]))
        copies.append(pltpu.make_async_copy(other.at[i], part.at[1], sem.at[k, 1]))
    for c in copies:
        c.start()
    for c in copies:
        c.wait()


def spread_call(place, images, other, through=(), after=()):
    batches, pixels, channels = images.shape
    skip = len(through) + len(after)

    def kernel(place, images, other, *refs):
        spread_kernel(batches, place, images, other, *refs[skip:])

    return pl.pallas_call(
        kernel,
        out_shape=[jax.ShapeDtypeStruct((2, pixels, channels), BF)] * PARTS + [jax.ShapeDtypeStruct(x.shape, x.dtype) for x in through],
        in_specs=[SMEM, VMEM, VMEM] + [ANY] * skip,
        out_specs=[ANY] * (PARTS + len(through)),
        scratch_shapes=[pltpu.SemaphoreType.DMA((PARTS, 2))],
        input_output_aliases={3 + i: PARTS + i for i in range(len(through))},
        name="spread_images",
        compiler_params=pltpu.CompilerParams(vmem_limit_bytes=VMEM_LIMIT),
    )(place, images, other, *through, *after)


def second_images(p0, p1, p2, p3, out, stage, sem_in, sem_out):
    pixels = out.shape[1]
    loads = [pltpu.make_async_copy(p.at[pl.ds(pixels, pixels)], stage.at[k], sem_in.at[k]) for k, p in enumerate((p0, p1, p2, p3))]
    for c in loads:
        c.start()
    stores = [pltpu.make_async_copy(stage.at[k], out.at[k], sem_out.at[k]) for k in range(PARTS)]
    for load, store in zip(loads, stores):
        load.wait()
        store.start()
    for c in stores:
        c.wait()


def second_images_call(parts):
    rows, channels = parts[0].shape
    dma = pltpu.SemaphoreType.DMA
    return pl.pallas_call(
        second_images,
        out_shape=jax.ShapeDtypeStruct((PARTS, rows // 2, channels), BF),
        in_specs=[ANY] * PARTS,
        out_specs=ANY,
        scratch_shapes=[pltpu.VMEM((PARTS, rows // 2, channels), BF), dma((PARTS,)), dma((PARTS,))],
        name="second_images",
    )(*parts)


def collect_kernel(batches, place, p0, p1, p2, p3, other, out, stage, sem):
    core, z = place[1], place[2]
    parts = (p0, p1, p2, p3)
    pixels = p0.shape[0] // 2
    copies = []
    for k, part in enumerate(parts):
        copies.append(pltpu.make_async_copy(part.at[pl.ds(0, pixels)], stage.at[k, 0], sem.at[k, 0]))
        copies.append(pltpu.make_async_copy(other.at[k], stage.at[k, 1], sem.at[k, 1]))
    for c in copies:
        c.start()
    for k in range(PARTS):
        for j in range(2):
            copies[2 * k + j].wait()
            batch = 2 * (z ^ k) + (1 - core if j else core) - 1

            @pl.when(jnp.logical_and(batch >= 0, batch < batches))
            def _():
                out[batch] = stage[k, j].astype(out.dtype)


def collect_call(place, batches, parts, other, dtype):
    rows, channels = parts[0].shape
    return pl.pallas_call(
        functools.partial(collect_kernel, batches),
        out_shape=jax.ShapeDtypeStruct((batches, rows // 2, channels), dtype),
        in_specs=[SMEM] + [ANY] * (PARTS + 1),
        out_specs=VMEM,
        scratch_shapes=[pltpu.VMEM((PARTS, 2, rows // 2, channels), BF), pltpu.SemaphoreType.DMA((PARTS, 2))],
        name="collect_images",
        compiler_params=pltpu.CompilerParams(vmem_limit_bytes=VMEM_LIMIT),
    )(place, *parts, other)


SOURCES = (
    (("own", "own"), ("x1", "x1"), ("y1", "y1"), ("x2", "y2")),
    (("x1", "x1"), ("own", "own"), ("x2", "y2"), ("y1", "y1")),
    (("y1", "y1"), ("x2", "y2"), ("own", "own"), ("x1", "x1")),
    (("x2", "y2"), ("y1", "y1"), ("x1", "x1"), ("own", "own")),
)


def load_weights(place, arrived, low, high, w, sems):
    rank, core = place[0], place[1]
    for s in range(low, high):
        for r, sources in enumerate(SOURCES):

            @pl.when(rank == r)
            def _():
                for half, name in enumerate(sources[s]):
                    for other in range(2):
                        quarter = 2 * half + (1 - core if other else core)
                        if name == "own":
                            src = arrived["own"].at[pl.ds(pl.multiple_of(quarter * QROWS, 16), QROWS)]
                        else:
                            src = arrived[name][other].at[half if name in ("x1", "y1") else 0]
                        pltpu.make_async_copy(src, w.at[s - low, quarter], sems.at[s - low, 2 * half + other]).start()


def wait_weights(own, index, w, sems):
    for n in range(4):
        pltpu.make_async_copy(own.at[pl.ds(0, QROWS)], w.at[index, 0], sems.at[index, n]).wait()


def moments_of(v):
    mean = jnp.mean(v, axis=0, keepdims=True)
    centred = v - mean
    return mean, jnp.sum(centred * centred, axis=0, keepdims=True)


def combined(mean_ref, square_ref, rows):
    images = mean_ref.shape[0]
    means = [mean_ref[b] for b in range(images)]
    mean = sum(means) / images
    total = sum(square_ref[b] + rows * (means[b] - mean) ** 2 for b in range(images))
    return mean, lax.rsqrt(total / (images * rows) + EPS)


def halves(gain, bias, mean, inv):
    scale = 0.5 * gain * inv
    return scale, 0.5 * bias - mean * scale


def beside(v, column, by, side):
    if by < 0:
        return jnp.where(column == 0, 0.0, pltpu.roll(v, 1, 0))
    return jnp.where(column == side - 1, 0.0, pltpu.roll(v, v.shape[0] - 1, 0))


def three_columns(dst, b, x, column, side):
    pixels = x.shape[0]
    wide = x.astype(F32)
    for i, v in enumerate((beside(wide, column, -1, side).astype(BF), x, beside(wide, column, 1, side).astype(BF))):
        dst[i, b, 0:side] = jnp.zeros((side, CL), BF)
        dst[i, b, side : side + pixels] = v
        dst[i, b, side + pixels : 2 * side + pixels] = jnp.zeros((side, CL), BF)


def three_rows(x, side, images):
    pixels = x.shape[0] // images
    none = jnp.zeros((side, x.shape[1]), x.dtype)
    back, on = [], []
    for i in range(images):
        back += [none, x[i * pixels : (i + 1) * pixels - side]]
        on += [x[i * pixels + side : (i + 1) * pixels], none]
    return stack_rows(back), x, stack_rows(on)


def nine(src, b, side, flipped):
    pixels = side * side
    parts = []
    for dh in range(3):
        for dw in range(3):
            i, j = (2 - dh, 2 - dw) if flipped else (dh, dw)
            parts.append(src[j, b, i * side : i * side + pixels])
    return parts


def part_copies(whole, parts, sems):
    rows = whole.shape[0] // len(parts)
    return [pltpu.make_async_copy(whole.at[pl.ds(k * rows, rows)], ref, sems.at[k]) for k, ref in enumerate(parts)]


def needed(low, high):
    return sorted({name for sources in SOURCES for s in range(low, high) for name in sources[s]} - {"own"})


class Space:
    def __init__(self, **named):
        self.__dict__.update(named)


def geometry(side, images):
    pixels, modes = side * side, side * (side // 2 + 1)
    column = lambda: lax.broadcasted_iota(jnp.int32, (pixels, 1), 0) % side
    wide = lambda: lax.broadcasted_iota(jnp.int32, (IM * pixels, 1), 0) % side
    return Space(
        side=side,
        images=images,
        pixels=pixels,
        modes=modes,
        steps=images // IM,
        column=column,
        wide=wide,
        rows_of=lambda b: pl.ds(pl.multiple_of(b * (IM * pixels), IM * pixels), IM * pixels),
        modes_of=lambda b: pl.ds(pl.multiple_of(b * (IM * modes), IM * modes), IM * modes),
        image_rows=lambda b, i: pl.ds(pl.multiple_of(b * (IM * pixels) + i * pixels, pixels), pixels),
    )


def forward_section(geo, v, ws, a, o, odd):
    column, wide = geo.column(), geo.wide()
    side, pixels, modes = geo.side, geo.pixels, geo.modes
    gain, bias = read_norms(ws)

    def reduce_step(b, _):
        r = geo.rows_of(b)
        for i in range(IM):
            three_columns(v.xp, b * IM + i, a[geo.image_rows(b, i), 0:CL], column, side)
        x = dot_nt(a[r, CL:CH], read(ws, "reduce", 0, CS))
        v.q[r] = x
        v.mu1[b], v.sq1[b] = moments_of(x)
        return 0

    lax.fori_loop(0, geo.steps, reduce_step, 0, unroll=UN)
    mean1, inv1 = combined(v.mu1, v.sq1, IM * pixels)
    scale1, shift1 = halves(gain[:, :CS], bias[:, :CS], mean1, inv1)

    def spectral_step(b, _):
        r, rs = geo.rows_of(b), geo.modes_of(b)
        h = v.q[r] * scale1 + shift1
        v.h1[r] = h.astype(BF)
        act = silu_of_half(h)
        v.t[r] = act
        act = act.astype(BF)
        spec = [dot(v.mf[...], act[i * pixels : (i + 1) * pixels]).astype(BF) for i in range(IM)]
        real = stack_rows([x[:modes] for x in spec])
        imaginary = stack_rows([x[modes:] for x in spec])
        v.sv[0, rs] = real
        v.sv[1, rs] = imaginary
        mix = dot(real, read(ws, "spectral", 0, CS)) + dot(imaginary, read(ws, "spectral", CS, CS))
        v.f[rs] = mix
        v.mu2[b], v.sq2[b] = moments_of(mix)
        taps = stack_rows([stack_cols(nine(v.xp, b * IM + i, side, False)) for i in range(IM)])
        v.p[r] = dot(taps, conv_matrix(ws))
        return 0

    lax.fori_loop(0, geo.steps, spectral_step, 0, unroll=UN)
    mean2, inv2 = combined(v.mu2, v.sq2, IM * modes)
    scale2, shift2 = halves(gain[:, CS : CS + CG], bias[:, CS : CS + CG], mean2, inv2)

    def join_step(b, _):
        r, rs = geo.rows_of(b), geo.modes_of(b)
        h = v.f[rs] * scale2 + shift2
        v.h2[rs] = h.astype(BF)
        e = silu_of_half(h)
        er, ei = e[:, :CS].astype(BF), e[:, CS:].astype(BF)
        back = []
        for i in range(IM):
            m = slice(i * modes, (i + 1) * modes)
            back.append(dot(v.mi[...], stack_rows([er[m], ei[m]])))
        j = (v.t[r] + stack_rows(back)).astype(BF)
        v.jv[r] = j
        pre_global = v.p[r, CL:CH] + dot(j, read(ws, "expand", 0, CS))
        y = dot(stack_cols(three_rows(a[r, CL:CH], side, IM)), global_by_row(ws))
        pre_local = v.p[r, 0:CL] + beside(y[:, :CL], wide, -1, side) + y[:, CL : 2 * CL] + beside(y[:, 2 * CL :], wide, 1, side)
        v.p[r, 0:CL] = pre_local
        v.p[r, CL:CH] = pre_global
        ml, sl = moments_of(pre_local)
        mg, sg = moments_of(pre_global)
        v.mu3[b] = stack_cols([ml, mg])
        v.sq3[b] = stack_cols([sl, sg])
        return 0

    lax.fori_loop(0, geo.steps, join_step, 0, unroll=UN)
    mean3, inv3 = combined(v.mu3, v.sq3, IM * pixels)
    scale3, shift3 = halves(gain[:, CS + CG :], bias[:, CS + CG :], mean3, inv3)

    def end_step(b, _):
        r = geo.rows_of(b)
        h = v.p[r] * scale3 + shift3
        v.h3[r] = h.astype(BF)
        y = silu_of_half(h)
        if odd is not None:
            y = y + jnp.where(odd, o[r].astype(F32), 0.0)
        o[r] = y.astype(BF)
        return 0

    lax.fori_loop(0, geo.steps, end_step, 0, unroll=UN)
    return stack_cols([inv1, inv2, inv3])


def norm_terms(sums, gain, bias, factor, count):
    first, second = (jnp.sum(x, axis=0, keepdims=True) for x in sums)
    first = 0.5 * first
    second = (second - bias * first) / gain
    k1 = factor / count * (second * bias / gain - first)
    return first, second, (0.5 * factor, k1, 2.0 / count * factor * second / gain)


def part_sums(c, d, h):
    add = lambda x: jnp.sum(x.reshape(x.shape[0] // 8, 8, x.shape[1]), axis=0)
    return c[0] + add(d), c[1] + add(d * h)


def no_sums(c):
    return jnp.zeros((8, c), F32), jnp.zeros((8, c), F32)


def local_adjoint(geo, v, ws, dp, wide):
    back, same, on = three_rows(dp, geo.side, IM)
    y = dot_nt(stack_cols([on, same, back]), conv_by_column(ws))
    return beside(y[:, :CL], wide, 1, geo.side) + y[:, CL : 2 * CL] + beside(y[:, 2 * CL :], wide, -1, geo.side)


def global_adjoint(geo, v, ws, b):
    taps = stack_rows([stack_cols(nine(v.xp, b * IM + i, geo.side, True)) for i in range(IM)])
    return dot_nt(taps, global_matrix(ws))


def backward_section(geo, v, ws, inv, g, o, even, convs):
    column, wide = geo.column(), geo.wide()
    side, pixels, modes = geo.side, geo.pixels, geo.modes
    n1, n2 = float(geo.images * pixels), float(geo.images * modes)
    gain, bias = read_norms(ws)
    g1, g2, g3 = gain[:, :CS], gain[:, CS : CS + CG], gain[:, CS + CG :]
    b1, b2, b3 = bias[:, :CS], bias[:, CS : CS + CG], bias[:, CS + CG :]
    c1, c2, c3 = g1 * inv[:, :CS], g2 * inv[:, CS : CS + CG], g3 * inv[:, CS + CG :]

    def end_step(b, c):
        r = geo.rows_of(b)
        h = v.h3[r].astype(F32)
        d = g[r].astype(F32) * twice_slope(h)
        v.p[r] = d
        return part_sums(c, d, h)

    first3, second3, k3 = norm_terms(lax.fori_loop(0, geo.steps, end_step, no_sums(CH), unroll=UN), g3, b3, c3, n1)

    def join_step(b, c):
        r, rs = geo.rows_of(b), geo.modes_of(b)
        dp = (k3[0] * v.p[r] + (k3[1] - k3[2] * v.h3[r].astype(F32))).astype(BF)
        v.dpv[r] = dp
        djv = dot_nt(dp[:, CL:], read(ws, "expand", 0, CS))
        v.dj[r] = djv
        djv = djv.astype(BF)
        de = [dot(v.mit[...], djv[i * pixels : (i + 1) * pixels]) for i in range(IM)]
        de = stack_cols([stack_rows([x[:modes] for x in de]), stack_rows([x[modes:] for x in de])])
        h = v.h2[rs].astype(F32)
        d = de * twice_slope(h)
        v.du2[rs] = d
        if convs:
            for i in range(IM):
                three_columns(v.xp, b * IM + i, dp[i * pixels : (i + 1) * pixels, :CL], column, side)
            v.p[r, 0:CL] = local_adjoint(geo, v, ws, dp, wide)
        return part_sums(c, d, h)

    first2, second2, k2 = norm_terms(lax.fori_loop(0, geo.steps, join_step, no_sums(CG), unroll=UN), g2, b2, c2, n2)

    def spectral_step(b, c):
        r, rs = geo.rows_of(b), geo.modes_of(b)
        df = (k2[0] * v.du2[rs] + (k2[1] - k2[2] * v.h2[rs].astype(F32))).astype(BF)
        v.dfv[rs] = df
        ds = dot_nt(df, read(ws, "spectral", 0, CG))
        dr, di = ds[:, :CS].astype(BF), ds[:, CS:].astype(BF)
        back = []
        for i in range(IM):
            m = slice(i * modes, (i + 1) * modes)
            back.append(dot(v.mft[...], stack_rows([dr[m], di[m]])))
        dt = v.dj[r] + stack_rows(back)
        h = v.h1[r].astype(F32)
        d = dt * twice_slope(h)
        v.du1[r] = d
        if convs:
            v.p[r, CL:CH] = global_adjoint(geo, v, ws, b)
        return part_sums(c, d, h)

    first1, second1, k1 = norm_terms(lax.fori_loop(0, geo.steps, spectral_step, no_sums(CS), unroll=UN), g1, b1, c1, n1)

    def reduce_step(b, c):
        r = geo.rows_of(b)
        dq = (k1[0] * v.du1[r] + (k1[1] - k1[2] * v.h1[r].astype(F32))).astype(BF)
        v.dqv[r] = dq
        if convs:
            dx = stack_cols([v.p[r, 0:CL], v.p[r, CL:CH] + dot(dq, read(ws, "reduce", 0, CS))])
            if even is not None:
                dx = dx + jnp.where(even, o[r].astype(F32), 0.0)
            o[r] = dx.astype(BF)
        return c

    lax.fori_loop(0, geo.steps, reduce_step, 0, unroll=UN)
    return stack_cols([first1, first2, first3]), stack_cols([second1, second2, second3])


def weight_terms(geo, v, norms):
    column, side, pixels = geo.column(), geo.side, geo.pixels

    def tap_products(source, flipped, product):
        def columns(b, _):
            three_columns(v.xp, b, source[pl.ds(pl.multiple_of(b * pixels, pixels), pixels), 0:CL], column, side)
            return 0

        lax.fori_loop(0, geo.images, columns, 0)

        def one_row(dh, _):
            def gather(b, _):
                r = pl.ds(pl.multiple_of(b * pixels, pixels), pixels)
                first = pl.multiple_of((2 - dh if flipped else dh) * side, side)
                for dw in range(3):
                    v.taps[r, dw * CL : (dw + 1) * CL] = v.xp[2 - dw if flipped else dw, b, pl.ds(first, pixels)]
                return 0

            lax.fori_loop(0, geo.images, gather, 0)
            product(dh)
            return 0

        lax.fori_loop(0, 3, one_row, 0)

    def from_gradient(dh):
        u = dot_tn(v.ain[:, CL:], v.taps[...])
        for dw in range(3):
            put_terms(v.terms, "local", (dh * 3 + dw) * CH + CL, u[:, dw * CL : (dw + 1) * CL])

    def from_input(dh):
        u = dot_tn(v.taps[...], v.dpv[...])
        for dw in range(3):
            tap = slice(dw * CL, (dw + 1) * CL)
            put_terms(v.terms, "local", (dh * 3 + dw) * CH, u[tap, :CL])
            put_terms(v.terms, "cross", (dh * 3 + dw) * CL, u[tap, CL:])

    tap_products(v.dpv, True, from_gradient)
    tap_products(v.ain, False, from_input)
    put_terms(v.terms, "reduce", 0, dot_tn(v.dqv[...], v.ain[:, CL:]))
    put_terms(v.terms, "spectral", 0, dot_tn(v.sv[0], v.dfv[...]))
    put_terms(v.terms, "spectral", CS, dot_tn(v.sv[1], v.dfv[...]))
    put_terms(v.terms, "expand", 0, dot_tn(v.jv[...], v.dpv[:, CL:]))
    put_norm_terms(v.terms, norms)


def fill_parts(parts, whole, sems):
    rows = whole.shape[0] // len(parts)
    return [pltpu.make_async_copy(ref, whole.at[pl.ds(k * rows, rows)], sems.at[k]) for k, ref in enumerate(parts)]


def start_all(copies):
    for c in copies:
        c.start()


def wait_all(copies):
    for c in copies:
        c.wait()


DMA = pltpu.SemaphoreType.DMA


class Arguments:
    def __init__(self):
        self.ins, self.specs, self.outs, self.out_specs, self.scratch, self.aliases = [], [], [], [], [], {}
        self.names = [[], [], []]

    def take(self, name, value, spec):
        many = isinstance(value, (list, tuple))
        values = list(value) if many else [value]
        self.names[0].append((name, len(values) if many else None))
        at = len(self.ins)
        self.ins += values
        self.specs += [spec] * len(values)
        return at

    def give(self, name, shape, dtype, spec, count=None, over=None):
        self.names[1].append((name, count))
        for i in range(count or 1):
            if over is not None:
                self.aliases[over + i] = len(self.outs)
            self.outs.append(jax.ShapeDtypeStruct(shape, dtype))
            self.out_specs.append(spec)

    def hold(self, name, kind):
        self.names[2].append((name, None))
        self.scratch.append(kind)

    def unpack(self, refs):
        refs, space = list(refs), Space()
        for group in self.names:
            for name, count in group:
                setattr(space, name, refs.pop(0) if count is None else [refs.pop(0) for _ in range(count)])
        return space

    def call(self, body, name, flops, moved=20_000_000):
        results = pl.pallas_call(
            lambda *refs: body(self.unpack(refs)),
            out_shape=self.outs,
            in_specs=self.specs,
            out_specs=self.out_specs,
            scratch_shapes=self.scratch,
            input_output_aliases=self.aliases,
            name=name,
            cost_estimate=pl.CostEstimate(flops=int(flops), bytes_accessed=moved, transcendentals=0),
            compiler_params=pltpu.CompilerParams(vmem_limit_bytes=VMEM_LIMIT),
        )(*self.ins)
        results, space = list(results), Space()
        for out_name, count in self.names[1]:
            setattr(space, out_name, results.pop(0) if count is None else [results.pop(0) for _ in range(count)])
        return space


def take_weights(args, own, arrived, low, high):
    names = needed(low, high)
    args.take("own", own, ANY)
    for name in names:
        args.take("got_" + name, arrived[name], ANY)
    args.hold("w", pltpu.VMEM((high - low, QUARTERS, QROWS, 128), BF))
    args.hold("wsem", DMA((high - low, 4)))
    return names


def got_weights(v, names):
    return {"own": v.own, **{name: getattr(v, "got_" + name) for name in names}}


def hold_forward(args, n, m, images, pixels, side):
    args.hold("mu1", pltpu.VMEM((images // IM, 1, CS), F32))
    args.hold("sq1", pltpu.VMEM((images // IM, 1, CS), F32))
    args.hold("mu2", pltpu.VMEM((images // IM, 1, CG), F32))
    args.hold("sq2", pltpu.VMEM((images // IM, 1, CG), F32))
    args.hold("mu3", pltpu.VMEM((images // IM, 1, CH), F32))
    args.hold("sq3", pltpu.VMEM((images // IM, 1, CH), F32))


def hold_work(args, n, m, images, pixels, side):
    args.hold("xp", pltpu.VMEM((3, images, pixels + 2 * side, CL), BF))
    args.hold("q", pltpu.VMEM((n, CS), F32))
    args.hold("t", pltpu.VMEM((n, CS), F32))
    args.hold("f", pltpu.VMEM((m, CG), F32))
    args.hold("p", pltpu.VMEM((n, CH), F32))


def hold_terms(args, n, m):
    args.hold("dpv", pltpu.VMEM((n, CH), BF))
    args.hold("dqv", pltpu.VMEM((n, CS), BF))
    args.hold("dfv", pltpu.VMEM((m, CG), BF))
    args.hold("ain", pltpu.VMEM((n, CH), BF))
    args.hold("sv", pltpu.VMEM((2, m, CS), BF))
    args.hold("jv", pltpu.VMEM((n, CS), BF))
    args.hold("taps", pltpu.VMEM((n, 3 * CL), BF))
    args.hold("terms", pltpu.VMEM((QUARTERS * QROWS, 128), BF))


def first_call(place, inputs, own, arrived, mf, mi, after, side, images):
    geo = geometry(side, images)
    n, m = images * geo.pixels, images * geo.modes
    args = Arguments()
    args.take("place", place, SMEM)
    args.take("inputs", inputs, ANY)
    args.take("mf", mf, VMEM)
    args.take("mi", mi, VMEM)
    args.take("after", after, ANY)
    names = take_weights(args, own, arrived, 0, 1)
    args.give("out", (n, CH), BF, ANY)
    args.give("h1_out", (n, CS), BF, ANY)
    args.give("h2_out", (m, CG), BF, ANY)
    args.give("h3_out", (n, CH), BF, ANY)
    args.give("spec_out", (2, m, CS), BF, ANY)
    args.give("join_out", (n, CS), BF, ANY)
    args.give("inv_out", (1, NORMS), F32, VMEM)
    args.hold("a", pltpu.VMEM((n, CH), BF))
    args.hold("o", pltpu.VMEM((n, CH), BF))
    args.hold("h1", pltpu.VMEM((n, CS), BF))
    args.hold("h2", pltpu.VMEM((m, CG), BF))
    args.hold("h3", pltpu.VMEM((n, CH), BF))
    args.hold("sv", pltpu.VMEM((2, m, CS), BF))
    args.hold("jv", pltpu.VMEM((n, CS), BF))
    hold_work(args, n, m, images, geo.pixels, side)
    hold_forward(args, n, m, images, geo.pixels, side)
    args.hold("isem", DMA((PARTS,)))
    args.hold("osem", DMA((6,)))

    def body(v):
        loads = fill_parts(v.inputs, v.a, v.isem)
        start_all(loads)
        load_weights(v.place, got_weights(v, names), 0, 1, v.w, v.wsem)
        wait_all(loads)
        wait_weights(v.own, 0, v.w, v.wsem)
        v.inv_out[...] = forward_section(geo, v, v.w.at[0], v.a, v.o, None)
        pairs = (
            (v.o, v.out),
            (v.h1, v.h1_out),
            (v.h2, v.h2_out),
            (v.h3, v.h3_out),
            (v.sv, v.spec_out),
            (v.jv, v.join_out),
        )
        stores = [pltpu.make_async_copy(a, b, v.osem.at[i]) for i, (a, b) in enumerate(pairs)]
        start_all(stores)
        wait_all(stores)

    return args.call(body, "forward_0", 1, 1)


def middle_call(place, out0, inputs, seeds, own, arrived, tables, side, images):
    low, high = 1, 4
    geo = geometry(side, images)
    n, m, count = images * geo.pixels, images * geo.modes, high - low
    args = Arguments()
    args.take("place", place, SMEM)
    args.take("out0", out0, ANY)
    args.take("inputs", inputs, ANY)
    seeds_at = args.take("seeds", seeds, ANY)
    for name, table in zip(("mf", "mi", "mft", "mit"), tables):
        args.take(name, table, VMEM)
    names = take_weights(args, own, arrived, low, high)
    args.give("grads0", (n // PARTS, CH), BF, ANY, PARTS, seeds_at)
    args.give("grad1", (n, CH), BF, ANY)
    args.give("own_out", (n // PARTS, CH), BF, ANY, PARTS)
    args.give("own_grad", (n // PARTS, CH), BF, ANY, PARTS)
    args.give("own_terms", (QUARTERS * QROWS, 128), BF, ANY)
    args.hold("cur", pltpu.VMEM((2, n, CH), BF))
    args.hold("hats1", pltpu.VMEM((count, n, CS), BF))
    args.hold("hats2", pltpu.VMEM((count, m, CG), BF))
    args.hold("hats3", pltpu.VMEM((count, n, CH), BF))
    args.hold("inv", pltpu.VMEM((count, 1, NORMS), F32))
    args.hold("spec", pltpu.VMEM((2, m, CS), BF))
    args.hold("join", pltpu.VMEM((n, CS), BF))
    hold_work(args, n, m, images, geo.pixels, side)
    hold_forward(args, n, m, images, geo.pixels, side)
    hold_terms(args, n, m)
    args.hold("asem", DMA((1,)))
    args.hold("isem", DMA((PARTS,)))
    args.hold("gsem", DMA((PARTS,)))
    args.hold("outsem", DMA((PARTS,)))
    args.hold("gradsem", DMA((PARTS,)))
    args.hold("ksem", DMA((3,)))
    args.hold("tsem", DMA((1,)))
    args.hold("lastsem", DMA((PARTS + 1,)))

    def body(v):
        rank = v.place[0]
        loads = [pltpu.make_async_copy(v.out0, v.cur.at[1], v.asem.at[0])] + fill_parts(v.inputs, v.cur.at[0], v.isem)
        start_all(loads)
        load_weights(v.place, got_weights(v, names), low, high, v.w, v.wsem)
        wait_all(loads)
        rank0_out = part_copies(v.cur.at[1], v.own_out, v.outsem)

        @pl.when(rank == 0)
        def _():
            start_all(rank0_out)

        def at(index, **more):
            return Space(**{**v.__dict__, "h1": v.hats1.at[index], "h2": v.hats2.at[index], "h3": v.hats3.at[index], **more})

        def forward_one(index, _):
            s = index + low
            a, o = v.cur.at[s % 2], v.cur.at[(s + 1) % 2]
            mine = rank == s
            wait_weights(v.own, index, v.w, v.wsem)
            keep_in = pltpu.make_async_copy(a, v.ain, v.ksem.at[0])

            @pl.when(mine)
            def _():
                keep_in.start()

            v.inv[index] = forward_section(geo, at(index, sv=v.spec, jv=v.join), v.w.at[index], a, o, s % 2 == 1)

            @pl.when(mine)
            def _():
                keeps = [
                    pltpu.make_async_copy(v.spec, v.sv, v.ksem.at[1]),
                    pltpu.make_async_copy(v.join, v.jv, v.ksem.at[2]),
                    *part_copies(o, v.own_out, v.outsem),
                ]
                start_all(keeps)
                wait_all([keep_in, *keeps])

            @pl.when(jnp.logical_and(rank == 0, index == 0))
            def _():
                wait_all(rank0_out)

            return 0

        lax.fori_loop(0, count, forward_one, 0)
        loads = fill_parts(v.seeds, v.cur.at[(high - 1) % 2], v.gsem)
        start_all(loads)
        wait_all(loads)

        @pl.when(v.place[3] == 0)
        def _():
            v.cur[(high - 1) % 2] = jnp.zeros((n, CH), BF)

        def backward_one(step, _):
            index = count - 1 - step
            s = index + low
            g, o = v.cur.at[s % 2], v.cur.at[(s + 1) % 2]
            norms = backward_section(geo, at(index, du1=v.q, du2=v.f, dj=v.t), v.w.at[index], v.inv[index], g, o, s % 2 == 0, True)

            @pl.when(rank == s)
            def _():
                keeps = part_copies(o, v.own_grad, v.gradsem)
                start_all(keeps)
                weight_terms(geo, v, norms)
                keeps.append(pltpu.make_async_copy(v.terms, v.own_terms, v.tsem.at[0]))
                keeps[-1].start()
                wait_all(keeps)

            return 0

        lax.fori_loop(0, count, backward_one, 0)
        stores = part_copies(v.cur.at[0], v.grads0, v.lastsem)
        stores.append(pltpu.make_async_copy(v.cur.at[1], v.grad1, v.lastsem.at[PARTS]))
        start_all(stores)
        wait_all(stores)

    return args.call(body, "sections_1_3", images * 6e9)


def last_norms_call(place, first, grads0, inputs, own_terms, weights, arrived, tables, side, images):
    geo = geometry(side, images)
    n, m = images * geo.pixels, images * geo.modes
    args = Arguments()
    args.take("place", place, SMEM)
    args.take("grads0", grads0, ANY)
    args.take("inputs", inputs, ANY)
    args.take("h1_in", first.h1_out, ANY)
    args.take("h2_in", first.h2_out, ANY)
    args.take("h3_in", first.h3_out, ANY)
    args.take("spec_in", first.spec_out, ANY)
    args.take("join_in", first.join_out, ANY)
    args.take("inv", first.inv_out, VMEM)
    for name, table in zip(("mft", "mit"), tables):
        args.take(name, table, VMEM)
    terms_at = args.take("terms_in", own_terms, ANY)
    names = take_weights(args, weights, arrived, 0, 1)
    args.give("dp", (n, CH), BF, ANY)
    args.give("dq", (n, CS), BF, ANY)
    args.give("own_terms", (QUARTERS * QROWS, 128), BF, ANY, None, terms_at)
    args.hold("g", pltpu.VMEM((n, CH), BF))
    args.hold("h1", pltpu.VMEM((n, CS), BF))
    args.hold("h2", pltpu.VMEM((m, CG), BF))
    args.hold("h3", pltpu.VMEM((n, CH), BF))
    hold_work(args, n, m, images, geo.pixels, side)
    hold_terms(args, n, m)
    args.hold("gsem", DMA((PARTS,)))
    args.hold("isem", DMA((PARTS,)))
    args.hold("hsem", DMA((3,)))
    args.hold("ksem", DMA((2,)))
    args.hold("osem", DMA((3,)))

    def body(v):
        rank = v.place[0]
        loads = fill_parts(v.grads0, v.g, v.gsem)
        hats = ((v.h1_in, v.h1), (v.h2_in, v.h2), (v.h3_in, v.h3))
        loads += [pltpu.make_async_copy(a, b, v.hsem.at[i]) for i, (a, b) in enumerate(hats)]
        start_all(loads)
        load_weights(v.place, got_weights(v, names), 0, 1, v.w, v.wsem)
        kept = fill_parts(v.inputs, v.ain, v.isem)
        kept += [pltpu.make_async_copy(v.spec_in, v.sv, v.ksem.at[0]), pltpu.make_async_copy(v.join_in, v.jv, v.ksem.at[1])]

        @pl.when(rank == 0)
        def _():
            start_all(kept)

        wait_all(loads)
        wait_weights(v.own, 0, v.w, v.wsem)
        space = Space(**{**v.__dict__, "du1": v.q, "du2": v.f, "dj": v.t})
        norms = backward_section(geo, space, v.w.at[0], v.inv[...], v.g, None, None, False)
        stores = [pltpu.make_async_copy(v.dpv, v.dp, v.osem.at[0]), pltpu.make_async_copy(v.dqv, v.dq, v.osem.at[1])]
        start_all(stores)

        @pl.when(rank == 0)
        def _():
            wait_all(kept)
            weight_terms(geo, v, norms)
            out = pltpu.make_async_copy(v.terms, v.own_terms, v.osem.at[2])
            out.start()
            out.wait()

        wait_all(stores)

    return args.call(body, "backward_0_norms", images * 400e6)


def last_convs_call(place, back, grad1, own_grad, weights, arrived, side, images):
    geo = geometry(side, images)
    n, m = images * geo.pixels, images * geo.modes
    args = Arguments()
    args.take("place", place, SMEM)
    args.take("dp", back.dp, ANY)
    args.take("dq", back.dq, ANY)
    args.take("grad1", grad1, ANY)
    grad_at = args.take("grad_in", own_grad, ANY)
    names = take_weights(args, weights, arrived, 0, 1)
    args.give("own_grad", (n // PARTS, CH), BF, ANY, PARTS, grad_at)
    args.hold("dpv", pltpu.VMEM((n, CH), BF))
    args.hold("dqv", pltpu.VMEM((n, CS), BF))
    args.hold("o", pltpu.VMEM((n, CH), BF))
    args.hold("xp", pltpu.VMEM((3, images, geo.pixels + 2 * side, CL), BF))
    args.hold("lsem", DMA((3,)))
    args.hold("osem", DMA((PARTS,)))

    def body(v):
        @pl.when(v.place[0] == 0)
        def _():
            pairs = ((v.dp, v.dpv), (v.dq, v.dqv), (v.grad1, v.o))
            loads = [pltpu.make_async_copy(a, b, v.lsem.at[i]) for i, (a, b) in enumerate(pairs)]
            start_all(loads)
            load_weights(v.place, got_weights(v, names), 0, 1, v.w, v.wsem)
            wait_all(loads)
            wait_weights(v.own, 0, v.w, v.wsem)
            ws = v.w.at[0]
            column, wide = geo.column(), geo.wide()

            def step(b, _):
                r = geo.rows_of(b)
                dp = v.dpv[r]
                for i in range(IM):
                    three_columns(v.xp, b * IM + i, dp[i * geo.pixels : (i + 1) * geo.pixels, :CL], column, side)
                dxl = local_adjoint(geo, v, ws, dp, wide)
                dxg = global_adjoint(geo, v, ws, b) + dot(v.dqv[r], read(ws, "reduce", 0, CS))
                v.o[r] = (stack_cols([dxl, dxg]) + v.o[r].astype(F32)).astype(BF)
                return 0

            lax.fori_loop(0, geo.steps, step, 0)
            stores = part_copies(v.o, v.own_grad, v.osem)
            start_all(stores)
            wait_all(stores)

    return args.call(body, "backward_0_convs", images * 600e6)


def exchange_weights(send, after):
    def over(bit, x):
        return lax.ppermute(x, "pipe", [(i ^ bit, i) for i in range(4)])

    def swap(x):
        return lax.ppermute(x, "dp", [(i, i ^ 1) for i in range(lax.axis_size("dp"))])

    got = {"x1": over(1, send), "y1": over(2, send)}
    over_x, over_y = relay_call(got["y1"], got["x1"], after)
    got["x2"], got["y2"] = over(1, over_x), over(2, over_y)
    return {name: (x, swap(x)) for name, x in got.items()}


def local_device(images_in, conv_local, conv_cross, reduce_weight, spectral_weight, expand_weight, norm_gain, norm_bias, cotangent, hole_mask):
    batches, _, side, _, channels = images_in.shape
    pixels = side * side
    dp_size = lax.axis_size("dp")
    dp_rank = lax.axis_index("dp")
    core = dp_rank % 2
    holders = range(1, 1 + batches)
    holds = jnp.logical_and(dp_rank >= holders.start, dp_rank < holders.stop)
    place = jnp.stack([lax.axis_index("pipe"), core, dp_rank // 2, holds]).astype(jnp.int32)
    table_to, table_from = dft_np(side)
    mf, mi = jnp.asarray(table_to, BF), jnp.asarray(table_from, BF)
    mft, mit = jnp.asarray(table_to.T, BF), jnp.asarray(table_from.T, BF)

    def swap(x):
        return lax.ppermute(x, "dp", [(i, i ^ 1) for i in range(dp_size)])

    def along_z(k, x, pairs):
        return lax.ppermute(x, "dp", [(i, j) for i, j in pairs if i ^ j == 2 * k])

    to_holders = [(i, j) for i in range(dp_size) for j in holders]
    from_holders = [(j, i) for i, j in to_holders]

    def to_batches(x, through=(), after=()):
        other = swap(lax.dynamic_index_in_dim(x.reshape(batches // 2, 2, pixels, channels), core, 1, keepdims=False))
        parts = spread_call(place, x, other, through, after)
        through = parts[PARTS:]
        parts = list(parts[:1]) + [along_z(k, parts[k], to_holders) for k in range(1, PARTS)]
        return [part.reshape(2 * pixels, channels) for part in parts], *through

    def to_images(parts, dtype):
        parts = list(parts[:1]) + [along_z(k, parts[k], from_holders) for k in range(1, PARTS)]
        other = swap(second_images_call(parts))
        return collect_call(place, batches, parts, other, dtype).reshape(1, batches, 1, side, side, channels)

    own, send = pack_call(
        place,
        conv_local.reshape(-1, CL),
        conv_cross.reshape(-1, CG),
        reduce_weight[0].T,
        spectral_weight[0],
        expand_weight[0],
        norm_gain,
        norm_bias,
    )
    inputs, send = to_batches(images_in.reshape(batches, pixels, channels), (send,))
    hole_float = hole_mask.astype(F32)
    hole_counts = jnp.sum(hole_float, axis=(2, 3), keepdims=True)
    weighting = 0.25 + hole_float * pixels / (hole_counts + pixels / 8.0)
    seed = (cotangent.astype(F32) * weighting[..., None]).astype(BF)

    seeds, *_ = to_batches(seed.reshape(batches, pixels, channels))
    arrived = exchange_weights(send, seeds[:1])
    first = first_call(place, inputs, own, arrived, mf, mi, seeds[1:3], side, dp_size)
    middle = middle_call(place, first.out, inputs, seeds, own, arrived, (mf, mi, mft, mit), side, dp_size)
    activations = to_images(middle.own_out, BF)
    back = last_norms_call(
        place, first, middle.grads0, inputs, middle.own_terms, own, arrived, (mft, mit), side, dp_size
    )
    own_grad = last_convs_call(place, back, middle.grad1, middle.own_grad, own, arrived, side, dp_size).own_grad
    own_terms = back.own_terms
    input_grads = to_images(own_grad, F32)
    local, cross, reduce_w, spectral, expand, gain, bias = unpack_call(
        lax.psum(own_terms, "dp"), (activations, input_grads)
    )
    return (
        activations,
        input_grads,
        local.reshape(conv_local.shape),
        cross.reshape(conv_cross.shape),
        reduce_w.T[None],
        spectral[None],
        expand[None],
        gain,
        bias,
    )


def solution(mesh):
    placed = (
        P(None, "dp", None, None, None),
        P("pipe", None, None, None, None),
        P("pipe", None, None, None, None),
        P("pipe", None, None),
        P("pipe", None, None),
        P("pipe", None, None),
        P("pipe", None),
        P("pipe", None),
        P(None, "dp", None, None, None),
        P(None, "dp", None, None),
    )

    def on_device(images_in, *rest):
        dp_size = lax.axis_size("dp")
        fits = images_in.shape[1] == 1 and dp_size == 8 and images_in.shape[0] == dp_size - 2 and lax.axis_size("pipe") == 4
        return (local_device if fits else general_device)(images_in, *rest)

    return jax.shard_map(
        on_device,
        mesh=mesh,
        in_specs=placed,
        out_specs=(
            P("pipe", None, "dp", None, None, None),
            P("pipe", None, "dp", None, None, None),
            P("pipe", None, None, None, None),
            P("pipe", None, None, None, None),
            P("pipe", None, None),
            P("pipe", None, None),
            P("pipe", None, None),
            P("pipe", None),
            P("pipe", None),
        ),
        check_vma=False,
    )
```

```python
import functools
import math

import jax
import jax.numpy as jnp
import numpy as np
from jax import lax
from jax.experimental import pallas as pl
from jax.experimental.pallas import tpu as pltpu
from jax.sharding import PartitionSpec as P

CL = 128
CG = 384
CS = 192
CH = 512
NORMS = 1088
F32 = jnp.float32
BF = jnp.bfloat16
IM = 4
UN = 2


EPS = 1e-05
HIGH = lax.Precision.HIGHEST


def from_behind(x, axis, by):
    length = lax.axis_size(axis)
    pairs = [(i, i + by) for i in range(length) if 0 <= i + by < length]
    return lax.ppermute(x, axis, pairs)


def smooth(values):
    return values * jax.nn.sigmoid(values)


def smooth_slope(values):
    logistic = jax.nn.sigmoid(values)
    return logistic * (1.0 + values * (1.0 - logistic))


def patches(values):
    height, breadth = (values.shape[1], values.shape[2])
    padded = jnp.pad(values, ((0, 0), (1, 1), (1, 1), (0, 0)))
    return jnp.concatenate(
        [
            padded[:, row_off : row_off + height, col_off : col_off + breadth]
            for row_off in range(3)
            for col_off in range(3)
        ],
        axis=-1,
    )


def conv_apply(values, kernel):
    flat_kernel = kernel.reshape(-1, kernel.shape[-1])
    return jnp.einsum(
        "bhwk,kd->bhwd", patches(values), flat_kernel, preferred_element_type=jnp.float32
    )


def conv_weight_grad(values, grad_low, kernel_shape):
    return jnp.einsum(
        "bhwk,bhwd->kd", patches(values), grad_low, preferred_element_type=jnp.float32
    ).reshape(kernel_shape)


def conv_input_grad(grad_low, kernel):
    flipped = jnp.flip(kernel, (0, 1)).transpose(0, 1, 3, 2)
    return conv_apply(grad_low, flipped)


def dft_tables(side_len):
    frequencies = side_len // 2 + 1
    spatial = jnp.arange(side_len, dtype=jnp.int32)
    spectral = jnp.arange(frequencies, dtype=jnp.int32)
    angle_cols = (spatial[:, None] * spectral[None, :] % side_len).astype(jnp.float32) * (
        2.0 * math.pi / side_len
    )
    angle_rows = (spatial[:, None] * spatial[None, :] % side_len).astype(jnp.float32) * (
        2.0 * math.pi / side_len
    )
    fold_factor = jnp.where((spectral == 0) | (2 * spectral == side_len), 1.0, 2.0).astype(
        jnp.float32
    )
    return (
        jnp.cos(angle_cols),
        jnp.sin(angle_cols),
        jnp.cos(angle_rows),
        jnp.sin(angle_rows),
        fold_factor,
    )


def to_spectrum(field_in, tables):
    cosine_cols, sine_cols, cosine_rows, sine_rows, _ = tables
    scaling = 1.0 / math.sqrt(field_in.shape[1] * field_in.shape[2])
    real_along = jnp.einsum("bhwc,wk->bhkc", field_in, cosine_cols, precision=HIGH)
    imaginary_along = -jnp.einsum("bhwc,wk->bhkc", field_in, sine_cols, precision=HIGH)
    real_part = jnp.einsum("bhkc,gh->bgkc", real_along, cosine_rows, precision=HIGH) + jnp.einsum(
        "bhkc,gh->bgkc", imaginary_along, sine_rows, precision=HIGH
    )
    imaginary_part = jnp.einsum(
        "bhkc,gh->bgkc", imaginary_along, cosine_rows, precision=HIGH
    ) - jnp.einsum("bhkc,gh->bgkc", real_along, sine_rows, precision=HIGH)
    return jnp.concatenate([real_part, imaginary_part], axis=-1) * scaling


def from_spectrum(field_in, tables):
    cosine_cols, sine_cols, cosine_rows, sine_rows, fold_factor = tables
    scaling = 1.0 / math.sqrt(field_in.shape[1] * cosine_cols.shape[0])
    half_width = field_in.shape[-1] // 2
    real_in = field_in[..., :half_width]
    imaginary_in = field_in[..., half_width:]
    real_rows = jnp.einsum("bgkc,gh->bhkc", real_in, cosine_rows, precision=HIGH) - jnp.einsum(
        "bgkc,gh->bhkc", imaginary_in, sine_rows, precision=HIGH
    )
    imaginary_rows = jnp.einsum(
        "bgkc,gh->bhkc", imaginary_in, cosine_rows, precision=HIGH
    ) + jnp.einsum("bgkc,gh->bhkc", real_in, sine_rows, precision=HIGH)
    folding = fold_factor[None, None, :, None]
    field_out = jnp.einsum(
        "bhkc,wk->bhwc", real_rows * folding, cosine_cols, precision=HIGH
    ) - jnp.einsum("bhkc,wk->bhwc", imaginary_rows * folding, sine_cols, precision=HIGH)
    return field_out * scaling


def moments(values):
    sum_axes = tuple(range(values.ndim - 1))
    count_all = math.prod(values.shape[:-1]) * lax.axis_size("dp")
    average = lax.psum(jnp.sum(values, axis=sum_axes), "dp") / count_all
    centred = values - average
    spread = lax.psum(jnp.sum(centred * centred, axis=sum_axes), "dp") / count_all
    return (average, lax.rsqrt(spread + EPS))


def norm_back(grad_out, act_values, hat_values, gain_slice, inv_std):
    sum_axes = tuple(range(act_values.ndim - 1))
    count_all = math.prod(act_values.shape[:-1]) * lax.axis_size("dp")
    grad_act = grad_out * smooth_slope(act_values)
    sum_act, sum_hat = lax.psum(
        (jnp.sum(grad_act, axis=sum_axes), jnp.sum(grad_act * hat_values, axis=sum_axes)), "dp"
    )
    grad_values = gain_slice * inv_std * (grad_act - (sum_act + hat_values * sum_hat) / count_all)
    return (grad_values, sum_hat, sum_act)


def section_compute(inputs, weights, norm_gains, norm_biases, measure, tables):
    local_kernel, cross_kernel, reduce_matrix, spectral_matrix, expand_matrix = weights

    def normalize(values, offset):
        extent = values.shape[-1]
        average, inv_std = measure(values, offset)
        hat_values = (values - average) * inv_std
        return (
            hat_values,
            norm_gains[offset : offset + extent] * hat_values
            + norm_biases[offset : offset + extent],
        )

    local_part = inputs[..., :CL]
    global_part = inputs[..., CL:]
    pre_local = conv_apply(inputs, local_kernel)
    reduced = jnp.einsum(
        "bhwc,cd->bhwd", global_part, reduce_matrix, preferred_element_type=jnp.float32
    )
    hat_one, act_one = normalize(reduced, 0)
    activated = smooth(act_one)
    spec_low = to_spectrum(activated, tables).astype(jnp.bfloat16)
    spectral_mix = jnp.einsum(
        "bhkc,cd->bhkd", spec_low, spectral_matrix, preferred_element_type=jnp.float32
    )
    hat_two, act_two = normalize(spectral_mix, CS)
    joined = (activated + from_spectrum(smooth(act_two), tables)).astype(jnp.bfloat16)
    pre_global = conv_apply(local_part, cross_kernel) + jnp.einsum(
        "bhwc,cd->bhwd", joined, expand_matrix, preferred_element_type=jnp.float32
    )
    hat_end, act_end = normalize(jnp.concatenate([pre_local, pre_global], axis=-1), CS + CG)
    return (
        smooth(act_end),
        (hat_one, act_one, activated, spec_low, hat_two, act_two, joined, hat_end, act_end),
    )


def section_backward(inputs, weights, norm_gains, inv_std, saved, grad_result, tables):
    local_kernel, cross_kernel, reduce_matrix, spectral_matrix, expand_matrix = weights
    hat_one, act_one, activated, spec_low, hat_two, act_two, joined, hat_end, act_end = saved
    local_part = inputs[..., :CL]
    global_part = inputs[..., CL:]
    grad_end, gain_end, bias_end = norm_back(
        grad_result, act_end, hat_end, norm_gains[CS + CG :], inv_std[CS + CG :]
    )
    grad_end_low = grad_end.astype(jnp.bfloat16)
    grad_pre_local = grad_end_low[..., :CL]
    grad_pre_global = grad_end_low[..., CL:]
    grad_cross = conv_weight_grad(local_part, grad_pre_global, cross_kernel.shape)
    grad_expand = jnp.einsum(
        "bhwc,bhwd->cd", joined, grad_pre_global, preferred_element_type=jnp.float32
    )
    grad_joined = jnp.einsum(
        "bhwd,cd->bhwc", grad_pre_global, expand_matrix, preferred_element_type=jnp.float32
    )
    _, inverse_pull = jax.vjp(
        lambda field_in: from_spectrum(field_in, tables), jnp.zeros(act_two.shape, jnp.float32)
    )
    (grad_after,) = inverse_pull(grad_joined)
    grad_mix, gain_two, bias_two = norm_back(
        grad_after, act_two, hat_two, norm_gains[CS : CS + CG], inv_std[CS : CS + CG]
    )
    grad_mix_low = grad_mix.astype(jnp.bfloat16)
    grad_spectral = jnp.einsum(
        "bhkc,bhkd->cd", spec_low, grad_mix_low, preferred_element_type=jnp.float32
    )
    grad_spec = jnp.einsum(
        "bhkd,cd->bhkc", grad_mix_low, spectral_matrix, preferred_element_type=jnp.float32
    )
    _, forward_pull = jax.vjp(lambda field_in: to_spectrum(field_in, tables), activated)
    (grad_activated,) = forward_pull(grad_spec)
    grad_reduced, gain_one, bias_one = norm_back(
        grad_activated + grad_joined, act_one, hat_one, norm_gains[:CS], inv_std[:CS]
    )
    grad_reduced_low = grad_reduced.astype(jnp.bfloat16)
    grad_reduce = jnp.einsum(
        "bhwc,bhwd->cd", global_part, grad_reduced_low, preferred_element_type=jnp.float32
    )
    grad_global = jnp.einsum(
        "bhwd,cd->bhwc", grad_reduced_low, reduce_matrix, preferred_element_type=jnp.float32
    )
    grad_local = conv_input_grad(grad_pre_global, cross_kernel)
    grad_local_kernel = conv_weight_grad(inputs, grad_pre_local, local_kernel.shape)
    grad_inputs = conv_input_grad(grad_pre_local, local_kernel) + jnp.concatenate(
        [grad_local, grad_global], axis=-1
    )
    gain_terms = jnp.concatenate([gain_one, gain_two, gain_end])
    bias_terms = jnp.concatenate([bias_one, bias_two, bias_end])
    return (
        grad_inputs,
        (grad_local_kernel, grad_cross, grad_reduce, grad_spectral, grad_expand),
        gain_terms,
        bias_terms,
    )


def store(buffer, value, slot_index, active):
    previous = lax.dynamic_index_in_dim(buffer, slot_index, 0, keepdims=False)
    return lax.dynamic_update_index_in_dim(
        buffer, jnp.where(active, value, previous), slot_index, 0
    )


def general_device(
    images_in,
    conv_local,
    conv_cross,
    reduce_weight,
    spectral_weight,
    expand_weight,
    norm_gain,
    norm_bias,
    cotangent,
    hole_mask,
):
    section_count = lax.axis_size("pipe")
    section_rank = lax.axis_index("pipe")
    batches = images_in.shape[0]
    step_count = batches + section_count - 1
    odd_section = section_rank % 2 == 1
    last_section = section_rank == section_count - 1
    weights = (conv_local[0], conv_cross[0], reduce_weight[0], spectral_weight[0], expand_weight[0])
    norm_gains = norm_gain[0]
    norm_biases = norm_bias[0]
    tables = dft_tables(images_in.shape[2])
    blank = jnp.zeros(images_in.shape[1:], jnp.bfloat16)

    def forward_step(carried, step_index):
        recv_act, recv_res, kept_inputs, kept_stats, kept_outputs = carried
        batch_index = step_index - section_rank
        active = (batch_index >= 0) & (batch_index < batches)
        slot_index = jnp.clip(batch_index, 0, batches - 1)
        fresh_image = lax.dynamic_index_in_dim(images_in, slot_index, 0, keepdims=False)
        inputs = jnp.where(section_rank == 0, fresh_image, recv_act)
        recorded = []

        def measure(values, offset):
            average, inv_std = moments(values)
            recorded.append((average, inv_std))
            return (average, inv_std)

        result, _ = section_compute(inputs, weights, norm_gains, norm_biases, measure, tables)
        summed = result + jnp.where(odd_section, recv_res.astype(jnp.float32), 0.0)
        outgoing = summed.astype(jnp.bfloat16)
        residual_out = jnp.where(odd_section, outgoing, inputs)
        next_act, next_res = from_behind((outgoing, residual_out), "pipe", 1)
        statistics = jnp.stack(
            [
                jnp.concatenate([entry_pair[0] for entry_pair in recorded]),
                jnp.concatenate([entry_pair[1] for entry_pair in recorded]),
            ]
        )
        kept_inputs = store(kept_inputs, inputs, slot_index, active)
        kept_stats = store(kept_stats, statistics, slot_index, active)
        kept_outputs = store(kept_outputs, outgoing, slot_index, active)
        return ((next_act, next_res, kept_inputs, kept_stats, kept_outputs), None)

    forward_init = (
        blank,
        blank,
        jnp.zeros(images_in.shape, jnp.bfloat16),
        jnp.zeros((batches, 2, NORMS), jnp.float32),
        jnp.zeros(images_in.shape, jnp.bfloat16),
    )
    forward_state = lax.scan(forward_step, forward_init, jnp.arange(step_count))[0]
    kept_inputs, kept_stats, kept_outputs = (forward_state[2], forward_state[3], forward_state[4])
    pixels = images_in.shape[2] * images_in.shape[3]
    hole_float = hole_mask.astype(jnp.float32)
    hole_counts = jnp.sum(hole_float, axis=(2, 3), keepdims=True)
    weighting = 0.25 + hole_float * pixels / (hole_counts + pixels / 8.0)

    def backward_step(carried, step_index):
        recv_grad, recv_res, grad_store, weight_sums, gain_sum, bias_sum = carried
        batch_index = step_index - (section_count - 1 - section_rank)
        active = (batch_index >= 0) & (batch_index < batches)
        slot_index = jnp.clip(batch_index, 0, batches - 1)
        cotan_slot = lax.dynamic_index_in_dim(cotangent, slot_index, 0, keepdims=False).astype(
            jnp.float32
        )
        weight_slot = lax.dynamic_index_in_dim(weighting, slot_index, 0, keepdims=False)
        seed_grad = (cotan_slot * weight_slot[..., None]).astype(jnp.bfloat16)
        incoming = jnp.where(last_section, seed_grad, recv_grad)
        inputs = lax.dynamic_index_in_dim(kept_inputs, slot_index, 0, keepdims=False)
        statistics = lax.dynamic_index_in_dim(kept_stats, slot_index, 0, keepdims=False)

        def measure(values, offset):
            extent = values.shape[-1]
            return (
                statistics[0, offset : offset + extent],
                statistics[1, offset : offset + extent],
            )

        _, saved = section_compute(inputs, weights, norm_gains, norm_biases, measure, tables)
        grad_inputs, weight_terms, gain_terms, bias_terms = section_backward(
            inputs, weights, norm_gains, statistics[1], saved, incoming.astype(jnp.float32), tables
        )
        grad_total = grad_inputs + jnp.where(odd_section, 0.0, recv_res.astype(jnp.float32))
        outgoing = grad_total.astype(jnp.bfloat16)
        residual_out = jnp.where(odd_section, incoming, outgoing)
        next_grad, next_res = from_behind((outgoing, residual_out), "pipe", -1)
        weight_sums = tuple(
            (
                running + jnp.where(active, addend, 0.0)
                for running, addend in zip(weight_sums, weight_terms)
            )
        )
        gain_sum = gain_sum + jnp.where(active, gain_terms, 0.0)
        bias_sum = bias_sum + jnp.where(active, bias_terms, 0.0)
        grad_store = store(grad_store, grad_total, slot_index, active)
        return ((next_grad, next_res, grad_store, weight_sums, gain_sum, bias_sum), None)

    zero_weights = tuple((jnp.zeros(entry_weight.shape, jnp.float32) for entry_weight in weights))
    backward_init = (
        blank,
        blank,
        jnp.zeros(images_in.shape, jnp.float32),
        zero_weights,
        jnp.zeros((NORMS,), jnp.float32),
        jnp.zeros((NORMS,), jnp.float32),
    )
    state_end = lax.scan(backward_step, backward_init, jnp.arange(0, 0 + step_count))[0]
    sum_local, sum_cross, sum_reduce, sum_spectral, sum_expand = state_end[3]
    totals = lax.psum((sum_local, sum_cross, sum_reduce, sum_spectral, sum_expand), "dp")
    return (
        kept_outputs[None],
        state_end[2][None],
        totals[0][None],
        totals[1][None],
        totals[2][None],
        totals[3][None],
        totals[4][None],
        state_end[4][None],
        state_end[5][None],
    )


PARTS = 4
ANY = pl.BlockSpec(memory_space=pl.ANY)
VMEM = pl.BlockSpec(memory_space=pltpu.VMEM)
SMEM = pl.BlockSpec(memory_space=pltpu.SMEM)
VMEM_LIMIT = 63 * 2**20


def dft_np(side):
    spatial = np.arange(side)
    spectral = np.arange(side // 2 + 1)
    turns = spatial[:, None, None, None] * spatial[None, None, :, None] + spectral[None, :, None, None] * spatial[None, None, None, :]
    angle = (turns % side).reshape(side * spectral.size, side * side) * (2.0 * np.pi / side)
    fold = np.broadcast_to(np.where((spectral == 0) | (2 * spectral == side), 1.0, 2.0), (side, spectral.size)).reshape(-1, 1)
    forward = np.concatenate([np.cos(angle), -np.sin(angle)]) / side
    inverse = np.concatenate([np.cos(angle) * fold, -np.sin(angle) * fold]).T / side
    return forward, inverse


def dot(a, b):
    return lax.dot_general(a, b, (((1,), (0,)), ((), ())), preferred_element_type=F32)


def dot_nt(a, b):
    return lax.dot_general(a, b, (((1,), (1,)), ((), ())), preferred_element_type=F32)


def dot_tn(a, b):
    return lax.dot_general(a, b, (((0,), (0,)), ((), ())), preferred_element_type=F32)


def silu_of_half(h):
    return h + h * jnp.tanh(h)


def twice_slope(h):
    t = jnp.tanh(h)
    return (1.0 + t) * (1.0 + h * (1.0 - t))


QUARTERS, QROWS = 4, 2640
LAYOUT = {
    "local": (0, 1152, 1),
    "cross": (1152, 288, 3),
    "reduce": (2016, 48, 3),
    "spectral": (2160, 96, 3),
    "expand": (2448, 48, 3),
    "norms": (2592, 16, 3),
}


def pieces(name, start, count, block=0):
    base, rows, _ = LAYOUT[name]
    found = []
    while count:
        quarter, offset = divmod(start, rows)
        take = min(count, rows - offset)
        found.append((quarter, base + block * rows + offset, take))
        start, count = start + take, count - take
    return found


def stack_rows(parts):
    return parts[0] if len(parts) == 1 else jnp.concatenate(parts, axis=0)


def stack_cols(parts):
    return parts[0] if len(parts) == 1 else jnp.concatenate(parts, axis=1)


def read(w, name, start, count):
    blocks = LAYOUT[name][2]
    return stack_cols([stack_rows([w[q, r : r + n] for q, r, n in pieces(name, start, count, j)]) for j in range(blocks)])


def write(w, name, start, value):
    for j in range(LAYOUT[name][2]):
        done = 0
        for q, r, n in pieces(name, start, value.shape[0], j):
            w[q, r : r + n] = value[done : done + n, j * 128 : (j + 1) * 128].astype(w.dtype)
            done += n


def norm_rows(w):
    base = LAYOUT["norms"][0]
    return stack_cols([w[j // 3, base + 16 * (j % 3) : base + 16 * (j % 3) + 16] for j in range(9)]).astype(F32)[:, :NORMS]


def read_norms(w):
    rows = norm_rows(w)
    return rows[0:1] + rows[1:2], rows[2:3] + rows[3:4]


def norm_block(vectors):
    rows = stack_rows([*vectors, jnp.zeros((16 - len(vectors), NORMS), F32)])
    return stack_cols([rows, jnp.zeros((16, 12 * 128 - NORMS), F32)]).astype(BF)


def write_norms(w, vectors):
    base = LAYOUT["norms"][0]
    rows = norm_block(vectors)
    for j in range(12):
        w[j // 3, base + 16 * (j % 3) : base + 16 * (j % 3) + 16] = rows[:, j * 128 : (j + 1) * 128]


TERMS = {
    "local": (0, 9 * CH, 1),
    "cross": (9 * CH, 9 * CL, 3),
    "reduce": (9 * (CH + CG), CS, 3),
    "spectral": (9 * (CH + CG) + 3 * CS, CG, 3),
    "expand": (9 * (CH + CG) + 3 * (CS + CG), CS, 3),
    "norms": (9 * (CH + CG) + 3 * (2 * CS + CG), 16, 12),
}


def put_terms(w, name, start, value):
    base, rows, blocks = TERMS[name]
    count = value.shape[0]
    for j in range(blocks):
        first = base + j * rows + start
        w[pl.ds(first if isinstance(first, int) else pl.multiple_of(first, 128), count)] = value[:, j * 128 : (j + 1) * 128].astype(BF)


def put_norm_terms(w, vectors):
    base = TERMS["norms"][0]
    rows = norm_block(vectors)
    for j in range(12):
        w[base + 16 * j : base + 16 * (j + 1)] = rows[:, j * 128 : (j + 1) * 128]


def get_terms(w, name, columns):
    base, rows, blocks = TERMS[name]
    return stack_cols([w[base + j * rows : base + (j + 1) * rows] for j in range(blocks)]).astype(F32)[:, :columns]


def conv_matrix(w):
    return stack_rows([stack_cols([read(w, "local", k * CH, CL), read(w, "cross", k * CL, CL)]) for k in range(9)])


def global_matrix(w):
    return stack_cols([read(w, "local", k * CH + CL, CG) for k in range(9)])


def global_by_row(w):
    return stack_rows([stack_cols([read(w, "local", (dh * 3 + dw) * CH + CL, CG) for dw in range(3)]) for dh in range(3)])


def conv_by_column(w):
    return stack_rows(
        [
            stack_cols([part for k in (dw, 3 + dw, 6 + dw) for part in (read(w, "local", k * CH, CL), read(w, "cross", k * CL, CL))])
            for dw in range(3)
        ]
    )


def pack_kernel(place, local, cross, reduce_w, spectral, expand, gains, biases, own, send, packed, sem):
    packed_rows = lambda name, value: write(packed, name, 0, value)
    packed_rows("local", local[...])
    packed_rows("cross", cross[...])
    packed_rows("reduce", reduce_w[...])
    packed_rows("spectral", spectral[...])
    packed_rows("expand", expand[...])
    halves = []
    for values in (gains[...], biases[...]):
        high = values.astype(BF)
        halves += [high.astype(F32), values - high.astype(F32)]
    write_norms(packed, halves)
    core = place[1]
    copies = [pltpu.make_async_copy(packed.at[2 * half + core], send.at[half], sem.at[half]) for half in range(2)]
    copies += [pltpu.make_async_copy(packed.at[q], own.at[pl.ds(q * QROWS, QROWS)], sem.at[2 + q]) for q in range(QUARTERS)]
    for c in copies:
        c.start()
    for c in copies:
        c.wait()


def pack_call(place, *weights):
    shape = jax.ShapeDtypeStruct
    return pl.pallas_call(
        pack_kernel,
        out_shape=[shape((QUARTERS * QROWS, 128), BF), shape((2, QROWS, 128), BF)],
        in_specs=[SMEM] + [VMEM] * 7,
        out_specs=[ANY] * 2,
        scratch_shapes=[pltpu.VMEM((QUARTERS, QROWS, 128), BF), pltpu.SemaphoreType.DMA((2 + QUARTERS,))],
        name="pack_weights",
        compiler_params=pltpu.CompilerParams(vmem_limit_bytes=VMEM_LIMIT),
    )(place, *weights)


def relay_kernel(skip, *refs):
    y1, x1 = refs[:2]
    over_x, over_y, stage, sem_in, sem_out = refs[2 + skip :]
    loads = [pltpu.make_async_copy(y1.at[0], stage.at[0], sem_in.at[0]), pltpu.make_async_copy(x1.at[1], stage.at[1], sem_in.at[1])]
    stores = [pltpu.make_async_copy(stage.at[i], ref.at[0], sem_out.at[i]) for i, ref in enumerate((over_x, over_y))]
    for c in loads:
        c.start()
    for load, store in zip(loads, stores):
        load.wait()
        store.start()
    for c in stores:
        c.wait()


def relay_call(y1, x1, after):
    dma = pltpu.SemaphoreType.DMA
    return pl.pallas_call(
        functools.partial(relay_kernel, len(after)),
        out_shape=[jax.ShapeDtypeStruct((1, QROWS, 128), BF)] * 2,
        in_specs=[ANY] * (2 + len(after)),
        out_specs=[ANY] * 2,
        scratch_shapes=[pltpu.VMEM((2, QROWS, 128), BF), dma((2,)), dma((2,))],
        name="relay_weights",
    )(y1, x1, *after)


def unpack_kernel(packed, *refs):
    local, cross, reduce_w, spectral, expand, gains, biases = refs[-7:]
    local[...] = get_terms(packed, "local", CL)
    cross[...] = get_terms(packed, "cross", CG)
    reduce_w[...] = get_terms(packed, "reduce", CG)
    spectral[...] = get_terms(packed, "spectral", CG)
    expand[...] = get_terms(packed, "expand", CG)
    rows = get_terms(packed, "norms", NORMS)
    biases[...] = rows[0:1]
    gains[...] = rows[1:2]


def unpack_call(packed, after):
    shape = jax.ShapeDtypeStruct
    dims = ((9 * CH, CL), (9 * CL, CG), (CS, CG), (CG, CG), (CS, CG), (1, NORMS), (1, NORMS))
    return pl.pallas_call(
        unpack_kernel,
        out_shape=[shape(d, F32) for d in dims],
        in_specs=[VMEM] + [ANY] * len(after),
        out_specs=[VMEM] * 7,
        name="unpack_terms",
        compiler_params=pltpu.CompilerParams(vmem_limit_bytes=VMEM_LIMIT),
    )(packed, *after)


def spread_kernel(batches, place, images, other, *refs):
    parts, sem = refs[:PARTS], refs[-1]
    core, z = place[1], place[2]
    copies = []
    for k, part in enumerate(parts):
        i = jnp.clip((z ^ k) - (1 - core), 0, batches // 2 - 1)
        copies.append(pltpu.make_async_copy(images.at[2 * i + 1 - core], part.at[0], sem.at[k, 0]))
        copies.append(pltpu.make_async_copy(other.at[i], part.at[1], sem.at[k, 1]))
    for c in copies:
        c.start()
    for c in copies:
        c.wait()


def spread_call(place, images, other, through=(), after=()):
    batches, pixels, channels = images.shape
    skip = len(through) + len(after)

    def kernel(place, images, other, *refs):
        spread_kernel(batches, place, images, other, *refs[skip:])

    return pl.pallas_call(
        kernel,
        out_shape=[jax.ShapeDtypeStruct((2, pixels, channels), BF)] * PARTS + [jax.ShapeDtypeStruct(x.shape, x.dtype) for x in through],
        in_specs=[SMEM, VMEM, VMEM] + [ANY] * skip,
        out_specs=[ANY] * (PARTS + len(through)),
        scratch_shapes=[pltpu.SemaphoreType.DMA((PARTS, 2))],
        input_output_aliases={3 + i: PARTS + i for i in range(len(through))},
        name="spread_images",
        compiler_params=pltpu.CompilerParams(vmem_limit_bytes=VMEM_LIMIT),
    )(place, images, other, *through, *after)


def second_images(p0, p1, p2, p3, out, stage, sem_in, sem_out):
    pixels = out.shape[1]
    loads = [pltpu.make_async_copy(p.at[pl.ds(pixels, pixels)], stage.at[k], sem_in.at[k]) for k, p in enumerate((p0, p1, p2, p3))]
    for c in loads:
        c.start()
    stores = [pltpu.make_async_copy(stage.at[k], out.at[k], sem_out.at[k]) for k in range(PARTS)]
    for load, store in zip(loads, stores):
        load.wait()
        store.start()
    for c in stores:
        c.wait()


def second_images_call(parts):
    rows, channels = parts[0].shape
    dma = pltpu.SemaphoreType.DMA
    return pl.pallas_call(
        second_images,
        out_shape=jax.ShapeDtypeStruct((PARTS, rows // 2, channels), BF),
        in_specs=[ANY] * PARTS,
        out_specs=ANY,
        scratch_shapes=[pltpu.VMEM((PARTS, rows // 2, channels), BF), dma((PARTS,)), dma((PARTS,))],
        name="second_images",
    )(*parts)


def collect_kernel(batches, place, p0, p1, p2, p3, other, out, stage, sem):
    core, z = place[1], place[2]
    parts = (p0, p1, p2, p3)
    pixels = p0.shape[0] // 2
    copies = []
    for k, part in enumerate(parts):
        copies.append(pltpu.make_async_copy(part.at[pl.ds(0, pixels)], stage.at[k, 0], sem.at[k, 0]))
        copies.append(pltpu.make_async_copy(other.at[k], stage.at[k, 1], sem.at[k, 1]))
    for c in copies:
        c.start()
    for k in range(PARTS):
        for j in range(2):
            copies[2 * k + j].wait()
            batch = 2 * (z ^ k) + (1 - core if j else core) - 1

            @pl.when(jnp.logical_and(batch >= 0, batch < batches))
            def _():
                out[batch] = stage[k, j].astype(out.dtype)


def collect_call(place, batches, parts, other, dtype):
    rows, channels = parts[0].shape
    return pl.pallas_call(
        functools.partial(collect_kernel, batches),
        out_shape=jax.ShapeDtypeStruct((batches, rows // 2, channels), dtype),
        in_specs=[SMEM] + [ANY] * (PARTS + 1),
        out_specs=VMEM,
        scratch_shapes=[pltpu.VMEM((PARTS, 2, rows // 2, channels), BF), pltpu.SemaphoreType.DMA((PARTS, 2))],
        name="collect_images",
        compiler_params=pltpu.CompilerParams(vmem_limit_bytes=VMEM_LIMIT),
    )(place, *parts, other)


SOURCES = (
    (("own", "own"), ("x1", "x1"), ("y1", "y1"), ("x2", "y2")),
    (("x1", "x1"), ("own", "own"), ("x2", "y2"), ("y1", "y1")),
    (("y1", "y1"), ("x2", "y2"), ("own", "own"), ("x1", "x1")),
    (("x2", "y2"), ("y1", "y1"), ("x1", "x1"), ("own", "own")),
)


def load_weights(place, arrived, low, high, w, sems):
    rank, core = place[0], place[1]
    for s in range(low, high):
        for r, sources in enumerate(SOURCES):

            @pl.when(rank == r)
            def _():
                for half, name in enumerate(sources[s]):
                    for other in range(2):
                        quarter = 2 * half + (1 - core if other else core)
                        if name == "own":
                            src = arrived["own"].at[pl.ds(pl.multiple_of(quarter * QROWS, 16), QROWS)]
                        else:
                            src = arrived[name][other].at[half if name in ("x1", "y1") else 0]
                        pltpu.make_async_copy(src, w.at[s - low, quarter], sems.at[s - low, 2 * half + other]).start()


def wait_weights(own, index, w, sems):
    for n in range(4):
        pltpu.make_async_copy(own.at[pl.ds(0, QROWS)], w.at[index, 0], sems.at[index, n]).wait()


def moments_of(v):
    mean = jnp.mean(v, axis=0, keepdims=True)
    centred = v - mean
    return mean, jnp.sum(centred * centred, axis=0, keepdims=True)


def combined(mean_ref, square_ref, rows):
    images = mean_ref.shape[0]
    means = [mean_ref[b] for b in range(images)]
    mean = sum(means) / images
    total = sum(square_ref[b] + rows * (means[b] - mean) ** 2 for b in range(images))
    return mean, lax.rsqrt(total / (images * rows) + EPS)


def halves(gain, bias, mean, inv):
    scale = 0.5 * gain * inv
    return scale, 0.5 * bias - mean * scale


def beside(v, column, by, side):
    if by < 0:
        return jnp.where(column == 0, 0.0, pltpu.roll(v, 1, 0))
    return jnp.where(column == side - 1, 0.0, pltpu.roll(v, v.shape[0] - 1, 0))


def three_columns(dst, b, x, column, side):
    pixels = x.shape[0]
    wide = x.astype(F32)
    for i, v in enumerate((beside(wide, column, -1, side).astype(BF), x, beside(wide, column, 1, side).astype(BF))):
        dst[i, b, 0:side] = jnp.zeros((side, CL), BF)
        dst[i, b, side : side + pixels] = v
        dst[i, b, side + pixels : 2 * side + pixels] = jnp.zeros((side, CL), BF)


def three_rows(x, side, images):
    pixels = x.shape[0] // images
    none = jnp.zeros((side, x.shape[1]), x.dtype)
    back, on = [], []
    for i in range(images):
        back += [none, x[i * pixels : (i + 1) * pixels - side]]
        on += [x[i * pixels + side : (i + 1) * pixels], none]
    return stack_rows(back), x, stack_rows(on)


def nine(src, b, side, flipped):
    pixels = side * side
    parts = []
    for dh in range(3):
        for dw in range(3):
            i, j = (2 - dh, 2 - dw) if flipped else (dh, dw)
            parts.append(src[j, b, i * side : i * side + pixels])
    return parts


def part_copies(whole, parts, sems):
    rows = whole.shape[0] // len(parts)
    return [pltpu.make_async_copy(whole.at[pl.ds(k * rows, rows)], ref, sems.at[k]) for k, ref in enumerate(parts)]


def needed(low, high):
    return sorted({name for sources in SOURCES for s in range(low, high) for name in sources[s]} - {"own"})


class Space:
    def __init__(self, **named):
        self.__dict__.update(named)


def geometry(side, images):
    pixels, modes = side * side, side * (side // 2 + 1)
    column = lambda: lax.broadcasted_iota(jnp.int32, (pixels, 1), 0) % side
    wide = lambda: lax.broadcasted_iota(jnp.int32, (IM * pixels, 1), 0) % side
    return Space(
        side=side,
        images=images,
        pixels=pixels,
        modes=modes,
        steps=images // IM,
        column=column,
        wide=wide,
        rows_of=lambda b: pl.ds(pl.multiple_of(b * (IM * pixels), IM * pixels), IM * pixels),
        modes_of=lambda b: pl.ds(pl.multiple_of(b * (IM * modes), IM * modes), IM * modes),
        image_rows=lambda b, i: pl.ds(pl.multiple_of(b * (IM * pixels) + i * pixels, pixels), pixels),
    )


def forward_section(geo, v, ws, a, o, odd):
    column, wide = geo.column(), geo.wide()
    side, pixels, modes = geo.side, geo.pixels, geo.modes
    gain, bias = read_norms(ws)

    def reduce_step(b, _):
        r = geo.rows_of(b)
        for i in range(IM):
            three_columns(v.xp, b * IM + i, a[geo.image_rows(b, i), 0:CL], column, side)
        x = dot_nt(a[r, CL:CH], read(ws, "reduce", 0, CS))
        v.q[r] = x
        v.mu1[b], v.sq1[b] = moments_of(x)
        return 0

    lax.fori_loop(0, geo.steps, reduce_step, 0, unroll=UN)
    mean1, inv1 = combined(v.mu1, v.sq1, IM * pixels)
    scale1, shift1 = halves(gain[:, :CS], bias[:, :CS], mean1, inv1)

    def spectral_step(b, _):
        r, rs = geo.rows_of(b), geo.modes_of(b)
        h = v.q[r] * scale1 + shift1
        v.h1[r] = h.astype(BF)
        act = silu_of_half(h)
        v.t[r] = act
        act = act.astype(BF)
        spec = [dot(v.mf[...], act[i * pixels : (i + 1) * pixels]).astype(BF) for i in range(IM)]
        real = stack_rows([x[:modes] for x in spec])
        imaginary = stack_rows([x[modes:] for x in spec])
        v.sv[0, rs] = real
        v.sv[1, rs] = imaginary
        mix = dot(real, read(ws, "spectral", 0, CS)) + dot(imaginary, read(ws, "spectral", CS, CS))
        v.f[rs] = mix
        v.mu2[b], v.sq2[b] = moments_of(mix)
        taps = stack_rows([stack_cols(nine(v.xp, b * IM + i, side, False)) for i in range(IM)])
        v.p[r] = dot(taps, conv_matrix(ws))
        return 0

    lax.fori_loop(0, geo.steps, spectral_step, 0, unroll=UN)
    mean2, inv2 = combined(v.mu2, v.sq2, IM * modes)
    scale2, shift2 = halves(gain[:, CS : CS + CG], bias[:, CS : CS + CG], mean2, inv2)

    def join_step(b, _):
        r, rs = geo.rows_of(b), geo.modes_of(b)
        h = v.f[rs] * scale2 + shift2
        v.h2[rs] = h.astype(BF)
        e = silu_of_half(h)
        er, ei = e[:, :CS].astype(BF), e[:, CS:].astype(BF)
        back = []
        for i in range(IM):
            m = slice(i * modes, (i + 1) * modes)
            back.append(dot(v.mi[...], stack_rows([er[m], ei[m]])))
        j = (v.t[r] + stack_rows(back)).astype(BF)
        v.jv[r] = j
        pre_global = v.p[r, CL:CH] + dot(j, read(ws, "expand", 0, CS))
        y = dot(stack_cols(three_rows(a[r, CL:CH], side, IM)), global_by_row(ws))
        pre_local = v.p[r, 0:CL] + beside(y[:, :CL], wide, -1, side) + y[:, CL : 2 * CL] + beside(y[:, 2 * CL :], wide, 1, side)
        v.p[r, 0:CL] = pre_local
        v.p[r, CL:CH] = pre_global
        ml, sl = moments_of(pre_local)
        mg, sg = moments_of(pre_global)
        v.mu3[b] = stack_cols([ml, mg])
        v.sq3[b] = stack_cols([sl, sg])
        return 0

    lax.fori_loop(0, geo.steps, join_step, 0, unroll=UN)
    mean3, inv3 = combined(v.mu3, v.sq3, IM * pixels)
    scale3, shift3 = halves(gain[:, CS + CG :], bias[:, CS + CG :], mean3, inv3)

    def end_step(b, _):
        r = geo.rows_of(b)
        h = v.p[r] * scale3 + shift3
        v.h3[r] = h.astype(BF)
        y = silu_of_half(h)
        if odd is not None:
            y = y + jnp.where(odd, o[r].astype(F32), 0.0)
        o[r] = y.astype(BF)
        return 0

    lax.fori_loop(0, geo.steps, end_step, 0, unroll=UN)
    return stack_cols([inv1, inv2, inv3])


def norm_terms(sums, gain, bias, factor, count):
    first, second = (jnp.sum(x, axis=0, keepdims=True) for x in sums)
    first = 0.5 * first
    second = (second - bias * first) / gain
    k1 = factor / count * (second * bias / gain - first)
    return first, second, (0.5 * factor, k1, 2.0 / count * factor * second / gain)


def part_sums(c, d, h):
    add = lambda x: jnp.sum(x.reshape(x.shape[0] // 8, 8, x.shape[1]), axis=0)
    return c[0] + add(d), c[1] + add(d * h)


def no_sums(c):
    return jnp.zeros((8, c), F32), jnp.zeros((8, c), F32)


def local_adjoint(geo, v, ws, dp, wide):
    back, same, on = three_rows(dp, geo.side, IM)
    y = dot_nt(stack_cols([on, same, back]), conv_by_column(ws))
    return beside(y[:, :CL], wide, 1, geo.side) + y[:, CL : 2 * CL] + beside(y[:, 2 * CL :], wide, -1, geo.side)


def global_adjoint(geo, v, ws, b):
    taps = stack_rows([stack_cols(nine(v.xp, b * IM + i, geo.side, True)) for i in range(IM)])
    return dot_nt(taps, global_matrix(ws))


def backward_section(geo, v, ws, inv, g, o, even, convs):
    column, wide = geo.column(), geo.wide()
    side, pixels, modes = geo.side, geo.pixels, geo.modes
    n1, n2 = float(geo.images * pixels), float(geo.images * modes)
    gain, bias = read_norms(ws)
    g1, g2, g3 = gain[:, :CS], gain[:, CS : CS + CG], gain[:, CS + CG :]
    b1, b2, b3 = bias[:, :CS], bias[:, CS : CS + CG], bias[:, CS + CG :]
    c1, c2, c3 = g1 * inv[:, :CS], g2 * inv[:, CS : CS + CG], g3 * inv[:, CS + CG :]

    def end_step(b, c):
        r = geo.rows_of(b)
        h = v.h3[r].astype(F32)
        d = g[r].astype(F32) * twice_slope(h)
        v.p[r] = d
        return part_sums(c, d, h)

    first3, second3, k3 = norm_terms(lax.fori_loop(0, geo.steps, end_step, no_sums(CH), unroll=UN), g3, b3, c3, n1)

    def join_step(b, c):
        r, rs = geo.rows_of(b), geo.modes_of(b)
        dp = (k3[0] * v.p[r] + (k3[1] - k3[2] * v.h3[r].astype(F32))).astype(BF)
        v.dpv[r] = dp
        djv = dot_nt(dp[:, CL:], read(ws, "expand", 0, CS))
        v.dj[r] = djv
        djv = djv.astype(BF)
        de = [dot(v.mit[...], djv[i * pixels : (i + 1) * pixels]) for i in range(IM)]
        de = stack_cols([stack_rows([x[:modes] for x in de]), stack_rows([x[modes:] for x in de])])
        h = v.h2[rs].astype(F32)
        d = de * twice_slope(h)
        v.du2[rs] = d
        if convs:
            for i in range(IM):
                three_columns(v.xp, b * IM + i, dp[i * pixels : (i + 1) * pixels, :CL], column, side)
            v.p[r, 0:CL] = local_adjoint(geo, v, ws, dp, wide)
        return part_sums(c, d, h)

    first2, second2, k2 = norm_terms(lax.fori_loop(0, geo.steps, join_step, no_sums(CG), unroll=UN), g2, b2, c2, n2)

    def spectral_step(b, c):
        r, rs = geo.rows_of(b), geo.modes_of(b)
        df = (k2[0] * v.du2[rs] + (k2[1] - k2[2] * v.h2[rs].astype(F32))).astype(BF)
        v.dfv[rs] = df
        ds = dot_nt(df, read(ws, "spectral", 0, CG))
        dr, di = ds[:, :CS].astype(BF), ds[:, CS:].astype(BF)
        back = []
        for i in range(IM):
            m = slice(i * modes, (i + 1) * modes)
            back.append(dot(v.mft[...], stack_rows([dr[m], di[m]])))
        dt = v.dj[r] + stack_rows(back)
        h = v.h1[r].astype(F32)
        d = dt * twice_slope(h)
        v.du1[r] = d
        if convs:
            v.p[r, CL:CH] = global_adjoint(geo, v, ws, b)
        return part_sums(c, d, h)

    first1, second1, k1 = norm_terms(lax.fori_loop(0, geo.steps, spectral_step, no_sums(CS), unroll=UN), g1, b1, c1, n1)

    def reduce_step(b, c):
        r = geo.rows_of(b)
        dq = (k1[0] * v.du1[r] + (k1[1] - k1[2] * v.h1[r].astype(F32))).astype(BF)
        v.dqv[r] = dq
        if convs:
            dx = stack_cols([v.p[r, 0:CL], v.p[r, CL:CH] + dot(dq, read(ws, "reduce", 0, CS))])
            if even is not None:
                dx = dx + jnp.where(even, o[r].astype(F32), 0.0)
            o[r] = dx.astype(BF)
        return c

    lax.fori_loop(0, geo.steps, reduce_step, 0, unroll=UN)
    return stack_cols([first1, first2, first3]), stack_cols([second1, second2, second3])


def weight_terms(geo, v, norms):
    column, side, pixels = geo.column(), geo.side, geo.pixels

    def tap_products(source, flipped, product):
        def columns(b, _):
            three_columns(v.xp, b, source[pl.ds(pl.multiple_of(b * pixels, pixels), pixels), 0:CL], column, side)
            return 0

        lax.fori_loop(0, geo.images, columns, 0, unroll=4)

        def one_row(dh, _):
            def gather(b, _):
                r = pl.ds(pl.multiple_of(b * pixels, pixels), pixels)
                first = pl.multiple_of((2 - dh if flipped else dh) * side, side)
                for dw in range(3):
                    v.taps[r, dw * CL : (dw + 1) * CL] = v.xp[2 - dw if flipped else dw, b, pl.ds(first, pixels)]
                return 0

            lax.fori_loop(0, geo.images, gather, 0, unroll=4)
            product(dh)
            return 0

        lax.fori_loop(0, 3, one_row, 0)

    def from_gradient(dh):
        u = dot_tn(v.ain[:, CL:], v.taps[...])
        for dw in range(3):
            put_terms(v.terms, "local", (dh * 3 + dw) * CH + CL, u[:, dw * CL : (dw + 1) * CL])

    def from_input(dh):
        u = dot_tn(v.taps[...], v.dpv[...])
        for dw in range(3):
            tap = slice(dw * CL, (dw + 1) * CL)
            put_terms(v.terms, "local", (dh * 3 + dw) * CH, u[tap, :CL])
            put_terms(v.terms, "cross", (dh * 3 + dw) * CL, u[tap, CL:])

    tap_products(v.dpv, True, from_gradient)
    tap_products(v.ain, False, from_input)
    put_terms(v.terms, "reduce", 0, dot_tn(v.dqv[...], v.ain[:, CL:]))
    put_terms(v.terms, "spectral", 0, dot_tn(v.sv[0], v.dfv[...]))
    put_terms(v.terms, "spectral", CS, dot_tn(v.sv[1], v.dfv[...]))
    put_terms(v.terms, "expand", 0, dot_tn(v.jv[...], v.dpv[:, CL:]))
    put_norm_terms(v.terms, norms)


def fill_parts(parts, whole, sems):
    rows = whole.shape[0] // len(parts)
    return [pltpu.make_async_copy(ref, whole.at[pl.ds(k * rows, rows)], sems.at[k]) for k, ref in enumerate(parts)]


def start_all(copies):
    for c in copies:
        c.start()


def wait_all(copies):
    for c in copies:
        c.wait()


DMA = pltpu.SemaphoreType.DMA


class Arguments:
    def __init__(self):
        self.ins, self.specs, self.outs, self.out_specs, self.scratch, self.aliases = [], [], [], [], [], {}
        self.names = [[], [], []]

    def take(self, name, value, spec):
        many = isinstance(value, (list, tuple))
        values = list(value) if many else [value]
        self.names[0].append((name, len(values) if many else None))
        at = len(self.ins)
        self.ins += values
        self.specs += [spec] * len(values)
        return at

    def give(self, name, shape, dtype, spec, count=None, over=None):
        self.names[1].append((name, count))
        for i in range(count or 1):
            if over is not None:
                self.aliases[over + i] = len(self.outs)
            self.outs.append(jax.ShapeDtypeStruct(shape, dtype))
            self.out_specs.append(spec)

    def hold(self, name, kind):
        self.names[2].append((name, None))
        self.scratch.append(kind)

    def unpack(self, refs):
        refs, space = list(refs), Space()
        for group in self.names:
            for name, count in group:
                setattr(space, name, refs.pop(0) if count is None else [refs.pop(0) for _ in range(count)])
        return space

    def call(self, body, name, flops, moved=20_000_000):
        results = pl.pallas_call(
            lambda *refs: body(self.unpack(refs)),
            out_shape=self.outs,
            in_specs=self.specs,
            out_specs=self.out_specs,
            scratch_shapes=self.scratch,
            input_output_aliases=self.aliases,
            name=name,
            cost_estimate=pl.CostEstimate(flops=int(flops), bytes_accessed=moved, transcendentals=0),
            compiler_params=pltpu.CompilerParams(vmem_limit_bytes=VMEM_LIMIT),
        )(*self.ins)
        results, space = list(results), Space()
        for out_name, count in self.names[1]:
            setattr(space, out_name, results.pop(0) if count is None else [results.pop(0) for _ in range(count)])
        return space


def take_weights(args, own, arrived, low, high):
    names = needed(low, high)
    args.take("own", own, ANY)
    for name in names:
        args.take("got_" + name, arrived[name], ANY)
    args.hold("w", pltpu.VMEM((high - low, QUARTERS, QROWS, 128), BF))
    args.hold("wsem", DMA((high - low, 4)))
    return names


def got_weights(v, names):
    return {"own": v.own, **{name: getattr(v, "got_" + name) for name in names}}


def hold_forward(args, n, m, images, pixels, side):
    args.hold("mu1", pltpu.VMEM((images // IM, 1, CS), F32))
    args.hold("sq1", pltpu.VMEM((images // IM, 1, CS), F32))
    args.hold("mu2", pltpu.VMEM((images // IM, 1, CG), F32))
    args.hold("sq2", pltpu.VMEM((images // IM, 1, CG), F32))
    args.hold("mu3", pltpu.VMEM((images // IM, 1, CH), F32))
    args.hold("sq3", pltpu.VMEM((images // IM, 1, CH), F32))


def hold_work(args, n, m, images, pixels, side):
    args.hold("xp", pltpu.VMEM((3, images, pixels + 2 * side, CL), BF))
    args.hold("q", pltpu.VMEM((n, CS), F32))
    args.hold("t", pltpu.VMEM((n, CS), F32))
    args.hold("f", pltpu.VMEM((m, CG), F32))
    args.hold("p", pltpu.VMEM((n, CH), F32))


def hold_terms(args, n, m):
    args.hold("dpv", pltpu.VMEM((n, CH), BF))
    args.hold("dqv", pltpu.VMEM((n, CS), BF))
    args.hold("dfv", pltpu.VMEM((m, CG), BF))
    args.hold("ain", pltpu.VMEM((n, CH), BF))
    args.hold("sv", pltpu.VMEM((2, m, CS), BF))
    args.hold("jv", pltpu.VMEM((n, CS), BF))
    args.hold("taps", pltpu.VMEM((n, 3 * CL), BF))
    args.hold("terms", pltpu.VMEM((QUARTERS * QROWS, 128), BF))


def first_call(place, inputs, own, arrived, mf, mi, after, side, images):
    geo = geometry(side, images)
    n, m = images * geo.pixels, images * geo.modes
    args = Arguments()
    args.take("place", place, SMEM)
    args.take("inputs", inputs, ANY)
    args.take("mf", mf, VMEM)
    args.take("mi", mi, VMEM)
    args.take("after", after, ANY)
    names = take_weights(args, own, arrived, 0, 1)
    args.give("out", (n, CH), BF, ANY)
    args.give("h1_out", (n, CS), BF, ANY)
    args.give("h2_out", (m, CG), BF, ANY)
    args.give("h3_out", (n, CH), BF, ANY)
    args.give("spec_out", (2, m, CS), BF, ANY)
    args.give("join_out", (n, CS), BF, ANY)
    args.give("inv_out", (1, NORMS), F32, VMEM)
    args.hold("a", pltpu.VMEM((n, CH), BF))
    args.hold("o", pltpu.VMEM((n, CH), BF))
    args.hold("h1", pltpu.VMEM((n, CS), BF))
    args.hold("h2", pltpu.VMEM((m, CG), BF))
    args.hold("h3", pltpu.VMEM((n, CH), BF))
    args.hold("sv", pltpu.VMEM((2, m, CS), BF))
    args.hold("jv", pltpu.VMEM((n, CS), BF))
    hold_work(args, n, m, images, geo.pixels, side)
    hold_forward(args, n, m, images, geo.pixels, side)
    args.hold("isem", DMA((PARTS,)))
    args.hold("osem", DMA((6,)))

    def body(v):
        loads = fill_parts(v.inputs, v.a, v.isem)
        start_all(loads)
        load_weights(v.place, got_weights(v, names), 0, 1, v.w, v.wsem)
        wait_all(loads)
        wait_weights(v.own, 0, v.w, v.wsem)
        v.inv_out[...] = forward_section(geo, v, v.w.at[0], v.a, v.o, None)
        pairs = (
            (v.o, v.out),
            (v.h1, v.h1_out),
            (v.h2, v.h2_out),
            (v.h3, v.h3_out),
            (v.sv, v.spec_out),
            (v.jv, v.join_out),
        )
        stores = [pltpu.make_async_copy(a, b, v.osem.at[i]) for i, (a, b) in enumerate(pairs)]
        start_all(stores)
        wait_all(stores)

    return args.call(body, "forward_0", 1, 1)


def middle_call(place, out0, inputs, seeds, own, arrived, tables, side, images):
    low, high = 1, 4
    geo = geometry(side, images)
    n, m, count = images * geo.pixels, images * geo.modes, high - low
    args = Arguments()
    args.take("place", place, SMEM)
    args.take("out0", out0, ANY)
    args.take("inputs", inputs, ANY)
    seeds_at = args.take("seeds", seeds, ANY)
    for name, table in zip(("mf", "mi", "mft", "mit"), tables):
        args.take(name, table, VMEM)
    names = take_weights(args, own, arrived, low, high)
    args.give("grads0", (n // PARTS, CH), BF, ANY, PARTS, seeds_at)
    args.give("grad1", (n, CH), BF, ANY)
    args.give("own_out", (n // PARTS, CH), BF, ANY, PARTS)
    args.give("own_grad", (n // PARTS, CH), BF, ANY, PARTS)
    args.give("own_terms", (QUARTERS * QROWS, 128), BF, ANY)
    args.hold("cur", pltpu.VMEM((2, n, CH), BF))
    args.hold("hats1", pltpu.VMEM((count, n, CS), BF))
    args.hold("hats2", pltpu.VMEM((count, m, CG), BF))
    args.hold("hats3", pltpu.VMEM((count, n, CH), BF))
    args.hold("inv", pltpu.VMEM((count, 1, NORMS), F32))
    args.hold("spec", pltpu.VMEM((2, m, CS), BF))
    args.hold("join", pltpu.VMEM((n, CS), BF))
    hold_work(args, n, m, images, geo.pixels, side)
    hold_forward(args, n, m, images, geo.pixels, side)
    hold_terms(args, n, m)
    args.hold("asem", DMA((1,)))
    args.hold("isem", DMA((PARTS,)))
    args.hold("gsem", DMA((PARTS,)))
    args.hold("outsem", DMA((PARTS,)))
    args.hold("gradsem", DMA((PARTS,)))
    args.hold("ksem", DMA((3,)))
    args.hold("tsem", DMA((1,)))
    args.hold("lastsem", DMA((PARTS + 1,)))

    def body(v):
        rank = v.place[0]
        loads = [pltpu.make_async_copy(v.out0, v.cur.at[1], v.asem.at[0])] + fill_parts(v.inputs, v.cur.at[0], v.isem)
        start_all(loads)
        load_weights(v.place, got_weights(v, names), low, high, v.w, v.wsem)
        wait_all(loads)
        rank0_out = part_copies(v.cur.at[1], v.own_out, v.outsem)

        @pl.when(rank == 0)
        def _():
            start_all(rank0_out)

        def at(index, **more):
            return Space(**{**v.__dict__, "h1": v.hats1.at[index], "h2": v.hats2.at[index], "h3": v.hats3.at[index], **more})

        def forward_one(index, _):
            s = index + low
            a, o = v.cur.at[s % 2], v.cur.at[(s + 1) % 2]
            mine = rank == s
            wait_weights(v.own, index, v.w, v.wsem)
            keep_in = pltpu.make_async_copy(a, v.ain, v.ksem.at[0])

            @pl.when(mine)
            def _():
                keep_in.start()

            v.inv[index] = forward_section(geo, at(index, sv=v.spec, jv=v.join), v.w.at[index], a, o, s % 2 == 1)

            @pl.when(mine)
            def _():
                keeps = [
                    pltpu.make_async_copy(v.spec, v.sv, v.ksem.at[1]),
                    pltpu.make_async_copy(v.join, v.jv, v.ksem.at[2]),
                    *part_copies(o, v.own_out, v.outsem),
                ]
                start_all(keeps)
                wait_all([keep_in, *keeps])

            @pl.when(jnp.logical_and(rank == 0, index == 0))
            def _():
                wait_all(rank0_out)

            return 0

        lax.fori_loop(0, count, forward_one, 0)
        loads = fill_parts(v.seeds, v.cur.at[(high - 1) % 2], v.gsem)
        start_all(loads)
        wait_all(loads)

        @pl.when(v.place[3] == 0)
        def _():
            v.cur[(high - 1) % 2] = jnp.zeros((n, CH), BF)

        def backward_one(step, _):
            index = count - 1 - step
            s = index + low
            g, o = v.cur.at[s % 2], v.cur.at[(s + 1) % 2]
            norms = backward_section(geo, at(index, du1=v.q, du2=v.f, dj=v.t), v.w.at[index], v.inv[index], g, o, s % 2 == 0, True)

            @pl.when(rank == s)
            def _():
                keeps = part_copies(o, v.own_grad, v.gradsem)
                start_all(keeps)
                weight_terms(geo, v, norms)
                keeps.append(pltpu.make_async_copy(v.terms, v.own_terms, v.tsem.at[0]))
                keeps[-1].start()
                wait_all(keeps)

            return 0

        lax.fori_loop(0, count, backward_one, 0)
        stores = part_copies(v.cur.at[0], v.grads0, v.lastsem)
        stores.append(pltpu.make_async_copy(v.cur.at[1], v.grad1, v.lastsem.at[PARTS]))
        start_all(stores)
        wait_all(stores)

    return args.call(body, "sections_1_3", images * 6e9)


def last_norms_call(place, first, grads0, inputs, own_terms, weights, arrived, tables, side, images):
    geo = geometry(side, images)
    n, m = images * geo.pixels, images * geo.modes
    args = Arguments()
    args.take("place", place, SMEM)
    args.take("grads0", grads0, ANY)
    args.take("inputs", inputs, ANY)
    args.take("h1_in", first.h1_out, ANY)
    args.take("h2_in", first.h2_out, ANY)
    args.take("h3_in", first.h3_out, ANY)
    args.take("spec_in", first.spec_out, ANY)
    args.take("join_in", first.join_out, ANY)
    args.take("inv", first.inv_out, VMEM)
    for name, table in zip(("mft", "mit"), tables):
        args.take(name, table, VMEM)
    terms_at = args.take("terms_in", own_terms, ANY)
    names = take_weights(args, weights, arrived, 0, 1)
    args.give("dp", (n, CH), BF, ANY)
    args.give("dq", (n, CS), BF, ANY)
    args.give("own_terms", (QUARTERS * QROWS, 128), BF, ANY, None, terms_at)
    args.hold("g", pltpu.VMEM((n, CH), BF))
    args.hold("h1", pltpu.VMEM((n, CS), BF))
    args.hold("h2", pltpu.VMEM((m, CG), BF))
    args.hold("h3", pltpu.VMEM((n, CH), BF))
    hold_work(args, n, m, images, geo.pixels, side)
    hold_terms(args, n, m)
    args.hold("gsem", DMA((PARTS,)))
    args.hold("isem", DMA((PARTS,)))
    args.hold("hsem", DMA((3,)))
    args.hold("ksem", DMA((2,)))
    args.hold("osem", DMA((3,)))

    def body(v):
        rank = v.place[0]
        loads = fill_parts(v.grads0, v.g, v.gsem)
        hats = ((v.h1_in, v.h1), (v.h2_in, v.h2), (v.h3_in, v.h3))
        loads += [pltpu.make_async_copy(a, b, v.hsem.at[i]) for i, (a, b) in enumerate(hats)]
        start_all(loads)
        load_weights(v.place, got_weights(v, names), 0, 1, v.w, v.wsem)
        kept = fill_parts(v.inputs, v.ain, v.isem)
        kept += [pltpu.make_async_copy(v.spec_in, v.sv, v.ksem.at[0]), pltpu.make_async_copy(v.join_in, v.jv, v.ksem.at[1])]

        @pl.when(rank == 0)
        def _():
            start_all(kept)

        wait_all(loads)
        wait_weights(v.own, 0, v.w, v.wsem)
        space = Space(**{**v.__dict__, "du1": v.q, "du2": v.f, "dj": v.t})
        norms = backward_section(geo, space, v.w.at[0], v.inv[...], v.g, None, None, False)
        stores = [pltpu.make_async_copy(v.dpv, v.dp, v.osem.at[0]), pltpu.make_async_copy(v.dqv, v.dq, v.osem.at[1])]
        start_all(stores)

        @pl.when(rank == 0)
        def _():
            wait_all(kept)
            weight_terms(geo, v, norms)
            out = pltpu.make_async_copy(v.terms, v.own_terms, v.osem.at[2])
            out.start()
            out.wait()

        wait_all(stores)

    return args.call(body, "backward_0_norms", images * 400e6)


def last_convs_call(place, back, grad1, own_grad, weights, arrived, side, images):
    geo = geometry(side, images)
    n, m = images * geo.pixels, images * geo.modes
    args = Arguments()
    args.take("place", place, SMEM)
    args.take("dp", back.dp, ANY)
    args.take("dq", back.dq, ANY)
    args.take("grad1", grad1, ANY)
    grad_at = args.take("grad_in", own_grad, ANY)
    names = take_weights(args, weights, arrived, 0, 1)
    args.give("own_grad", (n // PARTS, CH), BF, ANY, PARTS, grad_at)
    args.hold("dpv", pltpu.VMEM((n, CH), BF))
    args.hold("dqv", pltpu.VMEM((n, CS), BF))
    args.hold("o", pltpu.VMEM((n, CH), BF))
    args.hold("xp", pltpu.VMEM((3, images, geo.pixels + 2 * side, CL), BF))
    args.hold("lsem", DMA((3,)))
    args.hold("osem", DMA((PARTS,)))

    def body(v):
        @pl.when(v.place[0] == 0)
        def _():
            pairs = ((v.dp, v.dpv), (v.dq, v.dqv), (v.grad1, v.o))
            loads = [pltpu.make_async_copy(a, b, v.lsem.at[i]) for i, (a, b) in enumerate(pairs)]
            start_all(loads)
            load_weights(v.place, got_weights(v, names), 0, 1, v.w, v.wsem)
            wait_all(loads)
            wait_weights(v.own, 0, v.w, v.wsem)
            ws = v.w.at[0]
            column, wide = geo.column(), geo.wide()

            def step(b, _):
                r = geo.rows_of(b)
                dp = v.dpv[r]
                for i in range(IM):
                    three_columns(v.xp, b * IM + i, dp[i * geo.pixels : (i + 1) * geo.pixels, :CL], column, side)
                dxl = local_adjoint(geo, v, ws, dp, wide)
                dxg = global_adjoint(geo, v, ws, b) + dot(v.dqv[r], read(ws, "reduce", 0, CS))
                v.o[r] = (stack_cols([dxl, dxg]) + v.o[r].astype(F32)).astype(BF)
                return 0

            lax.fori_loop(0, geo.steps, step, 0, unroll=UN)
            stores = part_copies(v.o, v.own_grad, v.osem)
            start_all(stores)
            wait_all(stores)

    return args.call(body, "backward_0_convs", images * 600e6)


def exchange_weights(send, after):
    def over(bit, x):
        return lax.ppermute(x, "pipe", [(i ^ bit, i) for i in range(4)])

    def swap(x):
        return lax.ppermute(x, "dp", [(i, i ^ 1) for i in range(lax.axis_size("dp"))])

    got = {"x1": over(1, send), "y1": over(2, send)}
    over_x, over_y = relay_call(got["y1"], got["x1"], after)
    got["x2"], got["y2"] = over(1, over_x), over(2, over_y)
    return {name: (x, swap(x)) for name, x in got.items()}


def local_device(images_in, conv_local, conv_cross, reduce_weight, spectral_weight, expand_weight, norm_gain, norm_bias, cotangent, hole_mask):
    batches, _, side, _, channels = images_in.shape
    pixels = side * side
    dp_size = lax.axis_size("dp")
    dp_rank = lax.axis_index("dp")
    core = dp_rank % 2
    holders = range(1, 1 + batches)
    holds = jnp.logical_and(dp_rank >= holders.start, dp_rank < holders.stop)
    place = jnp.stack([lax.axis_index("pipe"), core, dp_rank // 2, holds]).astype(jnp.int32)
    table_to, table_from = dft_np(side)
    mf, mi = jnp.asarray(table_to, BF), jnp.asarray(table_from, BF)
    mft, mit = jnp.asarray(table_to.T, BF), jnp.asarray(table_from.T, BF)

    def swap(x):
        return lax.ppermute(x, "dp", [(i, i ^ 1) for i in range(dp_size)])

    def along_z(k, x, pairs):
        return lax.ppermute(x, "dp", [(i, j) for i, j in pairs if i ^ j == 2 * k])

    to_holders = [(i, j) for i in range(dp_size) for j in holders]
    from_holders = [(j, i) for i, j in to_holders]

    def to_batches(x, through=(), after=()):
        other = swap(lax.dynamic_index_in_dim(x.reshape(batches // 2, 2, pixels, channels), core, 1, keepdims=False))
        parts = spread_call(place, x, other, through, after)
        through = parts[PARTS:]
        parts = list(parts[:1]) + [along_z(k, parts[k], to_holders) for k in range(1, PARTS)]
        return [part.reshape(2 * pixels, channels) for part in parts], *through

    def to_images(parts, dtype):
        parts = list(parts[:1]) + [along_z(k, parts[k], from_holders) for k in range(1, PARTS)]
        other = swap(second_images_call(parts))
        return collect_call(place, batches, parts, other, dtype).reshape(1, batches, 1, side, side, channels)

    own, send = pack_call(
        place,
        conv_local.reshape(-1, CL),
        conv_cross.reshape(-1, CG),
        reduce_weight[0].T,
        spectral_weight[0],
        expand_weight[0],
        norm_gain,
        norm_bias,
    )
    inputs, send = to_batches(images_in.reshape(batches, pixels, channels), (send,))
    hole_float = hole_mask.astype(F32)
    hole_counts = jnp.sum(hole_float, axis=(2, 3), keepdims=True)
    weighting = 0.25 + hole_float * pixels / (hole_counts + pixels / 8.0)
    seed = (cotangent.astype(F32) * weighting[..., None]).astype(BF)

    seeds, *_ = to_batches(seed.reshape(batches, pixels, channels))
    arrived = exchange_weights(send, seeds[:1])
    first = first_call(place, inputs, own, arrived, mf, mi, seeds[1:3], side, dp_size)
    middle = middle_call(place, first.out, inputs, seeds, own, arrived, (mf, mi, mft, mit), side, dp_size)
    activations = to_images(middle.own_out, BF)
    back = last_norms_call(
        place, first, middle.grads0, inputs, middle.own_terms, own, arrived, (mft, mit), side, dp_size
    )
    own_grad = last_convs_call(place, back, middle.grad1, middle.own_grad, own, arrived, side, dp_size).own_grad
    own_terms = back.own_terms
    input_grads = to_images(own_grad, F32)
    local, cross, reduce_w, spectral, expand, gain, bias = unpack_call(
        lax.psum(own_terms, "dp"), (activations, input_grads)
    )
    return (
        activations,
        input_grads,
        local.reshape(conv_local.shape),
        cross.reshape(conv_cross.shape),
        reduce_w.T[None],
        spectral[None],
        expand[None],
        gain,
        bias,
    )


def solution(mesh):
    placed = (
        P(None, "dp", None, None, None),
        P("pipe", None, None, None, None),
        P("pipe", None, None, None, None),
        P("pipe", None, None),
        P("pipe", None, None),
        P("pipe", None, None),
        P("pipe", None),
        P("pipe", None),
        P(None, "dp", None, None, None),
        P(None, "dp", None, None),
    )

    def on_device(images_in, *rest):
        dp_size = lax.axis_size("dp")
        fits = images_in.shape[1] == 1 and dp_size == 8 and images_in.shape[0] == dp_size - 2 and lax.axis_size("pipe") == 4
        return (local_device if fits else general_device)(images_in, *rest)

    return jax.shard_map(
        on_device,
        mesh=mesh,
        in_specs=placed,
        out_specs=(
            P("pipe", None, "dp", None, None, None),
            P("pipe", None, "dp", None, None, None),
            P("pipe", None, None, None, None),
            P("pipe", None, None, None, None),
            P("pipe", None, None),
            P("pipe", None, None),
            P("pipe", None, None),
            P("pipe", None),
            P("pipe", None),
        ),
        check_vma=False,
    )
```
